32 devices in a mesh: shot: 4 (over x, core), depth: 8 (over z, y).
Axes of the slice: x: 2, y: 2, z: 4, core: 2. Of those that a mesh axis runs over, the one named last changes fastest.
Arguments:
- field_prev: float32 [4, 256, 64, 128], P('shot', 'depth'), may hold values from -6 to 6
- field_now: float32 [4, 256, 64, 128], P('shot', 'depth'), may hold values from -6 to 6
- adjoint_next: float32 [4, 256, 64, 128], P('shot', 'depth'), may hold values from -6 to 6
- adjoint_after: float32 [4, 256, 64, 128], P('shot', 'depth'), may hold values from -6 to 6
- courant: float32 [256, 64, 128], P('depth'), may hold values from 0.05 to 0.2
- wavelet: float32 [4, 4], P('shot'), may hold values from -18 to 18
- source_cell: int32 [4], P('shot'), may hold values from 0 to 2097151
- receiver_cell: int32 [4, 128], P('shot'), may hold values from 0 to 2097151
- observed: float32 [4, 4, 128], P('shot'), may hold values from -6 to 6
- damping_table: float32 [64], replicated, may hold values from 0.1 to 10
- plan_step: int32 [1], replicated, may hold values from 0 to 63
Outputs:
- updated: float32 [256, 64, 128], P('depth')
The draws below stay inside these ranges and needn't reach their ends.
All inputs are finite; a program needn't handle non-finite values.
Results may differ from the reference program's by a relative error of at most 0.00002.
Values sent between devices are 32-bit elements; how exact they have to be, the bound alone decides.
No kernel may reach another device: no remote copies, remote signals or barrier semaphores. Data moves between devices by JAX's collectives and lax.ppermute only.
A program may use at most 128 MiB of HBM per device.

```python
import math
import jax
import jax.numpy as jnp

NX = 64
NY = 128
STEPS = 4
RECV = 128
LEVELS = 64
SHOTS = 4
NZ = 256


def set_ends(entries, rng, smallest, top_value):
    longest = entries.shape.index(max(entries.shape))
    spots = []
    for shift in (0, 1):
        where = [jax.random.randint(jax.random.fold_in(rng, axis), (), 0, length) for axis, length in enumerate(entries.shape)]
        where[longest] = (where[longest] + shift) % entries.shape[longest]
        spots.append(tuple(where))
    return entries.at[spots[0]].set(smallest).at[spots[1]].set(top_value)


def level_of(key, dims, split, low, largest):
    gain, own = 1.0, jax.random.fold_in(key, 6)
    for dim, shards_of in split:
        draws = jnp.exp(jax.random.uniform(jax.random.fold_in(own, dim), (shards_of,), jnp.float32, low / len(split), largest / len(split)))
        gain = gain * jnp.repeat(draws, dims[dim] // shards_of).reshape([-1 if axis == dim else 1 for axis in range(len(dims))])
    return gain


def scatter_about(rng, shape, scale, bound, cuts=(), held_as=jnp.bfloat16):
    values = jax.random.normal(rng, shape, jnp.float32) * scale
    if len(cuts) > 0:
        values = level_of(rng, shape, cuts, -0.22, 0.18) * values
    return jnp.clip(values, min=-bound, max=bound).astype(held_as)


def setup_inputs(seed: int = 0) -> dict:
    splits = jax.random.split(jax.random.key(seed), 12)
    field_prev = scatter_about(splits[0], (SHOTS, NZ, NX, NY), 1.0, 6.0, ((0, 4), (1, 8)), jnp.float32)
    field_now = scatter_about(splits[1], (SHOTS, NZ, NX, NY), 1.0, 6.0, ((0, 4), (1, 8)), jnp.float32)
    adjoint_next = scatter_about(splits[2], (SHOTS, NZ, NX, NY), 1.0, 6.0, ((0, 4), (1, 8)), jnp.float32)
    adjoint_after = scatter_about(splits[3], (SHOTS, NZ, NX, NY), 1.0, 6.0, ((0, 4), (1, 8)), jnp.float32)
    courant = jnp.clip(jnp.exp(math.log(0.2) - 1.3862944 * jax.random.uniform(splits[4], (NZ, NX, NY), jnp.float32) ** level_of(splits[4], (NZ, NX, NY), ((0, 8),), -0.2, 0.2)), 0.05, 0.2)
    wavelet = scatter_about(splits[5], (SHOTS, STEPS), 3.0, 18.0, ((0, 4),), jnp.float32)
    source_cell = set_ends(jax.random.randint(splits[6], (SHOTS,), 0, NZ * NX * NY), jax.random.fold_in(splits[6], 1), 0, (NZ * NX * NY) - 1).astype(jnp.int32)
    receiver_cell = set_ends(jax.random.randint(splits[7], (SHOTS, RECV), 0, NZ * NX * NY), jax.random.fold_in(splits[7], 1), 0, (NZ * NX * NY) - 1).astype(jnp.int32)
    observed = scatter_about(splits[8], (SHOTS, STEPS, RECV), 1.0, 6.0, ((0, 4),), jnp.float32)
    damping_table = jnp.clip(jnp.exp(jax.random.uniform(splits[9], (LEVELS,), jnp.float32, math.log(0.1), math.log(10.0))), 0.1, 10.0)
    plan_step = jax.random.randint(splits[10], (1,), 0, LEVELS).astype(jnp.int32)
    return {"field_prev": field_prev, "field_now": field_now, "adjoint_next": adjoint_next, "adjoint_after": adjoint_after, "courant": courant, "wavelet": wavelet, "source_cell": source_cell, "receiver_cell": receiver_cell, "observed": observed, "damping_table": damping_table, "plan_step": plan_step}


coeffs = (-205.0 / 72.0, 8.0 / 5.0, -1.0 / 5.0, 8.0 / 315.0, -1.0 / 560.0)


def laplace(padded):
    depth_len = padded.shape[1] - 8
    width_x = padded.shape[2]
    width_y = padded.shape[3]
    lateral = jnp.pad(padded, ((0, 0), (0, 0), (4, 4), (4, 4)))
    center = lateral[:, 4:4 + depth_len, 4:4 + width_x, 4:4 + width_y]
    result = 3.0 * coeffs[0] * center
    for k in range(1, 5):
        along = lateral[:, 4 + k:4 + k + depth_len, 4:4 + width_x, 4:4 + width_y]
        along = along + lateral[:, 4 - k:4 - k + depth_len, 4:4 + width_x, 4:4 + width_y]
        along = along + lateral[:, 4:4 + depth_len, 4 + k:4 + k + width_x, 4:4 + width_y]
        along = along + lateral[:, 4:4 + depth_len, 4 - k:4 - k + width_x, 4:4 + width_y]
        along = along + lateral[:, 4:4 + depth_len, 4:4 + width_x, 4 + k:4 + k + width_y]
        along = along + lateral[:, 4:4 + depth_len, 4:4 + width_x, 4 - k:4 - k + width_y]
        result = result + coeffs[k] * along
    return result


def whole_laplace(field):
    return laplace(jnp.pad(field, ((0, 0), (4, 4), (0, 0), (0, 0))))


def reference(field_prev, field_now, adjoint_next, adjoint_after, courant, wavelet, source_cell, receiver_cell, observed, damping_table, plan_step):
    shape = field_now.shape[1:]
    gradient = jnp.zeros(shape, jnp.float32)
    curvature = jnp.zeros(shape, jnp.float32)
    for shot_index in range(SHOTS):
        older = field_prev[shot_index:shot_index + 1]
        current = field_now[shot_index:shot_index + 1]
        saved = []
        residuals = []
        for step in range(STEPS):
            lap_now = whole_laplace(current)
            saved.append(lap_now)
            nxt = 2.0 * current - older + courant[None] * lap_now
            flat = nxt.reshape(-1).at[source_cell[shot_index]].add(wavelet[shot_index, step])
            residuals.append(flat[receiver_cell[shot_index]] - observed[shot_index, step])
            older = current
            current = flat.reshape(nxt.shape)
        after_one = adjoint_next[shot_index:shot_index + 1]
        after_two = adjoint_after[shot_index:shot_index + 1]
        for step in range(STEPS - 1, -1, -1):
            adjoint = 2.0 * after_one - after_two + courant[None] * whole_laplace(after_one)
            adjoint = adjoint.reshape(-1).at[receiver_cell[shot_index]].add(residuals[step]).reshape(current.shape)
            gradient = gradient + (adjoint * saved[step])[0]
            curvature = curvature + (saved[step] * saved[step])[0]
            after_two = after_one
            after_one = adjoint
    level = jnp.sum(curvature) / (NZ * NX * NY) + 1e-6
    damp = damping_table[plan_step[0]]
    return courant - gradient / (curvature + damp * level)
```

```python
import jax
import jax.numpy as jnp
from jax import lax
from jax.experimental import pallas as pl
from jax.experimental.pallas import tpu as pltpu
from jax.sharding import PartitionSpec as P

STEPS = 4
HALO = 4
PAD = 8

coeffs = (-205.0 / 72.0, 8.0 / 5.0, -1.0 / 5.0, 8.0 / 315.0, -1.0 / 560.0)

VMEM = pl.BlockSpec(memory_space=pltpu.VMEM)
SMEM = pl.BlockSpec(memory_space=pltpu.SMEM)
ANY = pl.BlockSpec(memory_space=pl.ANY)


def f32(*shape):
    return jax.ShapeDtypeStruct(shape, jnp.float32)


def params():
    return pltpu.CompilerParams(vmem_limit_bytes=24 * 2**20)


def cost(planes):
    return pl.CostEstimate(
        flops=planes * 2 * 10**6, bytes_accessed=planes * 2**16, transcendentals=0
    )


def margins(pad, width):
    planes = pad.shape[0]
    blank = jnp.zeros((planes, PAD, pad.shape[2]), jnp.float32)
    pad[:, 0:PAD, :] = blank
    pad[:, PAD + width : 2 * PAD + width, :] = blank


def fill(pad, start, field, first, count, width):
    origin = 0
    for ref in field:
        length = ref.shape[0]
        begin = max(first, origin)
        end = min(first + count, origin + length)
        if end > begin:
            at = start + begin - first
            pad[at : at + end - begin, PAD : PAD + width, :] = ref[begin - origin : end - origin]
        origin += length


def part(field, first):
    origin = 0
    for ref in field:
        if first < origin + ref.shape[0]:
            return ref, first - origin
        origin += ref.shape[0]


def stencil(pad, p, width, lane):
    rows = slice(PAD, PAD + width)
    center = pad[p, rows, :]
    length = center.shape[1]
    result = (3.0 * coeffs[0]) * center
    for k in range(1, 5):
        along = pad[p + k, rows, :] + pad[p - k, rows, :]
        along = along + pad[p, PAD + k : PAD + k + width, :]
        along = along + pad[p, PAD - k : PAD - k + width, :]
        up = pltpu.roll(center, length - k, 1)
        down = pltpu.roll(center, k, 1)
        along = along + jnp.where(lane < length - k, up, 0.0)
        along = along + jnp.where(lane >= k, down, 0.0)
        result = result + coeffs[k] * along
    return center, result


def fold(values):
    width, length = values.shape
    return jnp.sum(values.reshape(width // 8, 8, length), axis=0)


def regions(edge, slab):
    if edge:
        return [(HALO, 0, 0, HALO), (4 * HALO, slab - HALO, HALO, HALO)]
    return [(HALO, HALO, 0, slab - 2 * HALO)]


def load_pad(edge, pad, below, above, cur, slab, width):
    margins(pad, width)
    if edge:
        fill(pad, 0, [below], 0, HALO, width)
        fill(pad, HALO, cur, 0, 2 * HALO, width)
        fill(pad, 3 * HALO, cur, slab - 2 * HALO, 2 * HALO, width)
        fill(pad, 5 * HALO, [above], 0, HALO, width)
    else:
        fill(pad, 0, cur, 0, slab, width)


def march(count, body, carry=None):
    return lax.fori_loop(0, count, body, carry, unroll=2)


def forward(edge, step, halos, cur, old, courant, curv, tile, wavelet, source):
    slab, width, length = courant.shape
    planes = 2 * HALO if edge else slab - 2 * HALO
    last = step == STEPS - 1
    groups = [list(halos) if edge else [], list(cur), list(old), [courant]]
    groups.append([curv] if curv is not None else [])
    groups.append([tile] if tile is not None else [])
    sizes = [len(g) for g in groups]
    arrays = sum(groups, [])

    def kernel(*refs):
        wave_ref, source_ref = refs[:2]
        refs = refs[2:]
        split = []
        for size in sizes:
            split.append(refs[:size])
            refs = refs[size:]
        halo_refs, cur_refs, old_refs, (c_ref,), curv_in, tile_in = split
        below, above = halo_refs if edge else (None, None)
        refs = list(refs)
        pad = refs.pop()
        next_ref, lap_ref = refs[:2]
        refs = refs[2:]
        if edge:
            lo_ref, hi_ref = refs[:2]
            refs = refs[2:]
        load_pad(edge, pad, below, above, cur_refs, slab, width)
        lane = lax.broadcasted_iota(jnp.int32, (width, length), 1)
        total = jnp.zeros((8, length), jnp.float32)
        if last:
            keep_ref, send_ref, tile_ref, sum_ref = refs
            if tile_in:
                total = tile_in[0][...]
        else:
            (sum_ref,) = refs
        for spot, plane, place, count in regions(edge, slab):
            old_ref, old_at = part(old_refs, plane)

            def body(i, acc, spot=spot, plane=plane, place=place, old_ref=old_ref, old_at=old_at):
                center, lap = stencil(pad, spot + i, width, lane)
                lap_ref[place + i] = lap
                next_ref[place + i] = 2.0 * center - old_ref[old_at + i] + c_ref[plane + i] * lap
                square = lap * lap
                if curv_in:
                    square = curv_in[0][place + i] + square
                sum_ref[place + i] = square
                return acc + fold(square) if last else acc

            total = march(count, body, total)
        offset = lax.axis_index("depth") * (slab * width * length)
        local = source_ref[0] - offset
        row = local // length
        where = row // width
        x = row % width
        y = local % length
        spot = lax.broadcasted_iota(jnp.int32, (1, length), 1) == y
        add = jnp.where(spot, wave_ref[0, step], 0.0)
        for _, plane, place, count in regions(edge, slab):

            @pl.when((local >= 0) & (where >= plane) & (where < plane + count))
            def _(plane=plane, place=place):
                at = where - plane + place
                next_ref[at, pl.ds(x, 1), :] = next_ref[at, pl.ds(x, 1), :] + add

        if edge:
            lo_ref[...] = next_ref[0:HALO]
            hi_ref[...] = next_ref[HALO : 2 * HALO]
        if last:
            tile_ref[...] = total
            share(sum_ref, keep_ref, send_ref)

    shape = f32(planes, width, length)
    outs = [shape, shape]
    if edge:
        outs += [f32(HALO, width, length)] * 2
    scratch = []
    if last:
        outs += [f32(planes // 2, width, length)] * 2 + [f32(8, length)]
        scratch.append(pltpu.VMEM(shape.shape, jnp.float32))
    else:
        outs.append(shape)
    depth = 6 * HALO if edge else slab
    scratch.append(pltpu.VMEM((depth, width + 2 * PAD, length), jnp.float32))
    return pl.pallas_call(
        kernel,
        out_shape=tuple(outs),
        in_specs=[SMEM, SMEM] + [VMEM] * len(arrays),
        out_specs=tuple([VMEM] * len(outs)),
        scratch_shapes=scratch,
        compiler_params=params(),
        cost_estimate=cost(planes),
    )(wavelet, source, *arrays)


def share(sum_ref, keep_ref, send_ref):
    half = keep_ref.shape[0]
    core = lax.axis_index("shot") % 2

    def body(i, _):
        keep_ref[i] = sum_ref[core * half + i]
        send_ref[i] = sum_ref[(1 - core) * half + i]

    march(half, body)


def adjoint(edge, step, halos, cur, old, courant, lap, field, grad, listing, observed):
    slab, width, length = courant.shape
    planes = 2 * HALO if edge else slab - 2 * HALO
    last = step == 0
    groups = [list(halos) if edge else [], list(cur), list(old), [courant, lap, field]]
    groups.append([grad] if grad is not None else [])
    sizes = [len(g) for g in groups]
    arrays = sum(groups, [])
    base = 0 if edge else 4

    def kernel(*refs):
        list_ref, obs_ref = refs[:2]
        refs = refs[2:]
        split = []
        for size in sizes:
            split.append(refs[:size])
            refs = refs[size:]
        halo_refs, cur_refs, old_refs, (c_ref, lap_ref, field_ref), grad_in = split
        below, above = halo_refs if edge else (None, None)
        refs = list(refs)
        pad = refs.pop()
        if last:
            keep_ref, send_ref, next_ref, sum_ref = refs
        elif edge:
            sum_ref, lo_ref, hi_ref, next_ref = refs
        else:
            sum_ref, next_ref = refs
        load_pad(edge, pad, below, above, cur_refs, slab, width)
        lane = lax.broadcasted_iota(jnp.int32, (width, length), 1)
        for spot, plane, place, count in regions(edge, slab):
            old_ref, old_at = part(old_refs, plane)

            def body(i, _, spot=spot, plane=plane, place=place, old_ref=old_ref, old_at=old_at):
                center, value = stencil(pad, spot + i, width, lane)
                next_ref[place + i] = 2.0 * center - old_ref[old_at + i] + c_ref[plane + i] * value

            march(count, body)

        column = lax.broadcasted_iota(jnp.int32, (1, length), 1)

        def inject(k, _):
            at = list_ref[base, k]
            x = list_ref[base + 1, k]
            y = list_ref[base + 2, k]
            pred = field_ref[at, pl.ds(x, 1), :]
            res = jnp.where(column == y, pred - obs_ref[step, list_ref[base + 3, k]], 0.0)
            next_ref[at, pl.ds(x, 1), :] = next_ref[at, pl.ds(x, 1), :] + res

        lax.fori_loop(0, list_ref[8, 0 if edge else 1], inject, None)

        def collect(i, _):
            value = next_ref[i] * lap_ref[i]
            if grad_in:
                value = grad_in[0][i] + value
            sum_ref[i] = value

        march(planes, collect)
        if last:
            share(sum_ref, keep_ref, send_ref)
        elif edge:
            lo_ref[...] = next_ref[0:HALO]
            hi_ref[...] = next_ref[HALO : 2 * HALO]

    shape = f32(planes, width, length)
    buffer = pltpu.VMEM(shape.shape, jnp.float32)
    if last:
        outs = [f32(planes // 2, width, length)] * 2
        scratch = [buffer, buffer]
    elif edge:
        outs = [shape] + [f32(HALO, width, length)] * 2
        scratch = [buffer]
    else:
        outs = [shape, shape]
        scratch = []
    depth = 6 * HALO if edge else slab
    scratch.append(pltpu.VMEM((depth, width + 2 * PAD, length), jnp.float32))
    return pl.pallas_call(
        kernel,
        out_shape=tuple(outs),
        in_specs=[SMEM, SMEM] + [VMEM] * len(arrays),
        out_specs=tuple([VMEM] * len(outs)),
        scratch_shapes=scratch,
        compiler_params=params(),
        cost_estimate=cost(planes),
    )(listing, observed, *arrays)


def list_receivers(cells, slab, width, length):
    count = cells.shape[0]

    def kernel(cell_ref, out_ref):
        offset = lax.axis_index("depth") * (slab * width * length)

        def body(r, counts):
            edges, cores = counts
            local = cell_ref[r] - offset
            inside = (local >= 0) & (local < slab * width * length)
            row = local // length
            plane = row // width
            x = row % width
            y = local % length
            low = plane < HALO
            edge = low | (plane >= slab - HALO)

            @pl.when(inside & edge)
            def _():
                out_ref[0, edges] = jnp.where(low, plane, plane - (slab - 2 * HALO))
                out_ref[1, edges] = x
                out_ref[2, edges] = y
                out_ref[3, edges] = r

            @pl.when(inside & jnp.logical_not(edge))
            def _():
                out_ref[4, cores] = plane - HALO
                out_ref[5, cores] = x
                out_ref[6, cores] = y
                out_ref[7, cores] = r

            edges = edges + jnp.where(inside & edge, 1, 0)
            cores = cores + jnp.where(inside & jnp.logical_not(edge), 1, 0)
            return edges, cores

        edges, cores = lax.fori_loop(0, count, body, (jnp.int32(0), jnp.int32(0)))
        out_ref[8, 0] = edges
        out_ref[8, 1] = cores

    return pl.pallas_call(
        kernel,
        out_shape=jax.ShapeDtypeStruct((9, count), jnp.int32),
        in_specs=[SMEM],
        out_specs=SMEM,
        cost_estimate=cost(8),
    )(cells)


def refresh(edge, courant, parts, curv, tiles, table, plan):
    slab, width, length = courant.shape
    half = curv.shape[0]
    number = len(parts)
    cells = slab * width * length * lax.axis_size("depth")

    def kernel(table_ref, plan_ref, tiles_ref, c_ref, curv_ref, *rest):
        part_refs = rest[:number]
        out_ref = rest[number]
        level = jnp.sum(tiles_ref[...]) / cells + 1e-06
        extra = table_ref[plan_ref[0]] * level
        core = lax.axis_index("shot") % 2
        start = core * (slab - HALO) if edge else HALO + core * half

        def body(i, _):
            grad = part_refs[0][i]
            for ref in part_refs[1:]:
                grad = grad + ref[i]
            out_ref[i] = c_ref[start + i] - grad / (curv_ref[i] + extra)

        march(half, body)

    return pl.pallas_call(
        kernel,
        out_shape=f32(half, width, length),
        in_specs=[SMEM, SMEM] + [VMEM] * (3 + number),
        out_specs=VMEM,
        compiler_params=params(),
        cost_estimate=cost(half),
    )(table, plan, tiles, courant, curv, *parts)


def assemble(pieces, slab):
    inner = pieces[0].shape[0]
    width, length = pieces[0].shape[1:]

    def kernel(a_ref, b_ref, c_ref, d_ref, out_ref, sems):
        core = lax.axis_index("shot") % 2
        copies = []
        for n, (ref, start, count) in enumerate(
            [
                (a_ref, HALO + core * inner, inner),
                (b_ref, HALO + (1 - core) * inner, inner),
                (c_ref, core * (slab - HALO), HALO),
                (d_ref, (1 - core) * (slab - HALO), HALO),
            ]
        ):
            copy = pltpu.make_async_copy(ref, out_ref.at[pl.ds(start, count)], sems.at[n])
            copy.start()
            copies.append(copy)
        for copy in copies:
            copy.wait()

    return pl.pallas_call(
        kernel,
        out_shape=f32(slab, width, length),
        in_specs=[VMEM] * 4,
        out_specs=ANY,
        scratch_shapes=[pltpu.SemaphoreType.DMA((4,))],
        compiler_params=params(),
        cost_estimate=cost(8),
    )(*pieces)


def neighbours(low, high):
    count = lax.axis_size("depth")
    up = [(i, i + 1) for i in range(count - 1)]
    down = [(target, source) for source, target in up]
    return lax.ppermute(high, "depth", up), lax.ppermute(low, "depth", down)


def swap(values, bit):
    count = lax.axis_size("shot")
    return lax.ppermute(values, "shot", [(i, i ^ bit) for i in range(count)])


def total_parts(keep, send):
    parts = [keep, swap(send, 1)]
    bit = 2
    while bit < lax.axis_size("shot"):
        here = parts[0] + parts[1]
        parts = [here, swap(here, bit)]
        bit *= 2
    return parts


def on_device(
    field_prev,
    field_now,
    adjoint_next,
    adjoint_after,
    courant,
    wavelet,
    source_cell,
    receiver_cell,
    observed,
    damping_table,
    plan_step,
):
    slab, width, length = courant.shape
    start = field_now[0]
    halos = neighbours(start[:HALO], start[slab - HALO :])
    first = adjoint_next[0]
    adjoint_halos = neighbours(first[:HALO], first[slab - HALO :])
    listing = list_receivers(receiver_cell[0], slab, width, length)
    old = (field_prev[0],)
    cur = (start,)
    laps, fields = [], []
    edge_sum = core_sum = None
    for step in range(STEPS):
        core = forward(
            False, step, None, cur, old, courant, core_sum, None, wavelet, source_cell
        )
        tile = core[4] if step == STEPS - 1 else None
        edge = forward(
            True, step, halos, cur, old, courant, edge_sum, tile, wavelet, source_cell
        )
        laps.append((edge[1], core[1]))
        fields.append((edge[0], core[0]))
        if step < STEPS - 1:
            core_sum, edge_sum = core[2], edge[4]
            halos = neighbours(edge[2], edge[3])
            old = cur
            cur = (edge[2], core[0], edge[3])
    tiles = lax.all_gather(edge[6], ("shot", "depth"), axis=0, tiled=True)
    core_curv = sum(total_parts(core[2], core[3]))
    edge_curv = sum(total_parts(edge[4], edge[5]))
    old = (adjoint_after[0],)
    cur = (first,)
    halos = adjoint_halos
    edge_grad = core_grad = None
    traces = observed[0]
    for step in range(STEPS - 1, -1, -1):
        core = adjoint(
            False, step, None, cur, old, courant, laps[step][1], fields[step][1], core_grad,
            listing, traces,
        )
        edge = adjoint(
            True, step, halos, cur, old, courant, laps[step][0], fields[step][0], edge_grad,
            listing, traces,
        )
        if step > 0:
            core_grad, edge_grad = core[0], edge[0]
            halos = neighbours(edge[1], edge[2])
            old = cur
            cur = (edge[1], core[1], edge[2])
    pieces = []
    for is_edge, (keep, send), curv in ((False, core, core_curv), (True, edge, edge_curv)):
        parts = total_parts(keep, send)
        new = refresh(is_edge, courant, parts, curv, tiles, damping_table, plan_step)
        pieces += [new, swap(new, 1)]
    return assemble(pieces, slab)


def solution(mesh):
    in_specs = (
        P("shot", "depth", None, None),
        P("shot", "depth", None, None),
        P("shot", "depth", None, None),
        P("shot", "depth", None, None),
        P("depth", None, None),
        P("shot", None),
        P("shot"),
        P("shot", None),
        P("shot", None, None),
        P(),
        P(),
    )
    out_specs = P("depth", None, None)
    return jax.shard_map(
        on_device, mesh=mesh, in_specs=in_specs, out_specs=out_specs, check_vma=False
    )
```

```python
import jax
import jax.numpy as jnp
from jax import lax
from jax.experimental import pallas as pl
from jax.experimental.pallas import tpu as pltpu
from jax.sharding import PartitionSpec as P

STEPS = 4
HALO = 4
PAD = 8

coeffs = (-205.0 / 72.0, 8.0 / 5.0, -1.0 / 5.0, 8.0 / 315.0, -1.0 / 560.0)

VMEM = pl.BlockSpec(memory_space=pltpu.VMEM)
SMEM = pl.BlockSpec(memory_space=pltpu.SMEM)
HBM = pl.BlockSpec(memory_space=pltpu.HBM)


def f32(*shape):
    return jax.ShapeDtypeStruct(shape, jnp.float32)


def params(limit=24):
    return pltpu.CompilerParams(vmem_limit_bytes=limit * 2**20)


def cost(planes):
    return pl.CostEstimate(
        flops=planes * 2 * 10**6, bytes_accessed=planes * 2**16, transcendentals=0
    )


def split(value, size):
    if size & (size - 1) == 0:
        return value >> (size.bit_length() - 1), value & (size - 1)
    return value // size, value % size


def margins(pad, width):
    planes = pad.shape[0]
    blank = jnp.zeros((planes, PAD, pad.shape[2]), jnp.float32)
    pad[:, 0:PAD, :] = blank
    pad[:, PAD + width : 2 * PAD + width, :] = blank


def pieces_of(refs, slab):
    if len(refs) == 1:
        return [(refs[0], 0, 0, slab)]
    edge, core = refs
    return [
        (edge, 0, 0, HALO),
        (core, 0, HALO, slab - 2 * HALO),
        (edge, HALO, slab - HALO, HALO),
    ]


def fill(pad, start, pieces, first, count, width):
    for ref, inside, origin, length in pieces:
        begin = max(first, origin)
        end = min(first + count, origin + length)
        if end > begin:
            at = start + begin - first
            inside = inside + begin - origin
            pad[at : at + end - begin, PAD : PAD + width, :] = ref[inside : inside + end - begin]


def part(pieces, first):
    for ref, inside, origin, length in pieces:
        if origin <= first < origin + length:
            return ref, inside + first - origin


def stencil(pad, p, width, lane):
    rows = slice(PAD, PAD + width)
    center = pad[p, rows, :]
    length = center.shape[1]
    result = (3.0 * coeffs[0]) * center
    for k in range(1, 5):
        along = pad[p + k, rows, :] + pad[p - k, rows, :]
        along = along + pad[p, PAD + k : PAD + k + width, :]
        along = along + pad[p, PAD - k : PAD - k + width, :]
        up = pltpu.roll(center, length - k, 1)
        down = pltpu.roll(center, k, 1)
        along = along + jnp.where(lane < length - k, up, 0.0)
        along = along + jnp.where(lane >= k, down, 0.0)
        result = result + coeffs[k] * along
    return center, result


def fold(values):
    width, length = values.shape
    return jnp.sum(values.reshape(width // 8, 8, length), axis=0)


def regions(edge, slab):
    if edge:
        return [(HALO, 0, 0, HALO), (4 * HALO, slab - HALO, HALO, HALO)]
    return [(HALO, HALO, 0, slab - 2 * HALO)]


def load_pad(edge, pad, halos, halo_at, pieces, slab, width):
    margins(pad, width)
    if edge:
        fill(pad, HALO, pieces, 0, 2 * HALO, width)
        fill(pad, 3 * HALO, pieces, slab - 2 * HALO, 2 * HALO, width)
        odd = lax.axis_index("depth") % 2
        for ref, start in zip(halos, ((1 - odd) * (5 * HALO), odd * (5 * HALO))):
            pad[pl.ds(start, HALO), PAD : PAD + width, :] = ref[halo_at : halo_at + HALO]
    else:
        fill(pad, 0, pieces, 0, slab, width)


def messages(next_ref, first_ref, second_ref):
    odd = lax.axis_index("depth") % 2
    first_ref[...] = next_ref[pl.ds((1 - odd) * HALO, HALO)]
    second_ref[...] = next_ref[pl.ds(odd * HALO, HALO)]


def march(count, body, carry=None):
    return lax.fori_loop(0, count, body, carry, unroll=2)


def kernel_call(kernel, small, arrays, outs, scratch, planes):
    return pl.pallas_call(
        kernel,
        out_shape=tuple(outs),
        in_specs=[SMEM] * len(small) + [VMEM] * len(arrays),
        out_specs=tuple([VMEM] * len(outs)),
        scratch_shapes=scratch,
        compiler_params=params(),
        cost_estimate=cost(planes),
    )(*small, *arrays)


def grouped(refs, sizes):
    found = []
    for size in sizes:
        found.append(refs[:size])
        refs = refs[size:]
    return found, list(refs)


def pad_shape(edge, slab, width, length):
    return pltpu.VMEM((6 * HALO if edge else slab, width + 2 * PAD, length), jnp.float32)


def forward(edge, step, halos, cur, old, courant, after, wavelet, source):
    slab, width, length = courant.shape
    planes = 2 * HALO if edge else slab - 2 * HALO
    last = step == STEPS - 1
    groups = [list(halos or ()), list(cur), list(old), [courant], list(after)]
    sizes = [len(g) for g in groups]

    def kernel(wave_ref, source_ref, *refs):
        (halo_refs, cur_refs, old_refs, (c_ref,), _), refs = grouped(refs, sizes)
        pad = refs.pop()
        next_ref, lap_ref = refs[:2]
        load_pad(edge, pad, halo_refs, 0, pieces_of(cur_refs, slab), slab, width)
        lane = lax.broadcasted_iota(jnp.int32, (width, length), 1)
        old_pieces = pieces_of(old_refs, slab)
        for spot, plane, place, count in regions(edge, slab):
            old_ref, old_at = part(old_pieces, plane)

            def body(i, _, spot=spot, plane=plane, place=place, old_ref=old_ref, old_at=old_at):
                center, lap = stencil(pad, spot + i, width, lane)
                lap_ref[place + i] = lap
                next_ref[place + i] = 2.0 * center - old_ref[old_at + i] + c_ref[plane + i] * lap

            march(count, body)
        local = source_ref[0] - lax.axis_index("depth") * (slab * width * length)
        row, y = split(local, length)
        where, x = split(row, width)
        spot = lax.broadcasted_iota(jnp.int32, (1, length), 1) == y
        add = jnp.where(spot, wave_ref[0, step], 0.0)
        for _, plane, place, count in regions(edge, slab):

            @pl.when((local >= 0) & (where >= plane) & (where < plane + count))
            def _(plane=plane, place=place):
                at = where - plane + place
                next_ref[at, pl.ds(x, 1), :] = next_ref[at, pl.ds(x, 1), :] + add

        if edge and not last:
            messages(next_ref, *refs[2:])

    outs = [f32(planes, width, length)] * 2
    if edge and not last:
        outs += [f32(HALO, width, length)] * 2
    arrays = sum(groups, [])
    scratch = [pad_shape(edge, slab, width, length)]
    return kernel_call(kernel, [wavelet, source], arrays, outs, scratch, planes)


def adjoint(edge, step, halos, halo_at, cur, old, courant, field, after, listing, observed):
    slab, width, length = courant.shape
    planes = 2 * HALO if edge else slab - 2 * HALO
    groups = [list(halos or ()), list(cur), list(old), [courant, field], list(after)]
    sizes = [len(g) for g in groups]

    def kernel(list_ref, obs_ref, *refs):
        (halo_refs, cur_refs, old_refs, (c_ref, field_ref), _), refs = grouped(refs, sizes)
        pad = refs.pop()
        next_ref = refs[0]
        adjoint_step(
            edge, step, pad, halo_refs, halo_at, cur_refs, old_refs, c_ref, field_ref,
            list_ref, obs_ref, next_ref,
        )
        if edge:
            messages(next_ref, *refs[1:])

    outs = [f32(planes, width, length)]
    if edge:
        outs += [f32(HALO, width, length)] * 2
    arrays = sum(groups, [])
    scratch = [pad_shape(edge, slab, width, length)]
    return kernel_call(kernel, [listing, observed], arrays, outs, scratch, planes)


def adjoint_step(
    edge, step, pad, halos, halo_at, cur, old, c_ref, field_ref, list_ref, obs_ref, next_ref
):
    slab, width, length = c_ref.shape
    load_pad(edge, pad, halos, halo_at, pieces_of(cur, slab), slab, width)
    lane = lax.broadcasted_iota(jnp.int32, (width, length), 1)
    old_pieces = pieces_of(old, slab)
    for spot, plane, place, count in regions(edge, slab):
        old_ref, old_at = part(old_pieces, plane)

        def body(i, _, spot=spot, plane=plane, place=place, old_ref=old_ref, old_at=old_at):
            center, value = stencil(pad, spot + i, width, lane)
            next_ref[place + i] = 2.0 * center - old_ref[old_at + i] + c_ref[plane + i] * value

        march(count, body)

    column = lax.broadcasted_iota(jnp.int32, (1, length), 1)
    base = 0 if edge else 2

    def inject(k, _):
        row, y = split(list_ref[base, k], length)
        at, x = split(row, width)
        pred = field_ref[at, pl.ds(x, 1), :]
        res = jnp.where(column == y, pred - obs_ref[step, list_ref[base + 1, k]], 0.0)
        next_ref[at, pl.ds(x, 1), :] = next_ref[at, pl.ds(x, 1), :] + res

    lax.fori_loop(0, list_ref[4, 0 if edge else 1], inject, None)


def adjoint_last(edge, halos, cur, old, courant, field, laps, adjoints, after, listing, observed):
    slab, width, length = courant.shape
    planes = 2 * HALO if edge else slab - 2 * HALO
    groups = [list(halos or ()), list(cur), list(old), [courant, field], list(laps)]
    groups += [list(adjoints), list(after)]
    sizes = [len(g) for g in groups]

    def kernel(list_ref, obs_ref, *refs):
        (halo_refs, cur_refs, old_refs, (c_ref, field_ref), lap_refs, adj_refs, _), refs = grouped(
            refs, sizes
        )
        keep_ref, send_ref, next_ref, pad = refs
        adjoint_step(
            edge, 0, pad, halo_refs, 0, cur_refs, old_refs, c_ref, field_ref,
            list_ref, obs_ref, next_ref,
        )
        half = planes // 2
        core = lax.axis_index("shot") % 2

        def body(i, _):
            for ref, start in ((keep_ref, core * half), (send_ref, (1 - core) * half)):
                value = next_ref[start + i] * lap_refs[0][start + i]
                for lap_ref, adj_ref in zip(lap_refs[1:], adj_refs):
                    value = value + adj_ref[start + i] * lap_ref[start + i]
                ref[i] = value

        march(half, body)

    outs = [f32(planes // 2, width, length)] * 2
    arrays = sum(groups, [])
    scratch = [pltpu.VMEM((planes, width, length), jnp.float32)]
    scratch.append(pad_shape(edge, slab, width, length))
    return kernel_call(kernel, [listing, observed], arrays, outs, scratch, planes)


def curvature(edge_laps, core_laps):
    inner, width, length = core_laps[0].shape
    half = inner // 2
    size = half + HALO + 1
    number = len(edge_laps)

    def kernel(*refs):
        edge_refs, core_refs = refs[:number], refs[number : 2 * number]
        keep_ref, send_ref = refs[2 * number :]
        core = lax.axis_index("shot") % 2
        total = jnp.zeros((8, length), jnp.float32)
        for laps, place, count in ((core_refs, 0, half), (edge_refs, half, HALO)):

            def body(i, total, laps=laps, place=place, count=count):
                for ref, start in ((keep_ref, core * count), (send_ref, (1 - core) * count)):
                    value = laps[0][start + i] * laps[0][start + i]
                    for lap_ref in laps[1:]:
                        value = value + lap_ref[start + i] * lap_ref[start + i]
                    ref[place + i] = value
                    total = total + fold(value)
                return total

            total = march(count, body, total)
        keep_ref[size - 1] = jnp.zeros((width, length), jnp.float32)
        keep_ref[size - 1, 0:8, :] = total
        send_ref[size - 1] = jnp.zeros((width, length), jnp.float32)
        send_ref[size - 1, 0:8, :] = total

    outs = [f32(size, width, length)] * 2
    return kernel_call(kernel, [], list(edge_laps) + list(core_laps), outs, [], 8)


def list_receivers(cells, slab, width, length):
    count = cells.shape[0]
    area = width * length

    def kernel(cell_ref, out_ref):
        offset = lax.axis_index("depth") * (slab * area)

        def body(r, counts):
            edges, cores = counts
            local = cell_ref[r] - offset
            low = local < HALO * area
            high = local >= (slab - HALO) * area
            inside = (local >= 0) & (local < slab * area)
            edge = inside & (low | high)
            core = inside & jnp.logical_not(low | high)
            out_ref[0, edges] = jnp.where(low, local, local - (slab - 2 * HALO) * area)
            out_ref[1, edges] = r
            out_ref[2, cores] = local - HALO * area
            out_ref[3, cores] = r
            return edges + edge.astype(jnp.int32), cores + core.astype(jnp.int32)

        edges, cores = lax.fori_loop(0, count, body, (jnp.int32(0), jnp.int32(0)), unroll=8)
        out_ref[4, 0] = edges
        out_ref[4, 1] = cores

    return pl.pallas_call(
        kernel,
        out_shape=jax.ShapeDtypeStruct((5, 2 * count), jnp.int32),
        in_specs=[SMEM],
        out_specs=SMEM,
        cost_estimate=cost(8),
    )(cells)


def pack(field, adjoint_field):
    odd = lax.axis_index("depth") % 2
    far = field.shape[0] - HALO
    found = []
    for start in ((1 - odd) * far, odd * far):
        planes = [lax.dynamic_slice_in_dim(v, start, HALO, 0) for v in (field, adjoint_field)]
        found.append(jnp.concatenate(planes, axis=0))
    return found


def refresh(edge, courant, parts, curv, tile, table, plan):
    slab, width, length = courant.shape
    half = parts[0].shape[0]
    number = len(parts)
    cells = slab * width * length * lax.axis_size("depth")
    place = curv.shape[0] - 1 - HALO if edge else 0

    def kernel(table_ref, plan_ref, tile_ref, c_ref, curv_ref, *rest):
        part_refs = rest[:number]
        out_ref = rest[number]
        level = jnp.sum(tile_ref[...]) / cells + 1e-06
        extra = table_ref[plan_ref[0]] * level
        core = lax.axis_index("shot") % 2
        start = core * (slab - HALO) if edge else HALO + core * half

        def body(i, _):
            grad = part_refs[0][i]
            for ref in part_refs[1:]:
                grad = grad + ref[i]
            out_ref[i] = c_ref[start + i] - grad / (curv_ref[place + i] + extra)

        march(half, body)

    arrays = [tile, courant, curv, *parts]
    outs = [f32(half, width, length)]
    return kernel_call(kernel, [table, plan], arrays, outs, [], half)[0]


def assemble(pieces, slab):
    inner = pieces[0].shape[0]
    width, length = pieces[0].shape[1:]

    def kernel(a_ref, b_ref, c_ref, d_ref, out_ref, sems):
        core = lax.axis_index("shot") % 2
        copies = []
        for n, (ref, start, count) in enumerate(
            [
                (a_ref, HALO + core * inner, inner),
                (b_ref, HALO + (1 - core) * inner, inner),
                (c_ref, core * (slab - HALO), HALO),
                (d_ref, (1 - core) * (slab - HALO), HALO),
            ]
        ):
            copy = pltpu.make_async_copy(ref, out_ref.at[pl.ds(start, count)], sems.at[n])
            copy.start()
            copies.append(copy)
        for copy in copies:
            copy.wait()

    return pl.pallas_call(
        kernel,
        out_shape=f32(slab, width, length),
        in_specs=[VMEM] * 4,
        out_specs=HBM,
        scratch_shapes=[pltpu.SemaphoreType.DMA((4,))],
        compiler_params=params(),
        cost_estimate=cost(8),
    )(*pieces)


def exchange(first, second):
    count = lax.axis_size("depth")
    pairs = []
    for begin in (0, 1):
        links = []
        for i in range(begin, count - 1, 2):
            links += [(i, i + 1), (i + 1, i)]
        pairs.append(links)
    return lax.ppermute(first, "depth", pairs[0]), lax.ppermute(second, "depth", pairs[1])


def swap(values, axis, bit):
    count = lax.axis_size(axis)
    return lax.ppermute(values, axis, [(i, i ^ bit) for i in range(count)])


def total_parts(keep, send):
    parts = [keep, swap(send, "shot", 1)]
    bit = 2
    while bit < lax.axis_size("shot"):
        here = parts[0] + parts[1]
        parts = [here, swap(here, "shot", bit)]
        bit *= 2
    return parts


def on_device(
    field_prev,
    field_now,
    adjoint_next,
    adjoint_after,
    courant,
    wavelet,
    source_cell,
    receiver_cell,
    observed,
    damping_table,
    plan_step,
):
    slab, width, length = courant.shape
    halos = exchange(*pack(field_now[0], adjoint_next[0]))
    first_halos = halos
    start, before = field_now[0], field_prev[0]
    first, second = adjoint_next[0], adjoint_after[0]
    listing = list_receivers(receiver_cell[0], slab, width, length)
    traces = observed[0]
    old, cur = (before,), (start,)
    laps, fields = [], []
    for step in range(STEPS):
        core = forward(False, step, None, cur, old, courant, (), wavelet, source_cell)
        after = [core[0]]
        if step == STEPS - 1:
            core_adj = adjoint(
                False, step, None, 0, (first,), (second,), courant, core[0], (), listing, traces
            )
            after = core_adj
        edge = forward(True, step, halos, cur, old, courant, after, wavelet, source_cell)
        laps.append((edge[1], core[1]))
        fields.append((edge[0], core[0]))
        old, cur = cur, (edge[0], core[0])
        if step < STEPS - 1:
            halos = exchange(edge[2], edge[3])
    edge_laps = [lap[0] for lap in laps]
    core_laps = [lap[1] for lap in laps]
    curv = sum(total_parts(*curvature(edge_laps, core_laps)))
    tile = curv[curv.shape[0] - 1, 0:8, :]
    bit = 1
    while bit < lax.axis_size("depth"):
        tile = tile + swap(tile, "depth", bit)
        bit *= 2
    old, cur = (second,), (first,)
    halos, halo_at = first_halos, HALO
    edges, cores = [], []
    for step in range(STEPS - 1, 0, -1):
        field = fields[step]
        if step < STEPS - 1:
            core_adj = adjoint(
                False, step, None, 0, cur, old, courant, field[1], (), listing, traces
            )
        edge_adj = adjoint(
            True, step, halos, halo_at, cur, old, courant, field[0], core_adj, listing, traces
        )
        edges.insert(0, edge_adj[0])
        cores.insert(0, core_adj[0])
        halos, halo_at = exchange(edge_adj[1], edge_adj[2]), 0
        old, cur = cur, (edge_adj[0], core_adj[0])
    core = adjoint_last(
        False, None, cur, old, courant, fields[0][1], core_laps, cores, (), listing, traces
    )
    edge = adjoint_last(
        True, halos, cur, old, courant, fields[0][0], edge_laps, edges, core[:1], listing, traces
    )
    pieces = []
    for is_edge, (keep, send) in ((False, core), (True, edge)):
        parts = total_parts(keep, send)
        new = refresh(is_edge, courant, parts, curv, tile, damping_table, plan_step)
        pieces += [new, swap(new, "shot", 1)]
    return assemble(pieces, slab)


def solution(mesh):
    in_specs = (
        P("shot", "depth", None, None),
        P("shot", "depth", None, None),
        P("shot", "depth", None, None),
        P("shot", "depth", None, None),
        P("depth", None, None),
        P("shot", None),
        P("shot"),
        P("shot", None),
        P("shot", None, None),
        P(),
        P(),
    )
    out_specs = P("depth", None, None)
    return jax.shard_map(
        on_device, mesh=mesh, in_specs=in_specs, out_specs=out_specs, check_vma=False
    )
```

```python
import jax
import jax.numpy as jnp
from jax import lax
from jax.experimental import pallas as pl
from jax.experimental.pallas import tpu as pltpu
from jax.sharding import PartitionSpec as P

STEPS = 4
HALO = 4
PAD = 8

coeffs = (-205.0 / 72.0, 8.0 / 5.0, -1.0 / 5.0, 8.0 / 315.0, -1.0 / 560.0)

VMEM = pl.BlockSpec(memory_space=pltpu.VMEM)
SMEM = pl.BlockSpec(memory_space=pltpu.SMEM)
HBM = pl.BlockSpec(memory_space=pltpu.HBM)


def f32(*shape):
    return jax.ShapeDtypeStruct(shape, jnp.float32)


def params():
    return pltpu.CompilerParams(vmem_limit_bytes=6 * 2**20)


def cost(planes):
    return pl.CostEstimate(
        flops=planes * 10**4, bytes_accessed=planes * 2**10, transcendentals=0
    )


def split(value, size):
    if size & (size - 1) == 0:
        return value >> (size.bit_length() - 1), value & (size - 1)
    return value // size, value % size


def margins(pad, width):
    planes = pad.shape[0]
    blank = jnp.zeros((planes, PAD, pad.shape[2]), jnp.float32)
    pad[:, 0:PAD, :] = blank
    pad[:, PAD + width : 2 * PAD + width, :] = blank


def high(side):
    odd = lax.axis_index("depth") % 2
    return odd if side else 1 - odd


def fill_edge(pad, side, halo, halo_at, field, slab, width):
    margins(pad, width)
    up = high(side)
    rows = slice(PAD, PAD + width)
    pad[pl.ds(up * (2 * HALO), HALO), rows, :] = halo[halo_at : halo_at + HALO]
    inner = pl.ds((1 - up) * (2 * HALO), HALO)
    own = slice(HALO, 2 * HALO)
    if len(field) == 1:
        (ref,) = field
        slab = ref.shape[0]
        pad[own, rows, :] = ref[pl.ds(up * (slab - HALO), HALO)]
        pad[inner, rows, :] = ref[pl.ds(HALO + up * (slab - 3 * HALO), HALO)]
    else:
        core = field[2]
        pad[own, rows, :] = field[side][...]
        pad[inner, rows, :] = core[pl.ds(up * (core.shape[0] - HALO), HALO)]


def fill_core(pad, field, width):
    margins(pad, width)
    slab = pad.shape[0]
    rows = slice(PAD, PAD + width)
    if len(field) == 1:
        pad[:, rows, :] = field[0][...]
    else:
        for side in (0, 1):
            pad[pl.ds(high(side) * (slab - HALO), HALO), rows, :] = field[side][...]
        pad[HALO : slab - HALO, rows, :] = field[2][...]


def place_of(side, field, slab):
    if len(field) == 1:
        return field[0], HALO if side == 2 else high(side) * (slab - HALO)
    return field[side], 0


def stencil(pad, p, width, lane):
    rows = slice(PAD, PAD + width)
    center = pad[p, rows, :]
    length = center.shape[1]
    result = (3.0 * coeffs[0]) * center
    for k in range(1, 5):
        along = pad[p + k, rows, :] + pad[p - k, rows, :]
        along = along + pad[p, PAD + k : PAD + k + width, :]
        along = along + pad[p, PAD - k : PAD - k + width, :]
        up = pltpu.roll(center, length - k, 1)
        down = pltpu.roll(center, k, 1)
        along = along + jnp.where(lane < length - k, up, 0.0)
        along = along + jnp.where(lane >= k, down, 0.0)
        result = result + coeffs[k] * along
    return center, result


def fold(values):
    width, length = values.shape
    return jnp.sum(values.reshape(width // 8, 8, length), axis=0)


def march(count, body, carry=None):
    return lax.fori_loop(0, count, body, carry, unroll=2)


def kernel_call(kernel, small, arrays, outs, scratch, planes):
    return pl.pallas_call(
        kernel,
        out_shape=tuple(outs),
        in_specs=[SMEM] * len(small) + [VMEM] * len(arrays),
        out_specs=tuple([VMEM] * len(outs)),
        scratch_shapes=scratch,
        compiler_params=params(),
        cost_estimate=cost(planes),
    )(*small, *arrays)


def grouped(refs, sizes):
    found = []
    for size in sizes:
        found.append(refs[:size])
        refs = refs[size:]
    return found, list(refs)


def sizes_of(side, slab, width, length):
    planes = slab - 2 * HALO if side == 2 else HALO
    depth = slab if side == 2 else 3 * HALO
    return planes, pltpu.VMEM((depth, width + 2 * PAD, length), jnp.float32)


def step_planes(side, pad, halo, halo_at, cur, old, c_ref, next_ref, lap_ref):
    slab, width, length = c_ref.shape
    if side == 2:
        fill_core(pad, cur, width)
        plane = HALO
    else:
        fill_edge(pad, side, halo[0], halo_at, cur, slab, width)
        plane = high(side) * (slab - HALO)
    lane = lax.broadcasted_iota(jnp.int32, (width, length), 1)
    old_ref, old_at = place_of(side, old, slab)

    def body(i, _):
        center, lap = stencil(pad, HALO + i, width, lane)
        if lap_ref is not None:
            lap_ref[i] = lap
        next_ref[i] = 2.0 * center - old_ref[old_at + i] + c_ref[plane + i] * lap

    march(next_ref.shape[0], body)


def forward(side, step, halo, cur, old, courant, after, wavelet, source):
    slab, width, length = courant.shape
    planes, pad_scratch = sizes_of(side, slab, width, length)
    groups = [list(halo), list(cur), list(old), [courant], list(after)]
    sizes = [len(g) for g in groups]

    def kernel(wave_ref, source_ref, *refs):
        (halo_refs, cur_refs, old_refs, (c_ref,), _), refs = grouped(refs, sizes)
        next_ref, lap_ref, pad = refs
        step_planes(side, pad, halo_refs, 0, cur_refs, old_refs, c_ref, next_ref, lap_ref)
        plane = HALO if side == 2 else high(side) * (slab - HALO)
        base = (lax.axis_index("depth") * slab + plane) * (width * length)
        local = source_ref[0] - base

        @pl.when((local >= 0) & (local < planes * width * length))
        def _():
            row, y = split(local, length)
            at, x = split(row, width)
            spot = lax.broadcasted_iota(jnp.int32, (1, length), 1) == y
            add = jnp.where(spot, wave_ref[0, step], 0.0)
            next_ref[at, pl.ds(x, 1), :] = next_ref[at, pl.ds(x, 1), :] + add

    outs = [f32(planes, width, length)] * 2
    arrays = sum(groups, [])
    return kernel_call(kernel, [wavelet, source], arrays, outs, [pad_scratch], planes)


def adjoint_step(
    side, step, pad, halo, halo_at, cur, old, c_ref, field_ref, list_ref, obs_ref, next_ref
):
    slab, width, length = c_ref.shape
    step_planes(side, pad, halo, halo_at, cur, old, c_ref, next_ref, None)
    column = lax.broadcasted_iota(jnp.int32, (1, length), 1)

    def inject(k, _):
        row, y = split(list_ref[2 * side, k], length)
        at, x = split(row, width)
        pred = field_ref[at, pl.ds(x, 1), :]
        res = jnp.where(column == y, pred - obs_ref[step, list_ref[2 * side + 1, k]], 0.0)
        next_ref[at, pl.ds(x, 1), :] = next_ref[at, pl.ds(x, 1), :] + res

    lax.fori_loop(0, list_ref[6, side], inject, None)


def adjoint(side, step, halo, halo_at, cur, old, courant, field, after, listing, observed):
    slab, width, length = courant.shape
    planes, pad_scratch = sizes_of(side, slab, width, length)
    groups = [list(halo), list(cur), list(old), [courant, field], list(after)]
    sizes = [len(g) for g in groups]

    def kernel(list_ref, obs_ref, *refs):
        (halo_refs, cur_refs, old_refs, (c_ref, field_ref), _), refs = grouped(refs, sizes)
        next_ref, pad = refs
        adjoint_step(
            side, step, pad, halo_refs, halo_at, cur_refs, old_refs, c_ref, field_ref,
            list_ref, obs_ref, next_ref,
        )

    outs = [f32(planes, width, length)]
    arrays = sum(groups, [])
    return kernel_call(kernel, [listing, observed], arrays, outs, [pad_scratch], planes)[0]


def adjoint_last(
    side, halo, cur, old, courant, field, laps, adjoints, tile, other, after, listing, observed
):
    slab, width, length = courant.shape
    planes, pad_scratch = sizes_of(side, slab, width, length)
    groups = [list(halo), list(cur), list(old), [courant, field], list(laps)]
    groups += [list(adjoints), list(tile) + list(other), list(after)]
    sizes = [len(g) for g in groups]

    def kernel(list_ref, obs_ref, *refs):
        found, refs = grouped(refs, sizes)
        halo_refs, cur_refs, old_refs, (c_ref, field_ref), lap_refs, adj_refs, more, _ = found
        next_ref, pad = refs[-2:]
        adjoint_step(
            side, 0, pad, halo_refs, 0, cur_refs, old_refs, c_ref, field_ref,
            list_ref, obs_ref, next_ref,
        )
        core = lax.axis_index("shot") % 2

        def product(i):
            value = next_ref[i] * lap_refs[0][i]
            for lap_ref, adj_ref in zip(lap_refs[1:], adj_refs):
                value = value + adj_ref[i] * lap_ref[i]
            return value

        if side == 2:
            keep_ref, send_ref = refs[:2]
            half = planes // 2

            def body(i, _):
                keep_ref[i] = product(core * half + i)
                send_ref[i] = product((1 - core) * half + i)

            march(half, body)
        elif side == 0:
            for i in range(HALO):
                refs[0][i] = product(i)
        else:
            tile_ref, other_ref = more

            def write(own_ref, far_ref):
                for i in range(HALO):
                    rows = slice(i * width, (i + 1) * width)
                    own_ref[rows, :] = other_ref[i]
                    far_ref[rows, :] = product(i)

            @pl.when(core == 0)
            def _():
                write(refs[0], refs[1])

            @pl.when(core == 1)
            def _():
                write(refs[1], refs[0])

            for ref in refs[:2]:
                ref[HALO * width : HALO * width + 8, :] = tile_ref[...]

    if side == 2:
        outs = [f32(planes // 2, width, length)] * 2
    elif side == 0:
        outs = [f32(planes, width, length)]
    else:
        outs = [f32(HALO * width + 8, length)] * 2
    arrays = sum(groups, [])
    scratch = [pltpu.VMEM((planes, width, length), jnp.float32), pad_scratch]
    return kernel_call(kernel, [listing, observed], arrays, outs, scratch, planes)


def curvature(laps):
    number = len(laps)
    inner, width, length = laps[0][2].shape
    half = inner // 2
    size = half + HALO

    def kernel(*refs):
        sides = [refs[n * number : (n + 1) * number] for n in range(3)]
        keep_ref, send_ref, tile_ref = refs[3 * number :]
        core = lax.axis_index("shot") % 2

        def squares(lap_refs, at):
            value = lap_refs[0][at] * lap_refs[0][at]
            for ref in lap_refs[1:]:
                value = value + ref[at] * ref[at]
            return value

        def body(i, total):
            for ref, start in ((keep_ref, core * half), (send_ref, (1 - core) * half)):
                value = squares(sides[2], start + i)
                ref[i] = value
                total = total + fold(value)
            return total

        tile_ref[...] = march(half, body, jnp.zeros((8, length), jnp.float32))

        def outer(first_ref, second_ref):
            total = jnp.zeros((8, length), jnp.float32)
            for i in range(HALO):
                for ref, lap_refs in ((first_ref, sides[0]), (second_ref, sides[1])):
                    value = squares(lap_refs, i)
                    ref[half + i] = value
                    total = total + fold(value)
            tile_ref[...] = tile_ref[...] + total

        @pl.when(core == 0)
        def _():
            outer(keep_ref, send_ref)

        @pl.when(core == 1)
        def _():
            outer(send_ref, keep_ref)

    outs = [f32(size, width, length)] * 2 + [f32(8, length)]
    arrays = [lap[n] for n in range(3) for lap in laps]
    return kernel_call(kernel, [], arrays, outs, [], 8)


def list_receivers(cells, slab, width, length):
    count = cells.shape[0]
    area = width * length

    def kernel(cell_ref, out_ref):
        offset = lax.axis_index("depth") * (slab * area)
        starts = [high(0) * ((slab - HALO) * area), high(1) * ((slab - HALO) * area), HALO * area]
        lengths = [HALO * area, HALO * area, (slab - 2 * HALO) * area]

        def body(r, counts):
            cell = cell_ref[r] - offset
            found = []
            for n in range(3):
                local = cell - starts[n]
                inside = (local >= 0) & (local < lengths[n])
                out_ref[2 * n, counts[n]] = local
                out_ref[2 * n + 1, counts[n]] = r
                found.append(counts[n] + inside.astype(jnp.int32))
            return tuple(found)

        counts = lax.fori_loop(0, count, body, (jnp.int32(0),) * 3, unroll=8)
        for n in range(3):
            out_ref[6, n] = counts[n]

    return pl.pallas_call(
        kernel,
        out_shape=jax.ShapeDtypeStruct((7, 2 * count), jnp.int32),
        in_specs=[SMEM],
        out_specs=SMEM,
        compiler_params=params(),
        cost_estimate=cost(8),
    )(cells)


def pack(field, adjoint_field):
    odd = lax.axis_index("depth") % 2
    far = field.shape[0] - HALO
    found = []
    for start in ((1 - odd) * far, odd * far):
        planes = [lax.dynamic_slice_in_dim(v, start, HALO, 0) for v in (field, adjoint_field)]
        found.append(jnp.concatenate(planes, axis=0))
    return found


def refresh(courant, inner_parts, outer_parts, curv, table, plan):
    slab, width, length = courant.shape
    half = inner_parts[0].shape[0]
    number = len(inner_parts)
    cells = slab * width * length * lax.axis_size("depth")

    def kernel(table_ref, plan_ref, c_ref, curv_ref, *rest):
        inner_refs = rest[:number]
        outer_refs = rest[number : 2 * number]
        out_ref = rest[2 * number]
        tail = slice(HALO * width, HALO * width + 8)
        tile = outer_refs[0][tail, :]
        for ref in outer_refs[1:]:
            tile = tile + ref[tail, :]
        level = jnp.sum(tile) / cells + 1e-06
        extra = table_ref[plan_ref[0]] * level
        core = lax.axis_index("shot") % 2
        start = HALO + core * half

        def body(i, _):
            grad = inner_refs[0][i]
            for ref in inner_refs[1:]:
                grad = grad + ref[i]
            out_ref[i] = c_ref[start + i] - grad / (curv_ref[i] + extra)

        march(half, body)
        odd = lax.axis_index("depth") % 2
        up = core + odd == 0
        up = (up | (core + odd == 2)).astype(jnp.int32)
        for i in range(HALO):
            rows = slice(i * width, (i + 1) * width)
            grad = outer_refs[0][rows, :]
            for ref in outer_refs[1:]:
                grad = grad + ref[rows, :]
            model = c_ref[up * (slab - HALO) + i]
            out_ref[half + i] = model - grad / (curv_ref[half + i] + extra)

    arrays = [courant, curv, *inner_parts, *outer_parts]
    outs = [f32(half + HALO, width, length)]
    return kernel_call(kernel, [table, plan], arrays, outs, [], half)[0]


def assemble(own, other, slab):
    size, width, length = own.shape
    inner = size - HALO

    def kernel(own_ref, other_ref, out_ref, sems):
        core = lax.axis_index("shot") % 2
        up = (lax.axis_index("depth") + core + 1) % 2
        copies = []
        for n, (ref, c, u) in enumerate([(own_ref, core, up), (other_ref, 1 - core, 1 - up)]):
            for m, (first, count, start) in enumerate(
                [(0, inner, HALO + c * inner), (inner, HALO, u * (slab - HALO))]
            ):
                copies.append(
                    pltpu.make_async_copy(
                        ref.at[pl.ds(first, count)],
                        out_ref.at[pl.ds(start, count)],
                        sems.at[2 * n + m],
                    )
                )
        for copy in copies:
            copy.start()
        for copy in copies:
            copy.wait()

    return pl.pallas_call(
        kernel,
        out_shape=f32(slab, width, length),
        in_specs=[VMEM] * 2,
        out_specs=HBM,
        scratch_shapes=[pltpu.SemaphoreType.DMA((4,))],
        compiler_params=params(),
        cost_estimate=cost(8),
    )(own, other)


def exchange(values, side):
    links = []
    for i in range(side, lax.axis_size("depth") - 1, 2):
        links += [(i, i + 1), (i + 1, i)]
    return lax.ppermute(values, "depth", links)


def swap(values, axis, bit):
    count = lax.axis_size(axis)
    return lax.ppermute(values, axis, [(i, i ^ bit) for i in range(count)])


def total_parts(keep, send):
    parts = [keep, swap(send, "shot", 1)]
    bit = 2
    while bit < lax.axis_size("shot"):
        here = parts[0] + parts[1]
        parts = [here, swap(here, "shot", bit)]
        bit *= 2
    return parts


def on_device(
    field_prev,
    field_now,
    adjoint_next,
    adjoint_after,
    courant,
    wavelet,
    source_cell,
    receiver_cell,
    observed,
    damping_table,
    plan_step,
):
    slab, width, length = courant.shape
    halos = [exchange(v, side) for side, v in enumerate(pack(field_now[0], adjoint_next[0]))]
    first_halos = halos
    start, before = field_now[0], field_prev[0]
    first, second = adjoint_next[0], adjoint_after[0]
    listing = list_receivers(receiver_cell[0], slab, width, length)
    traces = observed[0]
    old, cur = (before,), (start,)
    laps, fields = [], []
    after = [listing]
    for step in range(STEPS):
        core = forward(2, step, (), cur, old, courant, (), wavelet, source_cell)
        after = after + [core[0]]
        if step == STEPS - 1:
            core_adj = adjoint(
                2, step, (), 0, (first,), (second,), courant, core[0], (), listing, traces
            )
            after = after + [core_adj]
        parts, coming = [], []
        for side in (0, 1):
            edge = forward(
                side, step, halos[side : side + 1], cur, old, courant, after, wavelet, source_cell
            )
            parts.append(edge)
            if step < STEPS - 1:
                coming.append(exchange(edge[0], side))
                after = [edge[0]]
        laps.append((parts[0][1], parts[1][1], core[1]))
        fields.append((parts[0][0], parts[1][0], core[0]))
        old, cur = cur, fields[-1]
        halos, after = coming, []
    old, cur = (second,), (first,)
    halos, halo_at = first_halos, HALO
    adjoints = []
    keep, send, tile = curvature(laps)
    curv = sum(total_parts(keep, send))
    bit = 1
    extra = []
    for step in range(STEPS - 1, 0, -1):
        field = fields[step]
        if step < STEPS - 1:
            core_adj = adjoint(2, step, (), 0, cur, old, courant, field[2], (), listing, traces)
        after = extra + [core_adj]
        edges, coming = [], []
        for side in (0, 1):
            edge = adjoint(
                side, step, halos[side : side + 1], halo_at, cur, old, courant, field[side], after,
                listing, traces,
            )
            edges.append(edge)
            coming.append(exchange(edge, side))
            after = [edge]
        adjoints.insert(0, (edges[0], edges[1], core_adj))
        old, cur = cur, adjoints[0]
        halos, halo_at = coming, 0
        if bit < lax.axis_size("depth"):
            tile = tile + swap(tile, "depth", bit)
            bit *= 2
            extra = [tile]
    while bit < lax.axis_size("depth"):
        tile = tile + swap(tile, "depth", bit)
        bit *= 2
    found = []
    for side, tiles, other in ((2, [], 0), (0, [], 0), (1, [tile], 1)):
        found.append(
            adjoint_last(
                side, halos[side : side + 1], cur, old, courant, fields[0][side],
                [lap[side] for lap in laps], [a[side] for a in adjoints], tiles,
                found[1] if other else [], [curv] if side == 2 else found[0][:1], listing, traces,
            )
        )
    inner_parts = total_parts(*found[0])
    outer_parts = total_parts(*found[2])
    own = refresh(courant, inner_parts, outer_parts, curv, damping_table, plan_step)
    return assemble(own, swap(own, "shot", 1), slab)


def solution(mesh):
    in_specs = (
        P("shot", "depth", None, None),
        P("shot", "depth", None, None),
        P("shot", "depth", None, None),
        P("shot", "depth", None, None),
        P("depth", None, None),
        P("shot", None),
        P("shot"),
        P("shot", None),
        P("shot", None, None),
        P(),
        P(),
    )
    out_specs = P("depth", None, None)
    return jax.shard_map(
        on_device, mesh=mesh, in_specs=in_specs, out_specs=out_specs, check_vma=False
    )
```

```python
import jax
import jax.numpy as jnp
from jax import lax
from jax.experimental import pallas as pl
from jax.experimental.pallas import tpu as pltpu
from jax.sharding import PartitionSpec as P

STEPS = 4
HALO = 4
ROWS = 8
PAD = HALO * ROWS

coeffs = (-205.0 / 72.0, 8.0 / 5.0, -1.0 / 5.0, 8.0 / 315.0, -1.0 / 560.0)

VMEM = pl.BlockSpec(memory_space=pltpu.VMEM)
SMEM = pl.BlockSpec(memory_space=pltpu.SMEM)
HBM = pl.BlockSpec(memory_space=pltpu.HBM)


def f32(*shape):
    return jax.ShapeDtypeStruct(shape, jnp.float32)


def params():
    return pltpu.CompilerParams(vmem_limit_bytes=6 * 2**20)


def cost(planes):
    return pl.CostEstimate(
        flops=planes * 10**4, bytes_accessed=planes * 2**10, transcendentals=0
    )


def split(value, size):
    if size & (size - 1) == 0:
        return value >> (size.bit_length() - 1), value & (size - 1)
    return value // size, value % size


def spread(x, width):
    s, g = split(x, width // ROWS)
    return g * ROWS + s


def interleave(put, get, width):
    for g in range(width // ROWS):
        put(g * ROWS, get(pl.ds(g, ROWS, stride=width // ROWS)))


def margins(pad, first, count, width):
    length = pad.shape[2]
    place = lax.broadcasted_iota(jnp.int32, (ROWS, length), 0)

    def body(i, _):
        p = first + i
        for j in range(HALO):
            at = j * ROWS
            low = pltpu.roll(pad[p, width + at : width + at + ROWS, :], 1, 0)
            pad[p, at : at + ROWS, :] = jnp.where(place == 0, 0.0, low)
            top = pltpu.roll(pad[p, PAD + at : PAD + at + ROWS, :], ROWS - 1, 0)
            beyond = PAD + width + at
            pad[p, beyond : beyond + ROWS, :] = jnp.where(place == ROWS - 1, 0.0, top)

    march(count, body)


def high(side):
    odd = lax.axis_index("depth") % 2
    return odd if side else 1 - odd


def fill_edge(pad, side, halo, halo_at, field, slab, width):
    up = high(side)
    rows = slice(PAD, PAD + width)
    if len(field) == 1:
        for i in range(HALO):

            def put(at, value, i=i):
                pad[up * (2 * HALO) + i, PAD + at : PAD + at + ROWS, :] = value

            interleave(put, lambda spot, i=i: halo[halo_at + i, spot, :], width)
    else:
        pad[pl.ds(up * (2 * HALO), HALO), rows, :] = halo[halo_at : halo_at + HALO]
    inner = pl.ds((1 - up) * (2 * HALO), HALO)
    own = slice(HALO, 2 * HALO)
    if len(field) == 1:
        (ref,) = field
        slab = ref.shape[0]
        pad[own, rows, :] = ref[pl.ds(up * (slab - HALO), HALO)]
        pad[inner, rows, :] = ref[pl.ds(HALO + up * (slab - 3 * HALO), HALO)]
    else:
        core = field[2]
        pad[own, rows, :] = field[side][...]
        pad[inner, rows, :] = core[pl.ds(up * (core.shape[0] - HALO), HALO)]
    margins(pad, HALO, HALO, width)


def fill_core(pad, field, width):
    slab = pad.shape[0]
    rows = slice(PAD, PAD + width)
    if len(field) == 1:
        pad[:, rows, :] = field[0][...]
    else:
        for side in (0, 1):
            pad[pl.ds(high(side) * (slab - HALO), HALO), rows, :] = field[side][...]
        pad[HALO : slab - HALO, rows, :] = field[2][...]
    margins(pad, HALO, slab - 2 * HALO, width)


def place_of(side, field, slab):
    if len(field) == 1:
        return field[0], HALO if side == 2 else high(side) * (slab - HALO)
    return field[side], 0


def stencil(pad, p, width, lane):
    rows = slice(PAD, PAD + width)
    plane = pad[p]
    center = plane[rows]
    length = center.shape[1]
    result = (3.0 * coeffs[0]) * center
    for k in range(1, 5):
        along = pad[p + k, rows, :] + pad[p - k, rows, :]
        along = along + plane[PAD + k * ROWS : PAD + k * ROWS + width]
        along = along + plane[PAD - k * ROWS : PAD - k * ROWS + width]
        up = pltpu.roll(center, length - k, 1)
        down = pltpu.roll(center, k, 1)
        along = along + jnp.where(lane < length - k, up, 0.0)
        along = along + jnp.where(lane >= k, down, 0.0)
        result = result + coeffs[k] * along
    return center, result


def fold(values):
    width, length = values.shape
    return jnp.sum(values.reshape(width // 8, 8, length), axis=0)


def march(count, body, carry=None):
    return lax.fori_loop(0, count, body, carry, unroll=2)


def kernel_call(kernel, small, arrays, outs, scratch, planes):
    return pl.pallas_call(
        kernel,
        out_shape=tuple(outs),
        in_specs=[SMEM] * len(small) + [VMEM] * len(arrays),
        out_specs=tuple([VMEM] * len(outs)),
        scratch_shapes=scratch,
        compiler_params=params(),
        cost_estimate=cost(planes),
    )(*small, *arrays)


def grouped(refs, sizes):
    found = []
    for size in sizes:
        found.append(refs[:size])
        refs = refs[size:]
    return found, list(refs)


def sizes_of(side, slab, width, length):
    planes = slab - 2 * HALO if side == 2 else HALO
    depth = slab if side == 2 else 3 * HALO
    return planes, pltpu.VMEM((depth, width + 2 * PAD, length), jnp.float32)


def step_planes(side, pad, halo, halo_at, cur, old, c_ref, next_ref, lap_ref):
    slab, width, length = c_ref.shape
    if side == 2:
        fill_core(pad, cur, width)
        plane = HALO
    else:
        fill_edge(pad, side, halo[0], halo_at, cur, slab, width)
        plane = high(side) * (slab - HALO)
    lane = lax.broadcasted_iota(jnp.int32, (width, length), 1)
    old_ref, old_at = place_of(side, old, slab)

    def body(i, _):
        center, lap = stencil(pad, HALO + i, width, lane)
        if lap_ref is not None:
            lap_ref[i] = lap
        next_ref[i] = 2.0 * center - old_ref[old_at + i] + c_ref[plane + i] * lap

    march(next_ref.shape[0], body)


def forward(side, step, halo, cur, old, courant, after, wavelet, source):
    slab, width, length = courant.shape
    planes, pad_scratch = sizes_of(side, slab, width, length)
    groups = [list(halo), list(cur), list(old), [courant], list(after)]
    sizes = [len(g) for g in groups]

    def kernel(wave_ref, source_ref, *refs):
        (halo_refs, cur_refs, old_refs, (c_ref,), _), refs = grouped(refs, sizes)
        next_ref, lap_ref, pad = refs
        step_planes(side, pad, halo_refs, 0, cur_refs, old_refs, c_ref, next_ref, lap_ref)
        plane = HALO if side == 2 else high(side) * (slab - HALO)
        base = (lax.axis_index("depth") * slab + plane) * (width * length)
        local = source_ref[0] - base

        @pl.when((local >= 0) & (local < planes * width * length))
        def _():
            row, y = split(local, length)
            at, x = split(row, width)
            x = spread(x, width)
            spot = lax.broadcasted_iota(jnp.int32, (1, length), 1) == y
            add = jnp.where(spot, wave_ref[0, step], 0.0)
            next_ref[at, pl.ds(x, 1), :] = next_ref[at, pl.ds(x, 1), :] + add

    outs = [f32(planes, width, length)] * 2
    arrays = sum(groups, [])
    return kernel_call(kernel, [wavelet, source], arrays, outs, [pad_scratch], planes)


def adjoint_step(
    side, step, pad, halo, halo_at, cur, old, c_ref, field_ref, list_ref, obs_ref, next_ref
):
    slab, width, length = c_ref.shape
    step_planes(side, pad, halo, halo_at, cur, old, c_ref, next_ref, None)
    column = lax.broadcasted_iota(jnp.int32, (1, length), 1)

    def inject(k, _):
        row, y = split(list_ref[2 * side, k], length)
        at, x = split(row, width)
        x = spread(x, width)
        pred = field_ref[at, pl.ds(x, 1), :]
        res = jnp.where(column == y, pred - obs_ref[step, list_ref[2 * side + 1, k]], 0.0)
        next_ref[at, pl.ds(x, 1), :] = next_ref[at, pl.ds(x, 1), :] + res

    lax.fori_loop(0, list_ref[6, side], inject, None)


def adjoint(side, step, halo, halo_at, cur, old, courant, field, after, listing, observed):
    slab, width, length = courant.shape
    planes, pad_scratch = sizes_of(side, slab, width, length)
    groups = [list(halo), list(cur), list(old), [courant, field], list(after)]
    sizes = [len(g) for g in groups]

    def kernel(list_ref, obs_ref, *refs):
        (halo_refs, cur_refs, old_refs, (c_ref, field_ref), _), refs = grouped(refs, sizes)
        next_ref, pad = refs
        adjoint_step(
            side, step, pad, halo_refs, halo_at, cur_refs, old_refs, c_ref, field_ref,
            list_ref, obs_ref, next_ref,
        )

    outs = [f32(planes, width, length)]
    arrays = sum(groups, [])
    return kernel_call(kernel, [listing, observed], arrays, outs, [pad_scratch], planes)[0]


def adjoint_last(
    side, halo, cur, old, courant, field, laps, adjoints, tile, other, after, listing, observed
):
    slab, width, length = courant.shape
    planes, pad_scratch = sizes_of(side, slab, width, length)
    groups = [list(halo), list(cur), list(old), [courant, field], list(laps)]
    groups += [list(adjoints), list(tile) + list(other), list(after)]
    sizes = [len(g) for g in groups]

    def kernel(list_ref, obs_ref, *refs):
        found, refs = grouped(refs, sizes)
        halo_refs, cur_refs, old_refs, (c_ref, field_ref), lap_refs, adj_refs, more, _ = found
        next_ref, pad = refs[-2:]
        adjoint_step(
            side, 0, pad, halo_refs, 0, cur_refs, old_refs, c_ref, field_ref,
            list_ref, obs_ref, next_ref,
        )
        core = lax.axis_index("shot") % 2

        def product(i):
            value = next_ref[i] * lap_refs[0][i]
            for lap_ref, adj_ref in zip(lap_refs[1:], adj_refs):
                value = value + adj_ref[i] * lap_ref[i]
            return value

        if side == 2:
            keep_ref, send_ref = refs[:2]
            half = planes // 2

            def body(i, _):
                keep_ref[i] = product(core * half + i)
                send_ref[i] = product((1 - core) * half + i)

            march(half, body)
        elif side == 0:
            for i in range(HALO):
                refs[0][i] = product(i)
        else:
            tile_ref, tiles_ref, other_ref = more

            def write(own_ref, far_ref):
                for i in range(HALO):
                    rows = slice(i * width, (i + 1) * width)
                    own_ref[rows, :] = other_ref[i]
                    far_ref[rows, :] = product(i)

            @pl.when(core == 0)
            def _():
                write(refs[0], refs[1])

            @pl.when(core == 1)
            def _():
                write(refs[1], refs[0])

            for ref in refs[:2]:
                ref[HALO * width : HALO * width + 8, :] = tile_ref[...] + tiles_ref[...]

    if side == 2:
        outs = [f32(planes // 2, width, length)] * 2
    elif side == 0:
        outs = [f32(planes, width, length)]
    else:
        outs = [f32(HALO * width + 8, length)] * 2
    arrays = sum(groups, [])
    scratch = [pltpu.VMEM((planes, width, length), jnp.float32), pad_scratch]
    return kernel_call(kernel, [listing, observed], arrays, outs, scratch, planes)


def curvature(laps, after):
    number = len(laps)
    inner, width, length = laps[0][2].shape
    half = inner // 2
    size = half + HALO

    def kernel(*refs):
        sides = [refs[n * number : (n + 1) * number] for n in range(3)]
        keep_ref, send_ref, tile_ref = refs[3 * number + 1 :]
        core = lax.axis_index("shot") % 2

        def squares(lap_refs, at):
            value = lap_refs[0][at] * lap_refs[0][at]
            for ref in lap_refs[1:]:
                value = value + ref[at] * ref[at]
            return value

        def body(i, total):
            for ref, start in ((keep_ref, core * half), (send_ref, (1 - core) * half)):
                value = squares(sides[2], start + i)
                ref[i] = value
                total = total + fold(value)
            return total

        tile_ref[...] = march(half, body, jnp.zeros((8, length), jnp.float32))

        def outer(first_ref, second_ref):
            total = jnp.zeros((8, length), jnp.float32)
            for i in range(HALO):
                for ref, lap_refs in ((first_ref, sides[0]), (second_ref, sides[1])):
                    value = squares(lap_refs, i)
                    ref[half + i] = value
                    total = total + fold(value)
            tile_ref[...] = tile_ref[...] + total

        @pl.when(core == 0)
        def _():
            outer(keep_ref, send_ref)

        @pl.when(core == 1)
        def _():
            outer(send_ref, keep_ref)

    outs = [f32(size, width, length)] * 2 + [f32(8, length)]
    arrays = [lap[n] for n in range(3) for lap in laps] + [after]
    return kernel_call(kernel, [], arrays, outs, [], 8)


def list_receivers(cells, slab, width, length):
    count = cells.shape[0]
    area = width * length

    def kernel(cell_ref, out_ref):
        offset = lax.axis_index("depth") * (slab * area)
        starts = [high(0) * ((slab - HALO) * area), high(1) * ((slab - HALO) * area), HALO * area]
        lengths = [HALO * area, HALO * area, (slab - 2 * HALO) * area]

        def body(r, counts):
            cell = cell_ref[r] - offset
            found = []
            for n in range(3):
                local = cell - starts[n]
                inside = (local >= 0) & (local < lengths[n])
                out_ref[2 * n, counts[n]] = local
                out_ref[2 * n + 1, counts[n]] = r
                found.append(counts[n] + inside.astype(jnp.int32))
            return tuple(found)

        counts = lax.fori_loop(0, count, body, (jnp.int32(0),) * 3, unroll=8)
        for n in range(3):
            out_ref[6, n] = counts[n]

    return pl.pallas_call(
        kernel,
        out_shape=jax.ShapeDtypeStruct((7, 2 * count), jnp.int32),
        in_specs=[SMEM],
        out_specs=SMEM,
        compiler_params=params(),
        cost_estimate=cost(8),
    )(cells)


def interleaved(*arrays):
    number = len(arrays)
    slab, width, length = arrays[0].shape

    def kernel(*refs):
        def body(i, _):
            for ref, out_ref in zip(refs[:number], refs[number:]):

                def put(at, value, out_ref=out_ref):
                    out_ref[i, at : at + ROWS, :] = value

                interleave(put, lambda spot, ref=ref: ref[i, spot, :], width)

        march(slab, body)

    outs = [f32(slab, width, length)] * number
    return kernel_call(kernel, [], list(arrays), outs, [], 8)


def pack(field, adjoint_field):
    odd = lax.axis_index("depth") % 2
    far = field.shape[0] - HALO
    found = []
    for start in ((1 - odd) * far, odd * far):
        planes = [lax.dynamic_slice_in_dim(v, start, HALO, 0) for v in (field, adjoint_field)]
        found.append(jnp.concatenate(planes, axis=0))
    return found


def refresh(courant, inner_parts, outer_parts, curv, table, plan):
    slab, width, length = courant.shape
    half = inner_parts[0].shape[0]
    number = len(inner_parts)
    cells = slab * width * length * lax.axis_size("depth")

    def kernel(table_ref, plan_ref, c_ref, curv_ref, *rest):
        inner_refs = rest[:number]
        outer_refs = rest[number : 2 * number]
        out_ref = rest[2 * number]
        tail = slice(HALO * width, HALO * width + 8)
        tile = outer_refs[0][tail, :]
        for ref in outer_refs[1:]:
            tile = tile + ref[tail, :]
        level = jnp.sum(tile) / cells + 1e-06
        extra = table_ref[plan_ref[0]] * level
        core = lax.axis_index("shot") % 2
        start = HALO + core * half

        def store(i, value):
            for g in range(width // ROWS):
                spot = pl.ds(g, ROWS, stride=width // ROWS)
                out_ref[i, spot, :] = value[g * ROWS : (g + 1) * ROWS]

        def body(i, _):
            grad = inner_refs[0][i]
            for ref in inner_refs[1:]:
                grad = grad + ref[i]
            store(i, c_ref[start + i] - grad / (curv_ref[i] + extra))

        march(half, body)
        odd = lax.axis_index("depth") % 2
        up = core + odd == 0
        up = (up | (core + odd == 2)).astype(jnp.int32)
        for i in range(HALO):
            rows = slice(i * width, (i + 1) * width)
            grad = outer_refs[0][rows, :]
            for ref in outer_refs[1:]:
                grad = grad + ref[rows, :]
            model = c_ref[up * (slab - HALO) + i]
            store(half + i, model - grad / (curv_ref[half + i] + extra))

    arrays = [courant, curv, *inner_parts, *outer_parts]
    outs = [f32(half + HALO, width, length)]
    return kernel_call(kernel, [table, plan], arrays, outs, [], half)[0]


def assemble(own, other, slab):
    size, width, length = own.shape
    inner = size - HALO

    def kernel(own_ref, other_ref, out_ref, sems):
        core = lax.axis_index("shot") % 2
        up = (lax.axis_index("depth") + core + 1) % 2
        copies = []
        for n, (ref, c, u) in enumerate([(own_ref, core, up), (other_ref, 1 - core, 1 - up)]):
            for m, (first, count, start) in enumerate(
                [(0, inner, HALO + c * inner), (inner, HALO, u * (slab - HALO))]
            ):
                copies.append(
                    pltpu.make_async_copy(
                        ref.at[pl.ds(first, count)],
                        out_ref.at[pl.ds(start, count)],
                        sems.at[2 * n + m],
                    )
                )
        for copy in copies:
            copy.start()
        for copy in copies:
            copy.wait()

    return pl.pallas_call(
        kernel,
        out_shape=f32(slab, width, length),
        in_specs=[VMEM] * 2,
        out_specs=HBM,
        scratch_shapes=[pltpu.SemaphoreType.DMA((4,))],
        compiler_params=params(),
        cost_estimate=cost(8),
    )(own, other)


def exchange(values, side):
    links = []
    for i in range(side, lax.axis_size("depth") - 1, 2):
        links += [(i, i + 1), (i + 1, i)]
    return lax.ppermute(values, "depth", links)


def swap(values, axis, bit):
    count = lax.axis_size(axis)
    return lax.ppermute(values, axis, [(i, i ^ bit) for i in range(count)])


def sum_of(values, other, after):
    def kernel(values_ref, other_ref, _, out_ref):
        def body(i, _):
            out_ref[i] = values_ref[i] + other_ref[i]

        march(values.shape[0], body)

    return kernel_call(kernel, [], [values, other, after], [f32(*values.shape)], [], 8)[0]


def total_parts(keep, send, after=None):
    parts = [keep, swap(send, "shot", 1)]
    bit = 2
    while bit < lax.axis_size("shot"):
        if after is not None and bit == 2:
            here = sum_of(*parts, after)
        else:
            here = parts[0] + parts[1]
        parts = [here, swap(here, "shot", bit)]
        bit *= 2
    return parts


def on_device(
    field_prev,
    field_now,
    adjoint_next,
    adjoint_after,
    courant,
    wavelet,
    source_cell,
    receiver_cell,
    observed,
    damping_table,
    plan_step,
):
    slab, width, length = courant.shape
    halos = [exchange(v, side) for side, v in enumerate(pack(field_now[0], adjoint_next[0]))]
    first_halos = halos
    start, before, courant = interleaved(field_now[0], field_prev[0], courant)
    first, second = interleaved(adjoint_next[0], adjoint_after[0])
    listing = list_receivers(receiver_cell[0], slab, width, length)
    traces = observed[0]
    old, cur = (before,), (start,)
    laps, fields = [], []
    after = [listing]
    for step in range(STEPS):
        core = forward(2, step, (), cur, old, courant, (), wavelet, source_cell)
        after = after + [core[0]]
        if step == STEPS - 1:
            core_adj = adjoint(
                2, step, (), 0, (first,), (second,), courant, core[0], (), listing, traces
            )
            after = after + [core_adj]
        parts, coming = [], []
        for side in (0, 1):
            edge = forward(
                side, step, halos[side : side + 1], cur, old, courant, after, wavelet, source_cell
            )
            parts.append(edge)
            if step < STEPS - 1:
                coming.append(exchange(edge[0], side))
                after = [edge[0]]
        laps.append((parts[0][1], parts[1][1], core[1]))
        fields.append((parts[0][0], parts[1][0], core[0]))
        old, cur = cur, fields[-1]
        halos, after = coming, []
    old, cur = (second,), (first,)
    halos, halo_at = first_halos, HALO
    adjoints = []
    bit = 1
    extra = []
    for step in range(STEPS - 1, 0, -1):
        field = fields[step]
        if step < STEPS - 1:
            core_adj = adjoint(2, step, (), 0, cur, old, courant, field[2], (), listing, traces)
        after = extra + [core_adj]
        edges, coming = [], []
        for side in (0, 1):
            edge = adjoint(
                side, step, halos[side : side + 1], halo_at, cur, old, courant, field[side], after,
                listing, traces,
            )
            edges.append(edge)
            coming.append(exchange(edge, side))
            after = [edge]
        adjoints.insert(0, (edges[0], edges[1], core_adj))
        old, cur = cur, adjoints[0]
        halos, halo_at = coming, 0
        if step == STEPS - 1:
            keep, send, tile = curvature(laps, edges[1])
        else:
            tile = tile + tiles
        if step == STEPS - 2:
            curv = sum(total_parts(keep, send, edges[1]))
        tiles = swap(tile, "depth", bit)
        bit *= 2
        extra = [tiles]
    while bit < lax.axis_size("depth"):
        tile = tile + tiles
        tiles = swap(tile, "depth", bit)
        bit *= 2
    found = []
    for side, both, other in ((2, [], 0), (0, [], 0), (1, [tile, tiles], 1)):
        found.append(
            adjoint_last(
                side, halos[side : side + 1], cur, old, courant, fields[0][side],
                [lap[side] for lap in laps], [a[side] for a in adjoints], both,
                found[1] if other else [], [curv] if side == 2 else found[0][:1], listing, traces,
            )
        )
    inner_parts = total_parts(*found[0])
    outer_parts = total_parts(*found[2])
    own = refresh(courant, inner_parts, outer_parts, curv, damping_table, plan_step)
    return assemble(own, swap(own, "shot", 1), slab)


def solution(mesh):
    in_specs = (
        P("shot", "depth", None, None),
        P("shot", "depth", None, None),
        P("shot", "depth", None, None),
        P("shot", "depth", None, None),
        P("depth", None, None),
        P("shot", None),
        P("shot"),
        P("shot", None),
        P("shot", None, None),
        P(),
        P(),
    )
    out_specs = P("depth", None, None)
    return jax.shard_map(
        on_device, mesh=mesh, in_specs=in_specs, out_specs=out_specs, check_vma=False
    )
```

```python
import jax
import jax.numpy as jnp
from jax import lax
from jax.experimental import pallas as pl
from jax.experimental.pallas import tpu as pltpu
from jax.sharding import PartitionSpec as P

STEPS = 4
HALO = 4
ROWS = 8
PAD = HALO * ROWS

coeffs = (-205.0 / 72.0, 8.0 / 5.0, -1.0 / 5.0, 8.0 / 315.0, -1.0 / 560.0)

VMEM = pl.BlockSpec(memory_space=pltpu.VMEM)
SMEM = pl.BlockSpec(memory_space=pltpu.SMEM)
HBM = pl.BlockSpec(memory_space=pltpu.HBM)


def f32(*shape):
    return jax.ShapeDtypeStruct(shape, jnp.float32)


def params():
    return pltpu.CompilerParams(vmem_limit_bytes=6 * 2**20)


def cost(planes):
    return pl.CostEstimate(
        flops=planes * 10**4, bytes_accessed=planes * 2**10, transcendentals=0
    )


def split(value, size):
    if size & (size - 1) == 0:
        return value >> (size.bit_length() - 1), value & (size - 1)
    return value // size, value % size


def spread(x, width):
    s, g = split(x, width // ROWS)
    return g * ROWS + s


def interleave(put, get, width):
    for g in range(width // ROWS):
        put(g * ROWS, get(pl.ds(g, ROWS, stride=width // ROWS)))


def margins(pad, first, count, width):
    length = pad.shape[2]
    place = lax.broadcasted_iota(jnp.int32, (ROWS, length), 0)

    def body(i, _):
        p = first + i
        for j in range(HALO):
            at = j * ROWS
            low = pltpu.roll(pad[p, width + at : width + at + ROWS, :], 1, 0)
            pad[p, at : at + ROWS, :] = jnp.where(place == 0, 0.0, low)
            top = pltpu.roll(pad[p, PAD + at : PAD + at + ROWS, :], ROWS - 1, 0)
            beyond = PAD + width + at
            pad[p, beyond : beyond + ROWS, :] = jnp.where(place == ROWS - 1, 0.0, top)

    march(count, body)


def high(side):
    odd = lax.axis_index("depth") % 2
    return odd if side else 1 - odd


def fill_edge(pad, side, halo, halo_at, field, slab, width):
    up = high(side)
    rows = slice(PAD, PAD + width)
    if len(field) == 1:
        for i in range(HALO):

            def put(at, value, i=i):
                pad[up * (2 * HALO) + i, PAD + at : PAD + at + ROWS, :] = value

            interleave(put, lambda spot, i=i: halo[halo_at + i, spot, :], width)
    else:
        pad[pl.ds(up * (2 * HALO), HALO), rows, :] = halo[halo_at : halo_at + HALO]
    inner = pl.ds((1 - up) * (2 * HALO), HALO)
    own = slice(HALO, 2 * HALO)
    if len(field) == 1:
        (ref,) = field
        slab = ref.shape[0]
        pad[own, rows, :] = ref[pl.ds(up * (slab - HALO), HALO)]
        pad[inner, rows, :] = ref[pl.ds(HALO + up * (slab - 3 * HALO), HALO)]
    else:
        core = field[2]
        pad[own, rows, :] = field[side][...]
        pad[inner, rows, :] = core[pl.ds(up * (core.shape[0] - HALO), HALO)]
    margins(pad, HALO, HALO, width)


def fill_core(pad, field, width):
    slab = pad.shape[0]
    rows = slice(PAD, PAD + width)
    if len(field) == 1:
        pad[:, rows, :] = field[0][...]
    else:
        for side in (0, 1):
            pad[pl.ds(high(side) * (slab - HALO), HALO), rows, :] = field[side][...]
        pad[HALO : slab - HALO, rows, :] = field[2][...]
    margins(pad, HALO, slab - 2 * HALO, width)


def place_of(side, field, slab):
    if len(field) == 1:
        return field[0], HALO if side == 2 else high(side) * (slab - HALO)
    return field[side], 0


def columns(pad, along_ref, width):
    planes, _, length = along_ref.shape
    apart = lax.broadcasted_iota(jnp.int32, (length, length), 0)
    apart = jnp.abs(apart - lax.broadcasted_iota(jnp.int32, (length, length), 1))
    band = jnp.where(apart == 0, 3.0 * coeffs[0], 0.0)
    for k in range(1, 5):
        band = jnp.where(apart == k, coeffs[k], band)
    size = HALO if planes % (2 * HALO) else 2 * HALO
    for begin in range(0, planes, size):
        block = pad[HALO + begin : HALO + begin + size, PAD : PAD + width, :]
        product = jnp.dot(
            block.reshape(size * width, length),
            band,
            precision=lax.Precision.HIGHEST,
            preferred_element_type=jnp.float32,
        )
        along_ref[begin : begin + size] = product.reshape(size, width, length)


def stencil(pad, p, width, result):
    rows = slice(PAD, PAD + width)
    plane = pad[p]
    for k in range(1, 5):
        along = pad[p + k, rows, :] + pad[p - k, rows, :]
        along = along + plane[PAD + k * ROWS : PAD + k * ROWS + width]
        along = along + plane[PAD - k * ROWS : PAD - k * ROWS + width]
        result = result + coeffs[k] * along
    return plane[rows], result


def fold(values):
    width, length = values.shape
    return jnp.sum(values.reshape(width // 8, 8, length), axis=0)


def march(count, body, carry=None):
    return lax.fori_loop(0, count, body, carry, unroll=4 if count % 4 == 0 else 2)


def kernel_call(kernel, small, arrays, outs, scratch, planes):
    return pl.pallas_call(
        kernel,
        out_shape=tuple(outs),
        in_specs=[SMEM] * len(small) + [VMEM] * len(arrays),
        out_specs=tuple([VMEM] * len(outs)),
        scratch_shapes=scratch,
        compiler_params=params(),
        cost_estimate=cost(planes),
    )(*small, *arrays)


def grouped(refs, sizes):
    found = []
    for size in sizes:
        found.append(refs[:size])
        refs = refs[size:]
    return found, list(refs)


def sizes_of(side, slab, width, length):
    planes = slab - 2 * HALO if side == 2 else HALO
    depth = slab if side == 2 else 3 * HALO
    return planes, [
        pltpu.VMEM((planes, width, length), jnp.float32),
        pltpu.VMEM((depth, width + 2 * PAD, length), jnp.float32),
    ]


def step_planes(side, along_ref, pad, halo, halo_at, cur, old, c_ref, next_ref, lap_ref):
    slab, width, length = c_ref.shape
    if side == 2:
        fill_core(pad, cur, width)
        plane = HALO
    else:
        fill_edge(pad, side, halo[0], halo_at, cur, slab, width)
        plane = high(side) * (slab - HALO)
    columns(pad, along_ref, width)
    old_ref, old_at = place_of(side, old, slab)

    def body(i, _):
        center, lap = stencil(pad, HALO + i, width, along_ref[i])
        if lap_ref is not None:
            lap_ref[i] = lap
        next_ref[i] = 2.0 * center - old_ref[old_at + i] + c_ref[plane + i] * lap

    march(next_ref.shape[0], body)


def forward(side, step, halo, cur, old, courant, after, wavelet, source):
    slab, width, length = courant.shape
    planes, pad_scratch = sizes_of(side, slab, width, length)
    groups = [list(halo), list(cur), list(old), [courant], list(after)]
    sizes = [len(g) for g in groups]

    def kernel(wave_ref, source_ref, *refs):
        (halo_refs, cur_refs, old_refs, (c_ref,), _), refs = grouped(refs, sizes)
        next_ref, lap_ref, along, pad = refs
        step_planes(side, along, pad, halo_refs, 0, cur_refs, old_refs, c_ref, next_ref, lap_ref)
        plane = HALO if side == 2 else high(side) * (slab - HALO)
        base = (lax.axis_index("depth") * slab + plane) * (width * length)
        local = source_ref[0] - base

        @pl.when((local >= 0) & (local < planes * width * length))
        def _():
            row, y = split(local, length)
            at, x = split(row, width)
            x = spread(x, width)
            spot = lax.broadcasted_iota(jnp.int32, (1, length), 1) == y
            add = jnp.where(spot, wave_ref[0, step], 0.0)
            next_ref[at, pl.ds(x, 1), :] = next_ref[at, pl.ds(x, 1), :] + add

    outs = [f32(planes, width, length)] * 2
    arrays = sum(groups, [])
    return kernel_call(kernel, [wavelet, source], arrays, outs, pad_scratch, planes)


def adjoint_step(
    side, step, along, pad, halo, halo_at, cur, old, c_ref, field_ref, list_ref, obs_ref, next_ref
):
    slab, width, length = c_ref.shape
    step_planes(side, along, pad, halo, halo_at, cur, old, c_ref, next_ref, None)
    column = lax.broadcasted_iota(jnp.int32, (1, length), 1)

    def inject(k, _):
        row, y = split(list_ref[2 * side, k], length)
        at, x = split(row, width)
        x = spread(x, width)
        pred = field_ref[at, pl.ds(x, 1), :]
        res = jnp.where(column == y, pred - obs_ref[step, list_ref[2 * side + 1, k]], 0.0)
        next_ref[at, pl.ds(x, 1), :] = next_ref[at, pl.ds(x, 1), :] + res

    lax.fori_loop(0, list_ref[6, side], inject, None)


def adjoint(side, step, halo, halo_at, cur, old, courant, field, after, listing, observed):
    slab, width, length = courant.shape
    planes, pad_scratch = sizes_of(side, slab, width, length)
    groups = [list(halo), list(cur), list(old), [courant, field], list(after)]
    sizes = [len(g) for g in groups]

    def kernel(list_ref, obs_ref, *refs):
        (halo_refs, cur_refs, old_refs, (c_ref, field_ref), _), refs = grouped(refs, sizes)
        next_ref, along, pad = refs
        adjoint_step(
            side, step, along, pad, halo_refs, halo_at, cur_refs, old_refs, c_ref, field_ref,
            list_ref, obs_ref, next_ref,
        )

    outs = [f32(planes, width, length)]
    arrays = sum(groups, [])
    return kernel_call(kernel, [listing, observed], arrays, outs, pad_scratch, planes)[0]


def adjoint_last(
    side, halo, cur, old, courant, field, laps, adjoints, tile, other, after, listing, observed
):
    slab, width, length = courant.shape
    planes, pad_scratch = sizes_of(side, slab, width, length)
    groups = [list(halo), list(cur), list(old), [courant, field], list(laps)]
    groups += [list(adjoints), list(tile) + list(other), list(after)]
    sizes = [len(g) for g in groups]

    def kernel(list_ref, obs_ref, *refs):
        found, refs = grouped(refs, sizes)
        halo_refs, cur_refs, old_refs, (c_ref, field_ref), lap_refs, adj_refs, more, _ = found
        next_ref, along, pad = refs[-3:]
        adjoint_step(
            side, 0, along, pad, halo_refs, 0, cur_refs, old_refs, c_ref, field_ref,
            list_ref, obs_ref, next_ref,
        )
        core = lax.axis_index("shot") % 2

        def product(i):
            value = next_ref[i] * lap_refs[0][i]
            for lap_ref, adj_ref in zip(lap_refs[1:], adj_refs):
                value = value + adj_ref[i] * lap_ref[i]
            return value

        if side == 2:
            keep_ref, send_ref = refs[:2]
            half = planes // 2

            def body(i, _):
                keep_ref[i] = product(core * half + i)
                send_ref[i] = product((1 - core) * half + i)

            march(half, body)
        elif side == 0:
            for i in range(HALO):
                refs[0][i] = product(i)
        else:
            tile_ref, tiles_ref, other_ref = more

            def write(own_ref, far_ref):
                for i in range(HALO):
                    rows = slice(i * width, (i + 1) * width)
                    own_ref[rows, :] = other_ref[i]
                    far_ref[rows, :] = product(i)

            @pl.when(core == 0)
            def _():
                write(refs[0], refs[1])

            @pl.when(core == 1)
            def _():
                write(refs[1], refs[0])

            for ref in refs[:2]:
                ref[HALO * width : HALO * width + 8, :] = tile_ref[...] + tiles_ref[...]

    if side == 2:
        outs = [f32(planes // 2, width, length)] * 2
    elif side == 0:
        outs = [f32(planes, width, length)]
    else:
        outs = [f32(HALO * width + 8, length)] * 2
    arrays = sum(groups, [])
    scratch = [pltpu.VMEM((planes, width, length), jnp.float32)] + pad_scratch
    return kernel_call(kernel, [listing, observed], arrays, outs, scratch, planes)


def curvature(laps, after):
    number = len(laps)
    inner, width, length = laps[0][2].shape
    half = inner // 2
    size = half + HALO

    def kernel(*refs):
        sides = [refs[n * number : (n + 1) * number] for n in range(3)]
        keep_ref, send_ref, tile_ref = refs[3 * number + 1 :]
        core = lax.axis_index("shot") % 2

        def squares(lap_refs, at):
            value = lap_refs[0][at] * lap_refs[0][at]
            for ref in lap_refs[1:]:
                value = value + ref[at] * ref[at]
            return value

        def body(i, total):
            for ref, start in ((keep_ref, core * half), (send_ref, (1 - core) * half)):
                value = squares(sides[2], start + i)
                ref[i] = value
                total = total + fold(value)
            return total

        tile_ref[...] = march(half, body, jnp.zeros((8, length), jnp.float32))

        def outer(first_ref, second_ref):
            total = jnp.zeros((8, length), jnp.float32)
            for i in range(HALO):
                for ref, lap_refs in ((first_ref, sides[0]), (second_ref, sides[1])):
                    value = squares(lap_refs, i)
                    ref[half + i] = value
                    total = total + fold(value)
            tile_ref[...] = tile_ref[...] + total

        @pl.when(core == 0)
        def _():
            outer(keep_ref, send_ref)

        @pl.when(core == 1)
        def _():
            outer(send_ref, keep_ref)

    outs = [f32(size, width, length)] * 2 + [f32(8, length)]
    arrays = [lap[n] for n in range(3) for lap in laps] + [after]
    return kernel_call(kernel, [], arrays, outs, [], 8)


def list_receivers(cells, slab, width, length):
    count = cells.shape[0]
    area = width * length

    def kernel(cell_ref, out_ref):
        offset = lax.axis_index("depth") * (slab * area)
        starts = [high(0) * ((slab - HALO) * area), high(1) * ((slab - HALO) * area), HALO * area]
        lengths = [HALO * area, HALO * area, (slab - 2 * HALO) * area]

        def body(r, counts):
            cell = cell_ref[r] - offset
            found = []
            for n in range(3):
                local = cell - starts[n]
                inside = (local >= 0) & (local < lengths[n])
                out_ref[2 * n, counts[n]] = local
                out_ref[2 * n + 1, counts[n]] = r
                found.append(counts[n] + inside.astype(jnp.int32))
            return tuple(found)

        counts = lax.fori_loop(0, count, body, (jnp.int32(0),) * 3, unroll=8)
        for n in range(3):
            out_ref[6, n] = counts[n]

    return pl.pallas_call(
        kernel,
        out_shape=jax.ShapeDtypeStruct((7, 2 * count), jnp.int32),
        in_specs=[SMEM],
        out_specs=SMEM,
        compiler_params=params(),
        cost_estimate=cost(8),
    )(cells)


def interleaved(*arrays):
    number = len(arrays)
    slab, width, length = arrays[0].shape

    def kernel(*refs):
        def body(i, _):
            for ref, out_ref in zip(refs[:number], refs[number:]):

                def put(at, value, out_ref=out_ref):
                    out_ref[i, at : at + ROWS, :] = value

                interleave(put, lambda spot, ref=ref: ref[i, spot, :], width)

        march(slab, body)

    outs = [f32(slab, width, length)] * number
    return kernel_call(kernel, [], list(arrays), outs, [], 8)


def pack(field, adjoint_field):
    odd = lax.axis_index("depth") % 2
    far = field.shape[0] - HALO
    found = []
    for start in ((1 - odd) * far, odd * far):
        planes = [lax.dynamic_slice_in_dim(v, start, HALO, 0) for v in (field, adjoint_field)]
        found.append(jnp.concatenate(planes, axis=0))
    return found


def refresh(courant, inner_parts, outer_parts, curv, table, plan):
    slab, width, length = courant.shape
    half = inner_parts[0].shape[0]
    number = len(inner_parts)
    cells = slab * width * length * lax.axis_size("depth")

    def kernel(table_ref, plan_ref, c_ref, curv_ref, *rest):
        inner_refs = rest[:number]
        outer_refs = rest[number : 2 * number]
        out_ref = rest[2 * number]
        tail = slice(HALO * width, HALO * width + 8)
        tile = outer_refs[0][tail, :]
        for ref in outer_refs[1:]:
            tile = tile + ref[tail, :]
        level = jnp.sum(tile) / cells + 1e-06
        extra = table_ref[plan_ref[0]] * level
        core = lax.axis_index("shot") % 2
        start = HALO + core * half

        def store(i, value):
            for g in range(width // ROWS):
                spot = pl.ds(g, ROWS, stride=width // ROWS)
                out_ref[i, spot, :] = value[g * ROWS : (g + 1) * ROWS]

        def body(i, _):
            grad = inner_refs[0][i]
            for ref in inner_refs[1:]:
                grad = grad + ref[i]
            store(i, c_ref[start + i] - grad / (curv_ref[i] + extra))

        march(half, body)
        odd = lax.axis_index("depth") % 2
        up = core + odd == 0
        up = (up | (core + odd == 2)).astype(jnp.int32)
        for i in range(HALO):
            rows = slice(i * width, (i + 1) * width)
            grad = outer_refs[0][rows, :]
            for ref in outer_refs[1:]:
                grad = grad + ref[rows, :]
            model = c_ref[up * (slab - HALO) + i]
            store(half + i, model - grad / (curv_ref[half + i] + extra))

    arrays = [courant, curv, *inner_parts, *outer_parts]
    outs = [f32(half + HALO, width, length)]
    return kernel_call(kernel, [table, plan], arrays, outs, [], half)[0]


def assemble(own, other, slab):
    size, width, length = own.shape
    inner = size - HALO

    def kernel(own_ref, other_ref, out_ref, sems):
        core = lax.axis_index("shot") % 2
        up = (lax.axis_index("depth") + core + 1) % 2
        copies = []
        for n, (ref, c, u) in enumerate([(own_ref, core, up), (other_ref, 1 - core, 1 - up)]):
            for m, (first, count, start) in enumerate(
                [(0, inner, HALO + c * inner), (inner, HALO, u * (slab - HALO))]
            ):
                copies.append(
                    pltpu.make_async_copy(
                        ref.at[pl.ds(first, count)],
                        out_ref.at[pl.ds(start, count)],
                        sems.at[2 * n + m],
                    )
                )
        for copy in copies:
            copy.start()
        for copy in copies:
            copy.wait()

    return pl.pallas_call(
        kernel,
        out_shape=f32(slab, width, length),
        in_specs=[VMEM] * 2,
        out_specs=HBM,
        scratch_shapes=[pltpu.SemaphoreType.DMA((4,))],
        compiler_params=params(),
        cost_estimate=cost(8),
    )(own, other)


def exchange(values, side):
    links = []
    for i in range(side, lax.axis_size("depth") - 1, 2):
        links += [(i, i + 1), (i + 1, i)]
    return lax.ppermute(values, "depth", links)


def swap(values, axis, bit):
    count = lax.axis_size(axis)
    return lax.ppermute(values, axis, [(i, i ^ bit) for i in range(count)])


def sum_of(values, other, after):
    def kernel(values_ref, other_ref, _, out_ref):
        def body(i, _):
            out_ref[i] = values_ref[i] + other_ref[i]

        march(values.shape[0], body)

    return kernel_call(kernel, [], [values, other, after], [f32(*values.shape)], [], 8)[0]


def total_parts(keep, send, after=None):
    parts = [keep, swap(send, "shot", 1)]
    bit = 2
    while bit < lax.axis_size("shot"):
        if after is not None and bit == 2:
            here = sum_of(*parts, after)
        else:
            here = parts[0] + parts[1]
        parts = [here, swap(here, "shot", bit)]
        bit *= 2
    return parts


def on_device(
    field_prev,
    field_now,
    adjoint_next,
    adjoint_after,
    courant,
    wavelet,
    source_cell,
    receiver_cell,
    observed,
    damping_table,
    plan_step,
):
    slab, width, length = courant.shape
    halos = [exchange(v, side) for side, v in enumerate(pack(field_now[0], adjoint_next[0]))]
    first_halos = halos
    start, before, courant = interleaved(field_now[0], field_prev[0], courant)
    first, second = interleaved(adjoint_next[0], adjoint_after[0])
    listing = list_receivers(receiver_cell[0], slab, width, length)
    traces = observed[0]
    old, cur = (before,), (start,)
    laps, fields = [], []
    after = [listing]
    for step in range(STEPS):
        core = forward(2, step, (), cur, old, courant, (), wavelet, source_cell)
        after = after + [core[0]]
        if step == STEPS - 1:
            core_adj = adjoint(
                2, step, (), 0, (first,), (second,), courant, core[0], (), listing, traces
            )
            after = after + [core_adj]
        parts, coming = [], []
        for side in (0, 1):
            edge = forward(
                side, step, halos[side : side + 1], cur, old, courant, after, wavelet, source_cell
            )
            parts.append(edge)
            if step < STEPS - 1:
                coming.append(exchange(edge[0], side))
                after = [edge[0]]
        laps.append((parts[0][1], parts[1][1], core[1]))
        fields.append((parts[0][0], parts[1][0], core[0]))
        old, cur = cur, fields[-1]
        halos, after = coming, []
    old, cur = (second,), (first,)
    halos, halo_at = first_halos, HALO
    adjoints = []
    bit = 1
    extra = []
    for step in range(STEPS - 1, 0, -1):
        field = fields[step]
        if step < STEPS - 1:
            core_adj = adjoint(2, step, (), 0, cur, old, courant, field[2], (), listing, traces)
        after = extra + [core_adj]
        edges, coming = [], []
        for side in (0, 1):
            edge = adjoint(
                side, step, halos[side : side + 1], halo_at, cur, old, courant, field[side], after,
                listing, traces,
            )
            edges.append(edge)
            coming.append(exchange(edge, side))
            after = [edge]
        adjoints.insert(0, (edges[0], edges[1], core_adj))
        old, cur = cur, adjoints[0]
        halos, halo_at = coming, 0
        if step == STEPS - 1:
            keep, send, tile = curvature(laps, edges[1])
        else:
            tile = tile + tiles
        if step == STEPS - 2:
            curv = sum(total_parts(keep, send, edges[1]))
        tiles = swap(tile, "depth", bit)
        bit *= 2
        extra = [tiles]
    while bit < lax.axis_size("depth"):
        tile = tile + tiles
        tiles = swap(tile, "depth", bit)
        bit *= 2
    found = []
    for side, both, other in ((2, [], 0), (0, [], 0), (1, [tile, tiles], 1)):
        found.append(
            adjoint_last(
                side, halos[side : side + 1], cur, old, courant, fields[0][side],
                [lap[side] for lap in laps], [a[side] for a in adjoints], both,
                found[1] if other else [], [curv] if side == 2 else found[0][:1], listing, traces,
            )
        )
    inner_parts = total_parts(*found[0])
    outer_parts = total_parts(*found[2])
    own = refresh(courant, inner_parts, outer_parts, curv, damping_table, plan_step)
    return assemble(own, swap(own, "shot", 1), slab)


def solution(mesh):
    in_specs = (
        P("shot", "depth", None, None),
        P("shot", "depth", None, None),
        P("shot", "depth", None, None),
        P("shot", "depth", None, None),
        P("depth", None, None),
        P("shot", None),
        P("shot"),
        P("shot", None),
        P("shot", None, None),
        P(),
        P(),
    )
    out_specs = P("depth", None, None)
    return jax.shard_map(
        on_device, mesh=mesh, in_specs=in_specs, out_specs=out_specs, check_vma=False
    )
```

```python
import jax
import jax.numpy as jnp
from jax import lax
from jax.experimental import pallas as pl
from jax.experimental.pallas import tpu as pltpu
from jax.sharding import PartitionSpec as P

STEPS = 4
HALO = 4
ROWS = 8
PAD = HALO * ROWS

coeffs = (-205.0 / 72.0, 8.0 / 5.0, -1.0 / 5.0, 8.0 / 315.0, -1.0 / 560.0)

VMEM = pl.BlockSpec(memory_space=pltpu.VMEM)
SMEM = pl.BlockSpec(memory_space=pltpu.SMEM)
HBM = pl.BlockSpec(memory_space=pltpu.HBM)


def f32(*shape):
    return jax.ShapeDtypeStruct(shape, jnp.float32)


def params():
    return pltpu.CompilerParams(vmem_limit_bytes=6 * 2**20)


def cost(planes):
    return pl.CostEstimate(
        flops=planes * 10**4, bytes_accessed=planes * 2**10, transcendentals=0
    )


def split(value, size):
    if size & (size - 1) == 0:
        return value >> (size.bit_length() - 1), value & (size - 1)
    return value // size, value % size


def spread(x, width):
    s, g = split(x, width // ROWS)
    return g * ROWS + s


def interleave(put, get, width):
    for g in range(width // ROWS):
        put(g * ROWS, get(pl.ds(g, ROWS, stride=width // ROWS)))


def margins(pad, first, count, width):
    length = pad.shape[2]
    place = lax.broadcasted_iota(jnp.int32, (ROWS, length), 0)

    def body(i, _):
        p = first + i
        for j in range(HALO):
            at = j * ROWS
            low = pltpu.roll(pad[p, width + at : width + at + ROWS, :], 1, 0)
            pad[p, at : at + ROWS, :] = jnp.where(place == 0, 0.0, low)
            top = pltpu.roll(pad[p, PAD + at : PAD + at + ROWS, :], ROWS - 1, 0)
            beyond = PAD + width + at
            pad[p, beyond : beyond + ROWS, :] = jnp.where(place == ROWS - 1, 0.0, top)

    march(count, body)


def fill(pad, base, pieces, width):
    top = base + pad.shape[0]
    for ref, origin in pieces:
        begin = max(base, origin)
        end = min(top, origin + ref.shape[0])
        if end > begin:
            pad[begin - base : end - base, PAD : PAD + width, :] = ref[begin - origin : end - origin]


def fill_halo(pad, at, ref, ref_at, natural, width):
    odd = lax.axis_index("depth") % 2
    for i in range(HALO):
        if natural:

            def put(row, value, i=i):
                pad[at + i, PAD + row : PAD + row + ROWS, :] = value

            source = ref_at + jnp.where(odd == 1, i, HALO - 1 - i)
            interleave(put, lambda spot, source=source: ref[source, spot, :], width)
        else:
            pad[at + i, PAD : PAD + width, :] = ref[HALO - 1 - i]


def find(pieces, plane):
    for ref, origin in pieces:
        if origin <= plane < origin + ref.shape[0]:
            return ref, plane - origin


def columns(pad, along_ref, width):
    planes, _, length = along_ref.shape
    apart = lax.broadcasted_iota(jnp.int32, (length, length), 0)
    apart = jnp.abs(apart - lax.broadcasted_iota(jnp.int32, (length, length), 1))
    band = jnp.where(apart == 0, 3.0 * coeffs[0], 0.0)
    for k in range(1, 5):
        band = jnp.where(apart == k, coeffs[k], band)
    size = HALO if planes % (2 * HALO) else 2 * HALO
    for begin in range(0, planes, size):
        block = pad[HALO + begin : HALO + begin + size, PAD : PAD + width, :]
        product = jnp.dot(
            block.reshape(size * width, length),
            band,
            precision=lax.Precision.HIGHEST,
            preferred_element_type=jnp.float32,
        )
        along_ref[begin : begin + size] = product.reshape(size, width, length)


def stencil(pad, p, width, result):
    rows = slice(PAD, PAD + width)
    plane = pad[p]
    for k in range(1, 5):
        along = pad[p + k, rows, :] + pad[p - k, rows, :]
        along = along + plane[PAD + k * ROWS : PAD + k * ROWS + width]
        along = along + plane[PAD - k * ROWS : PAD - k * ROWS + width]
        result = result + coeffs[k] * along
    return plane[rows], result


def fold(values):
    width, length = values.shape
    return jnp.sum(values.reshape(width // 8, 8, length), axis=0)


def march(count, body, carry=None):
    return lax.fori_loop(0, count, body, carry, unroll=4 if count % 4 == 0 else 2)


def kernel_call(kernel, small, arrays, outs, scratch, planes):
    return pl.pallas_call(
        kernel,
        out_shape=tuple(outs),
        in_specs=[SMEM] * len(small) + [VMEM] * len(arrays),
        out_specs=tuple([VMEM] * len(outs)),
        scratch_shapes=scratch,
        compiler_params=params(),
        cost_estimate=cost(planes),
    )(*small, *arrays)


def grouped(refs, sizes):
    found = []
    for size in sizes:
        found.append(refs[:size])
        refs = refs[size:]
    return found, list(refs)


def ranges(slab):
    half = slab // 2 - HALO
    return [(0, HALO), (HALO, half), (HALO + half, half), (slab - HALO, HALO)]


def scratch_of(count, width, length):
    return [
        pltpu.VMEM((count, width, length), jnp.float32),
        pltpu.VMEM((count + 2 * HALO, width + 2 * PAD, length), jnp.float32),
    ]


def origins(field):
    return [at for _, at in field]


def arrays_of(field):
    return [values for values, _ in field]


def prepare(first, pad, along_ref, halo, cur, slab, width):
    count = along_ref.shape[0]
    fill(pad, first - HALO, cur, width)
    if halo is not None:
        fill_halo(pad, 0 if first == 0 else HALO + count, *halo, width)
    margins(pad, HALO, count, width)
    columns(pad, along_ref, width)


def forward(place, halo, cur, old, courant, source, wave, after):
    slab, width, length = courant.shape
    first, count = place
    groups = [[halo[0]] if halo else [], arrays_of(cur), arrays_of(old)]
    groups += [[courant, source, wave], list(after)]
    sizes = [len(g) for g in groups]

    def kernel(*refs):
        (halo_ref, cur_refs, old_refs, (c_ref, source_ref, wave_ref), _), refs = grouped(refs, sizes)
        next_ref, lap_ref, along_ref, pad = refs
        coming = (halo_ref[0], *halo[1:]) if halo else None
        prepare(first, pad, along_ref, coming, list(zip(cur_refs, origins(cur))), slab, width)
        old_ref, old_at = find(list(zip(old_refs, origins(old))), first)
        amplitude = wave_ref[0:1, :]

        def body(i, _):
            center, lap = stencil(pad, HALO + i, width, along_ref[i])
            lap_ref[i] = lap
            value = 2.0 * center - old_ref[old_at + i] + c_ref[first + i] * lap
            next_ref[i] = value + source_ref[first + i] * amplitude

        march(count, body)

    outs = [f32(count, width, length)] * 2
    return kernel_call(kernel, [], sum(groups, []), outs, scratch_of(count, width, length), count)


def adjoint(place, halo, cur, old, courant, field, number, observed, after):
    slab, width, length = courant.shape
    first, count = place
    groups = [[halo[0]] if halo else [], arrays_of(cur), arrays_of(old), arrays_of(field)]
    groups += [[courant, number, observed], list(after)]
    sizes = [len(g) for g in groups]

    def kernel(*refs):
        found, refs = grouped(refs, sizes)
        next_ref, along_ref, pad = refs
        adjoint_step(place, halo, cur, old, field, found, next_ref, along_ref, pad)

    outs = [f32(count, width, length)]
    scratch = scratch_of(count, width, length)
    return kernel_call(kernel, [], sum(groups, []), outs, scratch, count)[0]


def adjoint_step(place, halo, cur, old, field, found, next_ref, along_ref, pad):
    halo_ref, cur_refs, old_refs, field_refs, (c_ref, number_ref, observed_ref) = found[:5]
    slab, width, length = c_ref.shape
    first, count = place
    coming = (halo_ref[0], *halo[1:]) if halo else None
    prepare(first, pad, along_ref, coming, list(zip(cur_refs, origins(cur))), slab, width)
    for field_ref, field_at in zip(field_refs, origins(field)):
        begin, end = max(first, field_at), min(first + count, field_at + field_ref.shape[0])
        if end <= begin:
            continue
        old_ref, old_at = find(list(zip(old_refs, origins(old))), begin)

        def body(i, _, field_ref=field_ref, field_at=field_at, begin=begin, old_ref=old_ref, old_at=old_at):
            q = begin + i
            center, lap = stencil(pad, begin - first + HALO + i, width, along_ref[begin - first + i])
            value = 2.0 * center - old_ref[old_at + i] + c_ref[q] * lap
            miss = number_ref[q] * field_ref[begin - field_at + i] - observed_ref[q]
            next_ref[begin - first + i] = value + miss

        march(end - begin, body)


def adjoint_last(
    place, halo, cur, old, courant, field, number, observed, laps, adjoints, tile, other, after
):
    slab, width, length = courant.shape
    first, count = place
    inner = count > HALO
    groups = [[halo[0]] if halo else [], arrays_of(cur), arrays_of(old), arrays_of(field)]
    groups += [[courant, number, observed], sum(laps, []), sum(adjoints, [])]
    groups += [list(tile) + list(other), list(after)]
    sizes = [len(g) for g in groups]
    steps, parts = len(laps), len(laps[0])

    def kernel(*refs):
        found, refs = grouped(refs, sizes)
        next_ref, along_ref, pad = refs[-3:]
        adjoint_step(place, halo, cur, old, field, found, next_ref, along_ref, pad)
        lap_refs, adj_refs, more = found[5:8]
        core = lax.axis_index("shot") % 2

        def product(part, i):
            value = next_ref[part * (count // parts) + i] * lap_refs[part][i]
            for n in range(1, steps):
                value = value + adj_refs[(n - 1) * parts + part][i] * lap_refs[n * parts + part][i]
            return value

        def either(write):
            @pl.when(core == 0)
            def _():
                write(refs[0], refs[1])

            @pl.when(core == 1)
            def _():
                write(refs[1], refs[0])

        if inner:

            def write(first_ref, second_ref):
                def body(i, _):
                    first_ref[i] = product(0, i)
                    second_ref[i] = product(1, i)

                march(count // 2, body)

            either(write)
        elif not other:
            for i in range(HALO):
                refs[0][i] = product(0, i)
        else:
            tile_ref, tiles_ref, other_ref = more

            def write(first_ref, second_ref):
                for i in range(HALO):
                    rows = slice(i * width, (i + 1) * width)
                    first_ref[rows, :] = other_ref[i]
                    second_ref[rows, :] = product(0, i)

            either(write)
            for ref in refs[:2]:
                ref[HALO * width : HALO * width + 8, :] = tile_ref[...] + tiles_ref[...]

    if inner:
        outs = [f32(count // 2, width, length)] * 2
    elif not other:
        outs = [f32(count, width, length)]
    else:
        outs = [f32(HALO * width + 8, length)] * 2
    scratch = [pltpu.VMEM((count, width, length), jnp.float32)] + scratch_of(count, width, length)
    return kernel_call(kernel, [], sum(groups, []), outs, scratch, count)


def curvature(laps, after):
    number = len(laps)
    half, width, length = laps[0][1].shape
    size = half + HALO

    def kernel(*refs):
        ranged = [refs[n * number : (n + 1) * number] for n in range(4)]
        keep_ref, send_ref, tile_ref = refs[4 * number + 1 :]
        core = lax.axis_index("shot") % 2

        def squares(lap_refs, at):
            value = lap_refs[0][at] * lap_refs[0][at]
            for ref in lap_refs[1:]:
                value = value + ref[at] * ref[at]
            return value

        def write(first_ref, second_ref):
            def body(i, total):
                for ref, lap_refs in ((first_ref, ranged[1]), (second_ref, ranged[2])):
                    value = squares(lap_refs, i)
                    ref[i] = value
                    total = total + fold(value)
                return total

            total = march(half, body, jnp.zeros((8, length), jnp.float32))
            for i in range(HALO):
                for ref, lap_refs in ((first_ref, ranged[0]), (second_ref, ranged[3])):
                    value = squares(lap_refs, i)
                    ref[half + i] = value
                    total = total + fold(value)
            tile_ref[...] = total

        @pl.when(core == 0)
        def _():
            write(keep_ref, send_ref)

        @pl.when(core == 1)
        def _():
            write(send_ref, keep_ref)

    outs = [f32(size, width, length)] * 2 + [f32(8, length)]
    arrays = [lap[n] for n in range(4) for lap in laps] + [after]
    return kernel_call(kernel, [], arrays, outs, [], 8)


def points(wavelet, source, cells, observed, slab, width, length):
    receivers = cells.shape[0]
    steps = observed.shape[0]
    area = width * length

    def kernel(wave_ref, source_ref, cell_ref, obs_ref, spot_ref, number_ref, *refs):
        row_refs, sum_refs = refs[:steps], refs[steps:]
        blank = jnp.zeros((width, length), jnp.float32)

        def clear(i, _):
            for ref in (spot_ref, number_ref) + sum_refs:
                ref[i] = blank

        march(slab, clear)
        depth = lax.axis_index("depth")
        offset = depth * (slab * area)
        odd = depth % 2
        column = lax.broadcasted_iota(jnp.int32, (1, length), 1)

        def add(local, terms):
            @pl.when((local >= 0) & (local < slab * area))
            def _():
                row, y = split(local, length)
                plane, x = split(row, width)
                q = jnp.where(odd == 1, plane, slab - 1 - plane)
                at = pl.ds(spread(x, width), 1)
                for ref, term in terms():
                    ref[q, at, :] = ref[q, at, :] + jnp.where(column == y, term, 0.0)

        add(source_ref[0] - offset, lambda: [(spot_ref, 1.0)])
        for n in range(steps):
            row_refs[n][...] = jnp.full((8, length), wave_ref[0, n], jnp.float32)

        def body(r, _):
            def terms():
                found = [(number_ref, 1.0)]
                for n in range(steps):
                    found.append((sum_refs[n], obs_ref[n, r]))
                return found

            add(cell_ref[r] - offset, terms)

        lax.fori_loop(0, receivers, body, None)

    volume = f32(slab, width, length)
    outs = [volume, volume] + [f32(8, length)] * steps + [volume] * steps
    small = [wavelet, source, cells, observed]
    found = kernel_call(kernel, small, [], outs, [], 8)
    return found[0], found[1], found[2 : 2 + steps], found[2 + steps :]


def interleaved(*arrays):
    number = len(arrays)
    slab, width, length = arrays[0].shape

    def kernel(*refs):
        odd = lax.axis_index("depth") % 2

        def body(i, _):
            plane = jnp.where(odd == 1, i, slab - 1 - i)
            for ref, out_ref in zip(refs[:number], refs[number:]):

                def put(at, value, out_ref=out_ref):
                    out_ref[i, at : at + ROWS, :] = value

                interleave(put, lambda spot, ref=ref: ref[plane, spot, :], width)

        march(slab, body)

    outs = [f32(slab, width, length)] * number
    return kernel_call(kernel, [], list(arrays), outs, [], 8)


def pack(field, adjoint_field):
    odd = lax.axis_index("depth") % 2
    far = field.shape[0] - HALO
    found = []
    for start in ((1 - odd) * far, odd * far):
        planes = [lax.dynamic_slice_in_dim(v, start, HALO, 0) for v in (field, adjoint_field)]
        found.append(jnp.concatenate(planes, axis=0))
    return found


def refresh(courant, inner_parts, outer_parts, curv, table, plan):
    slab, width, length = courant.shape
    half = inner_parts[0].shape[0]
    number = len(inner_parts)
    cells = slab * width * length * lax.axis_size("depth")

    def kernel(table_ref, plan_ref, c_ref, curv_ref, *rest):
        inner_refs = rest[:number]
        outer_refs = rest[number : 2 * number]
        out_ref = rest[2 * number]
        tail = slice(HALO * width, HALO * width + 8)
        tile = outer_refs[0][tail, :]
        for ref in outer_refs[1:]:
            tile = tile + ref[tail, :]
        level = jnp.sum(tile) / cells + 1e-06
        extra = table_ref[plan_ref[0]] * level
        core = lax.axis_index("shot") % 2
        odd = lax.axis_index("depth") % 2
        size = half + HALO

        def store(q, value):
            plane = jnp.where(odd == 1, q, size - 1 - q)
            for g in range(width // ROWS):
                spot = pl.ds(g, ROWS, stride=width // ROWS)
                out_ref[plane, spot, :] = value[g * ROWS : (g + 1) * ROWS]

        def body(i, _):
            grad = inner_refs[0][i]
            for ref in inner_refs[1:]:
                grad = grad + ref[i]
            model = c_ref[HALO + core * half + i]
            store((1 - core) * HALO + i, model - grad / (curv_ref[i] + extra))

        march(half, body)
        for i in range(HALO):
            rows = slice(i * width, (i + 1) * width)
            grad = outer_refs[0][rows, :]
            for ref in outer_refs[1:]:
                grad = grad + ref[rows, :]
            model = c_ref[core * (slab - HALO) + i]
            store(core * half + i, model - grad / (curv_ref[half + i] + extra))

    arrays = [courant, curv, *inner_parts, *outer_parts]
    outs = [f32(half + HALO, width, length)]
    return kernel_call(kernel, [table, plan], arrays, outs, [], half)[0]


def assemble(own, other):
    half, width, length = own.shape

    def kernel(own_ref, other_ref, out_ref, sems):
        core = lax.axis_index("shot") % 2
        upper = (lax.axis_index("depth") + core + 1) % 2
        copies = []
        for n, (ref, place) in enumerate([(own_ref, upper), (other_ref, 1 - upper)]):
            spot = out_ref.at[pl.ds(place * half, half)]
            copies.append(pltpu.make_async_copy(ref, spot, sems.at[n]))
        for copy in copies:
            copy.start()
        for copy in copies:
            copy.wait()

    return pl.pallas_call(
        kernel,
        out_shape=f32(2 * half, width, length),
        in_specs=[VMEM] * 2,
        out_specs=HBM,
        scratch_shapes=[pltpu.SemaphoreType.DMA((2,))],
        compiler_params=params(),
        cost_estimate=cost(8),
    )(own, other)


def exchange(values, side):
    links = []
    for i in range(side, lax.axis_size("depth") - 1, 2):
        links += [(i, i + 1), (i + 1, i)]
    return lax.ppermute(values, "depth", links)


def swap(values, axis, bit):
    count = lax.axis_size(axis)
    return lax.ppermute(values, axis, [(i, i ^ bit) for i in range(count)])


def sum_of(values, other, after):
    def kernel(values_ref, other_ref, _, out_ref):
        def body(i, _):
            out_ref[i] = values_ref[i] + other_ref[i]

        march(values.shape[0], body)

    return kernel_call(kernel, [], [values, other, after], [f32(*values.shape)], [], 8)[0]


def total_parts(keep, send, after=None):
    parts = [keep, swap(send, "shot", 1)]
    bit = 2
    while bit < lax.axis_size("shot"):
        if after is not None and bit == 2:
            here = sum_of(*parts, after)
        else:
            here = parts[0] + parts[1]
        parts = [here, swap(here, "shot", bit)]
        bit *= 2
    return parts


def on_device(
    field_prev,
    field_now,
    adjoint_next,
    adjoint_after,
    courant,
    wavelet,
    source_cell,
    receiver_cell,
    observed,
    damping_table,
    plan_step,
):
    slab, width, length = courant.shape
    halos = [exchange(v, side) for side, v in enumerate(pack(field_now[0], adjoint_next[0]))]
    places = ranges(slab)
    starts = [first for first, _ in places]
    spot, number, waves, sums = points(
        wavelet, source_cell, receiver_cell[0], observed[0], slab, width, length
    )
    start, before, courant = interleaved(field_now[0], field_prev[0], courant)
    first, second = interleaved(adjoint_next[0], adjoint_after[0])
    old, cur = [(before, 0)], [(start, 0)]
    coming = [(halos[0], 0, True), (halos[1], 0, True)]

    def ahead(step, side, halo, cur, old, after):
        return forward(
            places[side], halo, cur, old, courant, spot, waves[step], after
        )

    def back(step, side, halo, cur, old, field, after):
        return adjoint(
            places[side], halo, cur, old, courant, [field], number, sums[step], after
        )

    laps, fields = [], []
    near = ahead(0, 1, None, cur, old, ())
    far = ahead(0, 2, None, cur, old, ())
    for step in range(STEPS):
        last = step == STEPS - 1
        after = [near[0], far[0]]
        if last:
            rest, more = [(second, 0)], [(first, 0)]
            near_adj = back(step, 1, None, more, rest, (near[0], starts[1]), ())
            far_adj = back(step, 2, None, more, rest, (far[0], starts[2]), ())
            after += [near_adj, far_adj]
        one = ahead(step, 0, coming[0], cur, old, after)
        if last:
            edge = (halos[0], HALO, True)
            one_adj = back(step, 0, edge, more, rest, (one[0], starts[0]), after)
            message = exchange(one_adj, 0)
            newer = [(one_adj, starts[0]), (near_adj, starts[1]), (far_adj, starts[2])]
            near_next = back(step - 1, 1, None, newer, more, (fields[-1][1], starts[1]), ())
            two = ahead(step, 3, coming[1], cur, old, [near_next])
            edge = (halos[1], HALO, True)
            two_adj = back(step, 3, edge, more, rest, (two[0], starts[3]), [near_next])
            newer.append((two_adj, starts[3]))
        else:
            message = exchange(one[0], 0)
            newer = [(one[0], starts[0]), (near[0], starts[1]), (far[0], starts[2])]
            near_next = ahead(step + 1, 1, None, newer, cur, ())
            two = ahead(step, 3, coming[1], cur, old, [near_next[0]])
            newer.append((two[0], starts[3]))
        laps.append((one[1], near[1], far[1], two[1]))
        fields.append((one[0], near[0], far[0], two[0]))
        if not last:
            coming = [(message, 0, False), (exchange(two[0], 1), 0, False)]
            far = ahead(step + 1, 2, None, newer, cur, ())
            near, old, cur = near_next, cur, newer
    coming = [(message, 0, False), (exchange(two_adj, 1), 0, False)]
    keep, send, tile = curvature(laps, two_adj)
    tiles = swap(tile, "depth", 1)
    bit = 2
    old, cur, near = more, newer, near_next
    adjoints = [arrays_of(cur)]
    for step in range(STEPS - 2, 0, -1):
        far = back(step, 2, None, cur, old, (fields[step][2], starts[2]), ())
        after = [near, far, tiles]
        one = back(step, 0, coming[0], cur, old, (fields[step][0], starts[0]), after)
        message = exchange(one, 0)
        newer = [(one, starts[0]), (near, starts[1]), (far, starts[2])]
        if step > 1:
            near_next = back(step - 1, 1, None, newer, cur, (fields[step - 1][1], starts[1]), ())
            after = [near_next]
        else:
            after = [one]
        two = back(step, 3, coming[1], cur, old, (fields[step][3], starts[3]), after)
        newer.append((two, starts[3]))
        coming = [(message, 0, False), (exchange(two, 1), 0, False)]
        near, old, cur = near_next, cur, newer
        adjoints.insert(0, arrays_of(cur))
        if step == STEPS - 2:
            curv = sum(total_parts(keep, send, two))
        tile = tile + tiles
        if bit < lax.axis_size("depth"):
            tiles = swap(tile, "depth", bit)
            bit *= 2
    while bit < lax.axis_size("depth"):
        tile = tile + tiles
        tiles = swap(tile, "depth", bit)
        bit *= 2
    pieces = [(values, at) for values, at in zip(fields[0], starts)]
    inner = (starts[1], 2 * places[1][1])

    def finish(place, halo, sides, both, other, after):
        return adjoint_last(
            place, halo, cur, old, courant, [pieces[n] for n in sides], number, sums[0],
            [[lap[n] for n in sides] for lap in laps],
            [[a[n] for n in sides] for a in adjoints], both, other, after,
        )

    inside = finish(inner, None, (1, 2), [], [], [curv])
    one = finish(places[0], coming[0], (0,), [], [], inside[:1])
    outside = finish(places[3], coming[1], (3,), [tile, tiles], one, [])
    inner_parts = total_parts(*inside)
    outer_parts = total_parts(*outside)
    own = refresh(courant, inner_parts, outer_parts, curv, damping_table, plan_step)
    return assemble(own, swap(own, "shot", 1))


def solution(mesh):
    in_specs = (
        P("shot", "depth", None, None),
        P("shot", "depth", None, None),
        P("shot", "depth", None, None),
        P("shot", "depth", None, None),
        P("depth", None, None),
        P("shot", None),
        P("shot"),
        P("shot", None),
        P("shot", None, None),
        P(),
        P(),
    )
    out_specs = P("depth", None, None)
    return jax.shard_map(
        on_device, mesh=mesh, in_specs=in_specs, out_specs=out_specs, check_vma=False
    )
```

```python
import jax
import jax.numpy as jnp
from jax import lax
from jax.experimental import pallas as pl
from jax.experimental.pallas import tpu as pltpu
from jax.sharding import PartitionSpec as P

STEPS = 4
HALO = 4
ROWS = 8
PAD = HALO * ROWS

coeffs = (-205.0 / 72.0, 8.0 / 5.0, -1.0 / 5.0, 8.0 / 315.0, -1.0 / 560.0)

VMEM = pl.BlockSpec(memory_space=pltpu.VMEM)
SMEM = pl.BlockSpec(memory_space=pltpu.SMEM)
HBM = pl.BlockSpec(memory_space=pltpu.HBM)


def f32(*shape):
    return jax.ShapeDtypeStruct(shape, jnp.float32)


def params():
    return pltpu.CompilerParams(vmem_limit_bytes=6 * 2**20)


def cost(planes):
    return pl.CostEstimate(
        flops=planes * 10**4, bytes_accessed=planes * 2**10, transcendentals=0
    )


def split(value, size):
    if size & (size - 1) == 0:
        return value >> (size.bit_length() - 1), value & (size - 1)
    return value // size, value % size


def spread(x, width):
    s, g = split(x, width // ROWS)
    return g * ROWS + s


def interleave(put, get, width):
    for g in range(width // ROWS):
        put(g * ROWS, get(pl.ds(g, ROWS, stride=width // ROWS)))


def margins(pad, first, count, width):
    length = pad.shape[2]
    place = lax.broadcasted_iota(jnp.int32, (ROWS, length), 0)

    def body(i, _):
        p = first + i
        for j in range(HALO):
            at = j * ROWS
            low = pltpu.roll(pad[p, width + at : width + at + ROWS, :], 1, 0)
            pad[p, at : at + ROWS, :] = jnp.where(place == 0, 0.0, low)
            top = pltpu.roll(pad[p, PAD + at : PAD + at + ROWS, :], ROWS - 1, 0)
            beyond = PAD + width + at
            pad[p, beyond : beyond + ROWS, :] = jnp.where(place == ROWS - 1, 0.0, top)

    march(count, body)


def fill(pad, base, pieces, width):
    top = base + pad.shape[0]
    for ref, origin in pieces:
        begin = max(base, origin)
        end = min(top, origin + ref.shape[0])
        if end > begin:
            pad[begin - base : end - base, PAD : PAD + width, :] = ref[begin - origin : end - origin]


def fill_halo(pad, at, ref, ref_at, natural, width):
    odd = lax.axis_index("depth") % 2
    for i in range(HALO):
        if natural:

            def put(row, value, i=i):
                pad[at + i, PAD + row : PAD + row + ROWS, :] = value

            source = ref_at + jnp.where(odd == 1, i, HALO - 1 - i)
            interleave(put, lambda spot, source=source: ref[source, spot, :], width)
        else:
            pad[at + i, PAD : PAD + width, :] = ref[HALO - 1 - i]


def find(pieces, plane):
    for ref, origin in pieces:
        if origin <= plane < origin + ref.shape[0]:
            return ref, plane - origin


def columns(pad, along_ref, width):
    planes, _, length = along_ref.shape
    apart = lax.broadcasted_iota(jnp.int32, (length, length), 0)
    apart = jnp.abs(apart - lax.broadcasted_iota(jnp.int32, (length, length), 1))
    band = jnp.where(apart == 0, 3.0 * coeffs[0], 0.0)
    for k in range(1, 5):
        band = jnp.where(apart == k, coeffs[k], band)
    size = HALO if planes % (2 * HALO) else 2 * HALO
    for begin in range(0, planes, size):
        block = pad[HALO + begin : HALO + begin + size, PAD : PAD + width, :]
        product = jnp.dot(
            block.reshape(size * width, length),
            band,
            precision=lax.Precision.HIGHEST,
            preferred_element_type=jnp.float32,
        )
        along_ref[begin : begin + size] = product.reshape(size, width, length)


def stencil(pad, p, width, result):
    rows = slice(PAD, PAD + width)
    plane = pad[p]
    for k in range(1, 5):
        along = pad[p + k, rows, :] + pad[p - k, rows, :]
        along = along + plane[PAD + k * ROWS : PAD + k * ROWS + width]
        along = along + plane[PAD - k * ROWS : PAD - k * ROWS + width]
        result = result + coeffs[k] * along
    return plane[rows], result


def fold(values):
    width, length = values.shape
    return jnp.sum(values.reshape(width // 8, 8, length), axis=0)


def march(count, body, carry=None):
    return lax.fori_loop(0, count, body, carry, unroll=4 if count % 4 == 0 else 2)


def kernel_call(kernel, small, arrays, outs, scratch, planes):
    return pl.pallas_call(
        kernel,
        out_shape=tuple(outs),
        in_specs=[SMEM] * len(small) + [VMEM] * len(arrays),
        out_specs=tuple([VMEM] * len(outs)),
        scratch_shapes=scratch,
        compiler_params=params(),
        cost_estimate=cost(planes),
    )(*small, *arrays)


def grouped(refs, sizes):
    found = []
    for size in sizes:
        found.append(refs[:size])
        refs = refs[size:]
    return found, list(refs)


def ranges(slab):
    half = slab // 2 - HALO
    return [(0, HALO), (HALO, half), (HALO + half, half), (slab - HALO, HALO)]


def scratch_of(count, width, length):
    return [
        pltpu.VMEM((count, width, length), jnp.float32),
        pltpu.VMEM((count + 2 * HALO, width + 2 * PAD, length), jnp.float32),
    ]


def origins(field):
    return [at for _, at in field]


def arrays_of(field):
    return [values for values, _ in field]


def prepare(first, pad, along_ref, halo, cur, slab, width):
    count = along_ref.shape[0]
    fill(pad, first - HALO, cur, width)
    if halo is not None:
        fill_halo(pad, 0 if first == 0 else HALO + count, *halo, width)
    margins(pad, HALO, count, width)
    columns(pad, along_ref, width)


def forward(place, halo, cur, old, courant, source, wave, after):
    slab, width, length = courant.shape
    first, count = place
    groups = [[halo[0]] if halo else [], arrays_of(cur), arrays_of(old)]
    groups += [[courant, source, wave], list(after)]
    sizes = [len(g) for g in groups]

    def kernel(*refs):
        (halo_ref, cur_refs, old_refs, (c_ref, source_ref, wave_ref), _), refs = grouped(refs, sizes)
        next_ref, lap_ref, along_ref, pad = refs
        coming = (halo_ref[0], *halo[1:]) if halo else None
        prepare(first, pad, along_ref, coming, list(zip(cur_refs, origins(cur))), slab, width)
        old_ref, old_at = find(list(zip(old_refs, origins(old))), first)
        amplitude = wave_ref[0:1, :]

        def body(i, _):
            center, lap = stencil(pad, HALO + i, width, along_ref[i])
            lap_ref[i] = lap
            value = 2.0 * center - old_ref[old_at + i] + c_ref[first + i] * lap
            next_ref[i] = value + source_ref[first + i] * amplitude

        march(count, body)

    outs = [f32(count, width, length)] * 2
    return kernel_call(kernel, [], sum(groups, []), outs, scratch_of(count, width, length), count)


def adjoint(place, halo, cur, old, courant, field, number, observed, after):
    slab, width, length = courant.shape
    first, count = place
    groups = [[halo[0]] if halo else [], arrays_of(cur), arrays_of(old), arrays_of(field)]
    groups += [[courant, number, observed], list(after)]
    sizes = [len(g) for g in groups]

    def kernel(*refs):
        found, refs = grouped(refs, sizes)
        next_ref, along_ref, pad = refs
        adjoint_step(place, halo, cur, old, field, found, next_ref, along_ref, pad)

    outs = [f32(count, width, length)]
    scratch = scratch_of(count, width, length)
    return kernel_call(kernel, [], sum(groups, []), outs, scratch, count)[0]


def adjoint_step(place, halo, cur, old, field, found, next_ref, along_ref, pad):
    halo_ref, cur_refs, old_refs, field_refs, (c_ref, number_ref, observed_ref) = found[:5]
    slab, width, length = c_ref.shape
    first, count = place
    coming = (halo_ref[0], *halo[1:]) if halo else None
    prepare(first, pad, along_ref, coming, list(zip(cur_refs, origins(cur))), slab, width)
    for field_ref, field_at in zip(field_refs, origins(field)):
        begin, end = max(first, field_at), min(first + count, field_at + field_ref.shape[0])
        if end <= begin:
            continue
        old_ref, old_at = find(list(zip(old_refs, origins(old))), begin)

        def body(i, _, field_ref=field_ref, field_at=field_at, begin=begin, old_ref=old_ref, old_at=old_at):
            q = begin + i
            center, lap = stencil(pad, begin - first + HALO + i, width, along_ref[begin - first + i])
            value = 2.0 * center - old_ref[old_at + i] + c_ref[q] * lap
            miss = number_ref[q] * field_ref[begin - field_at + i] - observed_ref[q]
            next_ref[begin - first + i] = value + miss

        march(end - begin, body)


def adjoint_last(
    place, halo, cur, old, courant, field, number, observed, laps, adjoints, tile, other, after
):
    slab, width, length = courant.shape
    first, count = place
    inner = count > HALO
    groups = [[halo[0]] if halo else [], arrays_of(cur), arrays_of(old), arrays_of(field)]
    groups += [[courant, number, observed], sum(laps, []), sum(adjoints, [])]
    groups += [list(tile) + list(other), list(after)]
    sizes = [len(g) for g in groups]
    steps, parts = len(laps), len(laps[0])

    def kernel(*refs):
        found, refs = grouped(refs, sizes)
        next_ref, along_ref, pad = refs[-3:]
        adjoint_step(place, halo, cur, old, field, found, next_ref, along_ref, pad)
        lap_refs, adj_refs, more = found[5:8]
        core = lax.axis_index("shot") % 2

        def product(part, i):
            value = next_ref[part * (count // parts) + i] * lap_refs[part][i]
            for n in range(1, steps):
                value = value + adj_refs[(n - 1) * parts + part][i] * lap_refs[n * parts + part][i]
            return value

        def either(write):
            @pl.when(core == 0)
            def _():
                write(refs[0], refs[1])

            @pl.when(core == 1)
            def _():
                write(refs[1], refs[0])

        if inner:
            for part in (0, 1):

                @pl.when(core == part)
                def _(part=part):
                    for i in range(count // 2):
                        refs[0][i] = product(part, i)
                        write_piece(refs[1:-3], i, product(1 - part, i))

        elif not other:
            for i in range(HALO):
                refs[0][i] = product(0, i)
        else:
            tile_ref, tiles_ref, other_ref = more

            def write(first_ref, second_ref):
                for i in range(HALO):
                    rows = slice(i * width, (i + 1) * width)
                    first_ref[rows, :] = other_ref[i]
                    second_ref[rows, :] = product(0, i)

            either(write)
            for ref in refs[:2]:
                ref[HALO * width : HALO * width + 8, :] = tile_ref[...] + tiles_ref[...]

    if inner:
        outs = [f32(count // 2, width, length)]
        outs += [f32(count // 2 // 1, width, length)] * 1
    elif not other:
        outs = [f32(count, width, length)]
    else:
        outs = [f32(HALO * width + 8, length)] * 2
    scratch = [pltpu.VMEM((count, width, length), jnp.float32)] + scratch_of(count, width, length)
    return kernel_call(kernel, [], sum(groups, []), outs, scratch, count)


def curvature(laps, after):
    number = len(laps)
    half, width, length = laps[0][1].shape
    size = half + HALO

    def kernel(*refs):
        ranged = [refs[n * number : (n + 1) * number] for n in range(4)]
        keep_ref, *send_refs, tile_ref = refs[4 * number + 1 :]
        core = lax.axis_index("shot") % 2

        def squares(lap_refs, at):
            value = lap_refs[0][at] * lap_refs[0][at]
            for ref in lap_refs[1:]:
                value = value + ref[at] * ref[at]
            return value

        for part in (0, 1):

            @pl.when(core == part)
            def _(part=part):
                total = jnp.zeros((8, length), jnp.float32)
                own, far = (0, 1) if part == 0 else (3, 2)
                other = (3, 2) if part == 0 else (0, 1)
                for i in range(size):
                    outer = i >= half
                    value = squares(ranged[own if outer else far], i % half)
                    keep_ref[i] = value
                    total = total + fold(value)
                    value = squares(ranged[other[0] if outer else other[1]], i % half)
                    write_piece(send_refs, i, value)
                    total = total + fold(value)
                tile_ref[...] = total

    outs = [f32(size, width, length)]
    outs += [f32(size // 1, width, length)] * 1 + [f32(8, length)]
    arrays = [lap[n] for n in range(4) for lap in laps] + [after]
    return kernel_call(kernel, [], arrays, outs, [], 8)


def points(wavelet, source, cells, observed, slab, width, length):
    receivers = cells.shape[0]
    steps = observed.shape[0]
    area = width * length

    def kernel(wave_ref, source_ref, cell_ref, obs_ref, spot_ref, number_ref, *refs):
        row_refs, sum_refs = refs[:steps], refs[steps:]
        blank = jnp.zeros((width, length), jnp.float32)

        def clear(i, _):
            for ref in (spot_ref, number_ref) + sum_refs:
                ref[i] = blank

        march(slab, clear)
        depth = lax.axis_index("depth")
        offset = depth * (slab * area)
        odd = depth % 2
        column = lax.broadcasted_iota(jnp.int32, (1, length), 1)

        def add(local, terms):
            @pl.when((local >= 0) & (local < slab * area))
            def _():
                row, y = split(local, length)
                plane, x = split(row, width)
                q = jnp.where(odd == 1, plane, slab - 1 - plane)
                at = pl.ds(spread(x, width), 1)
                for ref, term in terms():
                    ref[q, at, :] = ref[q, at, :] + jnp.where(column == y, term, 0.0)

        add(source_ref[0] - offset, lambda: [(spot_ref, 1.0)])
        for n in range(steps):
            row_refs[n][...] = jnp.full((8, length), wave_ref[0, n], jnp.float32)

        def body(r, _):
            def terms():
                found = [(number_ref, 1.0)]
                for n in range(steps):
                    found.append((sum_refs[n], obs_ref[n, r]))
                return found

            add(cell_ref[r] - offset, terms)

        lax.fori_loop(0, receivers, body, None)

    volume = f32(slab, width, length)
    outs = [volume, volume] + [f32(8, length)] * steps + [volume] * steps
    small = [wavelet, source, cells, observed]
    found = kernel_call(kernel, small, [], outs, [], 8)
    return found[0], found[1], found[2 : 2 + steps], found[2 + steps :]


def interleaved(*arrays):
    number = len(arrays)
    slab, width, length = arrays[0].shape

    def kernel(*refs):
        odd = lax.axis_index("depth") % 2

        def body(i, _):
            plane = jnp.where(odd == 1, i, slab - 1 - i)
            for ref, out_ref in zip(refs[:number], refs[number:]):

                def put(at, value, out_ref=out_ref):
                    out_ref[i, at : at + ROWS, :] = value

                interleave(put, lambda spot, ref=ref: ref[plane, spot, :], width)

        march(slab, body)

    outs = [f32(slab, width, length)] * number
    return kernel_call(kernel, [], list(arrays), outs, [], 8)


def pack(field, adjoint_field):
    odd = lax.axis_index("depth") % 2
    far = field.shape[0] - HALO
    found = []
    for start in ((1 - odd) * far, odd * far):
        planes = [lax.dynamic_slice_in_dim(v, start, HALO, 0) for v in (field, adjoint_field)]
        found.append(jnp.concatenate(planes, axis=0))
    return found


def refresh(courant, inner_parts, outer_parts, curv, table, plan):
    slab, width, length = courant.shape
    half = inner_parts[0].shape[0]
    number = len(inner_parts)
    cells = slab * width * length * lax.axis_size("depth")

    def kernel(table_ref, plan_ref, c_ref, curv_ref, *rest):
        inner_refs = rest[:number]
        outer_refs = rest[number : 2 * number]
        out_ref = rest[2 * number]
        tail = slice(HALO * width, HALO * width + 8)
        tile = outer_refs[0][tail, :]
        for ref in outer_refs[1:]:
            tile = tile + ref[tail, :]
        level = jnp.sum(tile) / cells + 1e-06
        extra = table_ref[plan_ref[0]] * level
        core = lax.axis_index("shot") % 2
        odd = lax.axis_index("depth") % 2
        size = half + HALO

        def store(q, value):
            plane = jnp.where(odd == 1, q, size - 1 - q)
            for g in range(width // ROWS):
                spot = pl.ds(g, ROWS, stride=width // ROWS)
                out_ref[plane, spot, :] = value[g * ROWS : (g + 1) * ROWS]

        def body(i, _):
            grad = inner_refs[0][i]
            for ref in inner_refs[1:]:
                grad = grad + ref[i]
            model = c_ref[HALO + core * half + i]
            store((1 - core) * HALO + i, model - grad / (curv_ref[i] + extra))

        march(half, body)
        for i in range(HALO):
            rows = slice(i * width, (i + 1) * width)
            grad = outer_refs[0][rows, :]
            for ref in outer_refs[1:]:
                grad = grad + ref[rows, :]
            model = c_ref[core * (slab - HALO) + i]
            store(core * half + i, model - grad / (curv_ref[half + i] + extra))

    arrays = [courant, curv, *inner_parts, *outer_parts]
    outs = [f32(half + HALO, width, length)]
    return kernel_call(kernel, [table, plan], arrays, outs, [], half)[0]


def assemble(own, other):
    half, width, length = own.shape

    def kernel(own_ref, other_ref, out_ref, sems):
        core = lax.axis_index("shot") % 2
        upper = (lax.axis_index("depth") + core + 1) % 2
        copies = []
        for n, (ref, place) in enumerate([(own_ref, upper), (other_ref, 1 - upper)]):
            spot = out_ref.at[pl.ds(place * half, half)]
            copies.append(pltpu.make_async_copy(ref, spot, sems.at[n]))
        for copy in copies:
            copy.start()
        for copy in copies:
            copy.wait()

    return pl.pallas_call(
        kernel,
        out_shape=f32(2 * half, width, length),
        in_specs=[VMEM] * 2,
        out_specs=HBM,
        scratch_shapes=[pltpu.SemaphoreType.DMA((2,))],
        compiler_params=params(),
        cost_estimate=cost(8),
    )(own, other)


def exchange(values, side):
    links = []
    for i in range(side, lax.axis_size("depth") - 1, 2):
        links += [(i, i + 1), (i + 1, i)]
    return lax.ppermute(values, "depth", links)


def swap(values, axis, bit):
    count = lax.axis_size(axis)
    return lax.ppermute(values, axis, [(i, i ^ bit) for i in range(count)])


def sum_of(values, pieces, after):
    size = pieces[0].shape[0]

    def kernel(values_ref, *refs):
        for i in range(values.shape[0]):
            refs[-1][i] = values_ref[i] + refs[i // size][i % size]

    arrays = [values, *pieces, *after]
    return kernel_call(kernel, [], arrays, [f32(*values.shape)], [], 8)[0]


def total_parts(keep, send, after=()):
    if isinstance(send, (list, tuple)):
        parts = [keep, [swap(piece, "shot", 1) for piece in send]]
    else:
        parts = [keep, swap(send, "shot", 1)]
    bit = 2
    while bit < lax.axis_size("shot"):
        if isinstance(parts[1], list):
            here = sum_of(*parts, after)
        else:
            here = parts[0] + parts[1]
        parts = [here, swap(here, "shot", bit)]
        bit *= 2
    return parts


def write_piece(refs, i, value):
    size = refs[0].shape[0]
    refs[i // size][i % size] = value


def on_device(
    field_prev,
    field_now,
    adjoint_next,
    adjoint_after,
    courant,
    wavelet,
    source_cell,
    receiver_cell,
    observed,
    damping_table,
    plan_step,
):
    slab, width, length = courant.shape
    halos = [exchange(v, side) for side, v in enumerate(pack(field_now[0], adjoint_next[0]))]
    places = ranges(slab)
    starts = [first for first, _ in places]
    spot, number, waves, sums = points(
        wavelet, source_cell, receiver_cell[0], observed[0], slab, width, length
    )
    start, before, courant = interleaved(field_now[0], field_prev[0], courant)
    first, second = interleaved(adjoint_next[0], adjoint_after[0])
    old, cur = [(before, 0)], [(start, 0)]
    coming = [(halos[0], 0, True), (halos[1], 0, True)]

    def ahead(step, side, halo, cur, old, after):
        return forward(
            places[side], halo, cur, old, courant, spot, waves[step], after
        )

    def back(step, side, halo, cur, old, field, after):
        return adjoint(
            places[side], halo, cur, old, courant, [field], number, sums[step], after
        )

    laps, fields = [], []
    near = ahead(0, 1, None, cur, old, ())
    far = ahead(0, 2, None, cur, old, ())
    for step in range(STEPS):
        last = step == STEPS - 1
        after = [near[0], far[0]]
        if last:
            rest, more = [(second, 0)], [(first, 0)]
            near_adj = back(step, 1, None, more, rest, (near[0], starts[1]), ())
            far_adj = back(step, 2, None, more, rest, (far[0], starts[2]), ())
            after += [near_adj, far_adj]
        one = ahead(step, 0, coming[0], cur, old, after)
        if last:
            edge = (halos[0], HALO, True)
            one_adj = back(step, 0, edge, more, rest, (one[0], starts[0]), after)
            message = exchange(one_adj, 0)
            newer = [(one_adj, starts[0]), (near_adj, starts[1]), (far_adj, starts[2])]
            near_next = back(step - 1, 1, None, newer, more, (fields[-1][1], starts[1]), ())
            two = ahead(step, 3, coming[1], cur, old, [near_next])
            edge = (halos[1], HALO, True)
            two_adj = back(step, 3, edge, more, rest, (two[0], starts[3]), [near_next])
            newer.append((two_adj, starts[3]))
        else:
            message = exchange(one[0], 0)
            newer = [(one[0], starts[0]), (near[0], starts[1]), (far[0], starts[2])]
            near_next = ahead(step + 1, 1, None, newer, cur, ())
            two = ahead(step, 3, coming[1], cur, old, [near_next[0]])
            newer.append((two[0], starts[3]))
        laps.append((one[1], near[1], far[1], two[1]))
        fields.append((one[0], near[0], far[0], two[0]))
        if not last:
            coming = [(message, 0, False), (exchange(two[0], 1), 0, False)]
            far = ahead(step + 1, 2, None, newer, cur, ())
            near, old, cur = near_next, cur, newer
    coming = [(message, 0, False), (exchange(two_adj, 1), 0, False)]
    keep, *send, tile = curvature(laps, two_adj)
    tiles = swap(tile, "depth", 1)
    bit = 2
    old, cur, near = more, newer, near_next
    adjoints = [arrays_of(cur)]
    for step in range(STEPS - 2, 0, -1):
        far = back(step, 2, None, cur, old, (fields[step][2], starts[2]), ())
        after = [near, far]
        one = back(step, 0, coming[0], cur, old, (fields[step][0], starts[0]), after)
        message = exchange(one, 0)
        newer = [(one, starts[0]), (near, starts[1]), (far, starts[2])]
        if step > 1:
            near_next = back(step - 1, 1, None, newer, cur, (fields[step - 1][1], starts[1]), ())
            after = [near_next, tiles]
        else:
            after = [one, tiles]
        two = back(step, 3, coming[1], cur, old, (fields[step][3], starts[3]), after)
        newer.append((two, starts[3]))
        coming = [(message, 0, False), (exchange(two, 1), 0, False)]
        near, old, cur = near_next, cur, newer
        adjoints.insert(0, arrays_of(cur))
        if step == STEPS - 2:
            curv = sum(total_parts(keep, send, [two]))
        tile = tile + tiles
        if bit < lax.axis_size("depth"):
            tiles = swap(tile, "depth", bit)
            bit *= 2
    while bit < lax.axis_size("depth"):
        tile = tile + tiles
        tiles = swap(tile, "depth", bit)
        bit *= 2
    pieces = [(values, at) for values, at in zip(fields[0], starts)]
    inner = (starts[1], 2 * places[1][1])

    def finish(place, halo, sides, both, other, after):
        return adjoint_last(
            place, halo, cur, old, courant, [pieces[n] for n in sides], number, sums[0],
            [[lap[n] for n in sides] for lap in laps],
            [[a[n] for n in sides] for a in adjoints], both, other, after,
        )

    inside = finish(inner, None, (1, 2), [], [], [])
    one = finish(places[0], coming[0], (0,), [], [], inside[:1])
    outside = finish(places[3], coming[1], (3,), [tile, tiles], one, [curv])
    inner_parts = total_parts(inside[0], inside[1:])
    outer_parts = total_parts(*outside)
    own = refresh(courant, inner_parts, outer_parts, curv, damping_table, plan_step)
    return assemble(own, swap(own, "shot", 1))


def solution(mesh):
    in_specs = (
        P("shot", "depth", None, None),
        P("shot", "depth", None, None),
        P("shot", "depth", None, None),
        P("shot", "depth", None, None),
        P("depth", None, None),
        P("shot", None),
        P("shot"),
        P("shot", None),
        P("shot", None, None),
        P(),
        P(),
    )
    out_specs = P("depth", None, None)
    return jax.shard_map(
        on_device, mesh=mesh, in_specs=in_specs, out_specs=out_specs, check_vma=False
    )
```

```python
import jax
import jax.numpy as jnp
from jax import lax
from jax.experimental import pallas as pl
from jax.experimental.pallas import tpu as pltpu
from jax.sharding import PartitionSpec as P

STEPS = 4
HALO = 4
ROWS = 8
PAD = HALO * ROWS

coeffs = (-205.0 / 72.0, 8.0 / 5.0, -1.0 / 5.0, 8.0 / 315.0, -1.0 / 560.0)

VMEM = pl.BlockSpec(memory_space=pltpu.VMEM)
SMEM = pl.BlockSpec(memory_space=pltpu.SMEM)
HBM = pl.BlockSpec(memory_space=pltpu.HBM)


def f32(*shape):
    return jax.ShapeDtypeStruct(shape, jnp.float32)


def params():
    return pltpu.CompilerParams(vmem_limit_bytes=6 * 2**20)


def cost(planes):
    return pl.CostEstimate(
        flops=planes * 10**4, bytes_accessed=planes * 2**10, transcendentals=0
    )


def split(value, size):
    if size & (size - 1) == 0:
        return value >> (size.bit_length() - 1), value & (size - 1)
    return value // size, value % size


def spread(x, width):
    s, g = split(x, width // ROWS)
    return g * ROWS + s


def interleave(put, get, width):
    for g in range(width // ROWS):
        put(g * ROWS, get(pl.ds(g, ROWS, stride=width // ROWS)))


def margins(pad, first, count, width):
    length = pad.shape[2]
    place = lax.broadcasted_iota(jnp.int32, (ROWS, length), 0)

    def body(i, _):
        p = first + i
        for j in range(HALO):
            at = j * ROWS
            low = pltpu.roll(pad[p, width + at : width + at + ROWS, :], 1, 0)
            pad[p, at : at + ROWS, :] = jnp.where(place == 0, 0.0, low)
            top = pltpu.roll(pad[p, PAD + at : PAD + at + ROWS, :], ROWS - 1, 0)
            beyond = PAD + width + at
            pad[p, beyond : beyond + ROWS, :] = jnp.where(place == ROWS - 1, 0.0, top)

    march(count, body)


def fill(pad, base, pieces, width):
    top = base + pad.shape[0]
    for ref, origin in pieces:
        begin = max(base, origin)
        end = min(top, origin + ref.shape[0])
        if end > begin:
            pad[begin - base : end - base, PAD : PAD + width, :] = ref[begin - origin : end - origin]


def fill_halo(pad, at, ref, ref_at, natural, width):
    odd = lax.axis_index("depth") % 2
    for i in range(HALO):
        if natural:

            def put(row, value, i=i):
                pad[at + i, PAD + row : PAD + row + ROWS, :] = value

            source = ref_at + jnp.where(odd == 1, i, HALO - 1 - i)
            interleave(put, lambda spot, source=source: ref[source, spot, :], width)
        elif len(ref.shape) == 2:
            rows = slice((HALO - 1 - i) * width, (HALO - i) * width)
            pad[at + i, PAD : PAD + width, :] = ref[rows, :]
        else:
            pad[at + i, PAD : PAD + width, :] = ref[HALO - 1 - i]


def find(pieces, plane):
    for ref, origin in pieces:
        if origin <= plane < origin + ref.shape[0]:
            return ref, plane - origin


def columns(pad, along_ref, width):
    planes, _, length = along_ref.shape
    apart = lax.broadcasted_iota(jnp.int32, (length, length), 0)
    apart = jnp.abs(apart - lax.broadcasted_iota(jnp.int32, (length, length), 1))
    band = jnp.where(apart == 0, 3.0 * coeffs[0], 0.0)
    for k in range(1, 5):
        band = jnp.where(apart == k, coeffs[k], band)
    size = HALO if planes % (2 * HALO) else 2 * HALO
    for begin in range(0, planes, size):
        block = pad[HALO + begin : HALO + begin + size, PAD : PAD + width, :]
        product = jnp.dot(
            block.reshape(size * width, length),
            band,
            precision=lax.Precision.HIGHEST,
            preferred_element_type=jnp.float32,
        )
        along_ref[begin : begin + size] = product.reshape(size, width, length)


def stencil(pad, p, width, result):
    rows = slice(PAD, PAD + width)
    plane = pad[p]
    for k in range(1, 5):
        along = pad[p + k, rows, :] + pad[p - k, rows, :]
        along = along + plane[PAD + k * ROWS : PAD + k * ROWS + width]
        along = along + plane[PAD - k * ROWS : PAD - k * ROWS + width]
        result = result + coeffs[k] * along
    return plane[rows], result


def fold(values):
    width, length = values.shape
    return jnp.sum(values.reshape(width // 8, 8, length), axis=0)


def march(count, body, carry=None):
    return lax.fori_loop(0, count, body, carry, unroll=4 if count % 4 == 0 else 2)


def kernel_call(kernel, small, arrays, outs, scratch, planes):
    return pl.pallas_call(
        kernel,
        out_shape=tuple(outs),
        in_specs=[SMEM] * len(small) + [VMEM] * len(arrays),
        out_specs=tuple([VMEM] * len(outs)),
        scratch_shapes=scratch,
        compiler_params=params(),
        cost_estimate=cost(planes),
    )(*small, *arrays)


def grouped(refs, sizes):
    found = []
    for size in sizes:
        found.append(refs[:size])
        refs = refs[size:]
    return found, list(refs)


def ranges(slab):
    half = slab // 2 - HALO
    return [(0, HALO), (HALO, half), (HALO + half, half), (slab - HALO, HALO)]


def scratch_of(count, width, length):
    return [
        pltpu.VMEM((count, width, length), jnp.float32),
        pltpu.VMEM((count + 2 * HALO, width + 2 * PAD, length), jnp.float32),
    ]


def origins(field):
    return [at for _, at in field]


def arrays_of(field):
    return [values for values, _ in field]


def prepare(first, pad, along_ref, halo, cur, slab, width):
    count = along_ref.shape[0]
    fill(pad, first - HALO, cur, width)
    if halo is not None:
        fill_halo(pad, 0 if first == 0 else HALO + count, *halo, width)
    margins(pad, HALO, count, width)
    columns(pad, along_ref, width)


def forward(place, halo, cur, old, courant, source, wave, after):
    slab, width, length = courant.shape
    first, count = place
    groups = [[halo[0]] if halo else [], arrays_of(cur), arrays_of(old)]
    groups += [[courant, source, wave], list(after)]
    sizes = [len(g) for g in groups]

    def kernel(*refs):
        (halo_ref, cur_refs, old_refs, (c_ref, source_ref, wave_ref), _), refs = grouped(refs, sizes)
        next_ref, lap_ref, along_ref, pad = refs
        coming = (halo_ref[0], *halo[1:]) if halo else None
        prepare(first, pad, along_ref, coming, list(zip(cur_refs, origins(cur))), slab, width)
        old_ref, old_at = find(list(zip(old_refs, origins(old))), first)
        amplitude = wave_ref[0:1, :]

        def body(i, _):
            center, lap = stencil(pad, HALO + i, width, along_ref[i])
            lap_ref[i] = lap
            value = 2.0 * center - old_ref[old_at + i] + c_ref[first + i] * lap
            next_ref[i] = value + source_ref[first + i] * amplitude

        march(count, body)

    outs = [f32(count, width, length)] * 2
    return kernel_call(kernel, [], sum(groups, []), outs, scratch_of(count, width, length), count)


def adjoint(place, halo, cur, old, courant, field, number, observed, after):
    slab, width, length = courant.shape
    first, count = place
    groups = [[halo[0]] if halo else [], arrays_of(cur), arrays_of(old), arrays_of(field)]
    groups += [[courant, number, observed], list(after)]
    sizes = [len(g) for g in groups]

    def kernel(*refs):
        found, refs = grouped(refs, sizes)
        next_ref, along_ref, pad = refs
        adjoint_step(place, halo, cur, old, field, found, next_ref, along_ref, pad)

    outs = [f32(count, width, length)]
    scratch = scratch_of(count, width, length)
    return kernel_call(kernel, [], sum(groups, []), outs, scratch, count)[0]


def adjoint_step(place, halo, cur, old, field, found, next_ref, along_ref, pad):
    halo_ref, cur_refs, old_refs, field_refs, (c_ref, number_ref, observed_ref) = found[:5]
    slab, width, length = c_ref.shape
    first, count = place
    coming = (halo_ref[0], *halo[1:]) if halo else None
    prepare(first, pad, along_ref, coming, list(zip(cur_refs, origins(cur))), slab, width)
    for field_ref, field_at in zip(field_refs, origins(field)):
        begin, end = max(first, field_at), min(first + count, field_at + field_ref.shape[0])
        if end <= begin:
            continue
        old_ref, old_at = find(list(zip(old_refs, origins(old))), begin)

        def body(i, _, field_ref=field_ref, field_at=field_at, begin=begin, old_ref=old_ref, old_at=old_at):
            q = begin + i
            center, lap = stencil(pad, begin - first + HALO + i, width, along_ref[begin - first + i])
            value = 2.0 * center - old_ref[old_at + i] + c_ref[q] * lap
            miss = number_ref[q] * field_ref[begin - field_at + i] - observed_ref[q]
            next_ref[begin - first + i] = value + miss

        march(end - begin, body)


def adjoint_last(
    place, halo, cur, old, courant, field, number, observed, laps, adjoints, tile, other, after
):
    slab, width, length = courant.shape
    first, count = place
    inner = count > HALO
    groups = [[halo[0]] if halo else [], arrays_of(cur), arrays_of(old), arrays_of(field)]
    groups += [[courant, number, observed], sum(laps, []), sum(adjoints, [])]
    groups += [list(tile) + list(other), list(after)]
    sizes = [len(g) for g in groups]
    steps, parts = len(laps), len(laps[0])

    def kernel(*refs):
        found, refs = grouped(refs, sizes)
        next_ref, along_ref, pad = refs[-3:]
        adjoint_step(place, halo, cur, old, field, found, next_ref, along_ref, pad)
        lap_refs, adj_refs, more = found[5:8]
        core = lax.axis_index("shot") % 2

        def product(part, i):
            value = next_ref[part * (count // parts) + i] * lap_refs[part][i]
            for n in range(1, steps):
                value = value + adj_refs[(n - 1) * parts + part][i] * lap_refs[n * parts + part][i]
            return value

        def either(write):
            @pl.when(core == 0)
            def _():
                write(refs[0], refs[1])

            @pl.when(core == 1)
            def _():
                write(refs[1], refs[0])

        if inner:
            for part in (0, 1):

                @pl.when(core == part)
                def _(part=part):
                    for i in range(count // 2):
                        refs[0][i] = product(part, i)
                        write_piece(refs[1:-3], i, product(1 - part, i))

        elif not other:
            for i in range(HALO):
                refs[0][i] = product(0, i)
        else:
            tile_ref, tiles_ref, other_ref = more

            def write(first_ref, second_ref):
                for i in range(HALO):
                    rows = slice(i * width, (i + 1) * width)
                    first_ref[rows, :] = other_ref[i]
                    second_ref[rows, :] = product(0, i)

            either(write)
            for ref in refs[:2]:
                ref[HALO * width : HALO * width + 8, :] = tile_ref[...] + tiles_ref[...]

    if inner:
        outs = [f32(count // 2, width, length)]
        outs += [f32(count // 2 // 1, width, length)] * 1
    elif not other:
        outs = [f32(count, width, length)]
    else:
        outs = [f32(HALO * width + 8, length)] * 2
    scratch = [pltpu.VMEM((count, width, length), jnp.float32)] + scratch_of(count, width, length)
    return kernel_call(kernel, [], sum(groups, []), outs, scratch, count)


def curvature(laps, message, after):
    number = len(laps)
    half, width, length = laps[0][1].shape
    size = half + HALO

    def kernel(*refs):
        ranged = [refs[n * number : (n + 1) * number] for n in range(4)]
        planes_ref = refs[4 * number]
        keep_ref, *send_refs, tile_ref, message_ref = refs[4 * number + 2 :]
        for i in range(HALO):
            message_ref[i * width : (i + 1) * width, :] = planes_ref[i]
        core = lax.axis_index("shot") % 2

        def squares(lap_refs, at):
            value = lap_refs[0][at] * lap_refs[0][at]
            for ref in lap_refs[1:]:
                value = value + ref[at] * ref[at]
            return value

        for part in (0, 1):

            @pl.when(core == part)
            def _(part=part):
                total = jnp.zeros((8, length), jnp.float32)
                own, far = (0, 1) if part == 0 else (3, 2)
                other = (3, 2) if part == 0 else (0, 1)
                for i in range(size):
                    outer = i >= half
                    value = squares(ranged[own if outer else far], i % half)
                    keep_ref[i] = value
                    total = total + fold(value)
                    value = squares(ranged[other[0] if outer else other[1]], i % half)
                    write_piece(send_refs, i, value)
                    total = total + fold(value)
                tile_ref[...] = total
                message_ref[HALO * width : HALO * width + 8, :] = total

    outs = [f32(size, width, length)]
    outs += [f32(size // 1, width, length)] * 1 + [f32(8, length), f32(HALO * width + 8, length)]
    arrays = [lap[n] for n in range(4) for lap in laps] + [message, after]
    return kernel_call(kernel, [], arrays, outs, [], 8)


def points(wavelet, source, cells, observed, slab, width, length):
    receivers = cells.shape[0]
    steps = observed.shape[0]
    area = width * length

    def kernel(wave_ref, source_ref, cell_ref, obs_ref, spot_ref, number_ref, *refs):
        row_refs, sum_refs = refs[:steps], refs[steps:]
        blank = jnp.zeros((width, length), jnp.float32)

        def clear(i, _):
            for ref in (spot_ref, number_ref) + sum_refs:
                ref[i] = blank

        march(slab, clear)
        depth = lax.axis_index("depth")
        offset = depth * (slab * area)
        odd = depth % 2
        column = lax.broadcasted_iota(jnp.int32, (1, length), 1)

        def add(local, terms):
            @pl.when((local >= 0) & (local < slab * area))
            def _():
                row, y = split(local, length)
                plane, x = split(row, width)
                q = jnp.where(odd == 1, plane, slab - 1 - plane)
                at = pl.ds(spread(x, width), 1)
                for ref, term in terms():
                    ref[q, at, :] = ref[q, at, :] + jnp.where(column == y, term, 0.0)

        add(source_ref[0] - offset, lambda: [(spot_ref, 1.0)])
        for n in range(steps):
            row_refs[n][...] = jnp.full((8, length), wave_ref[0, n], jnp.float32)

        def body(r, _):
            def terms():
                found = [(number_ref, 1.0)]
                for n in range(steps):
                    found.append((sum_refs[n], obs_ref[n, r]))
                return found

            add(cell_ref[r] - offset, terms)

        lax.fori_loop(0, receivers, body, None)

    volume = f32(slab, width, length)
    outs = [volume, volume] + [f32(8, length)] * steps + [volume] * steps
    small = [wavelet, source, cells, observed]
    found = kernel_call(kernel, small, [], outs, [], 8)
    return found[0], found[1], found[2 : 2 + steps], found[2 + steps :]


def interleaved(*arrays):
    number = len(arrays)
    slab, width, length = arrays[0].shape

    def kernel(*refs):
        odd = lax.axis_index("depth") % 2

        def body(i, _):
            plane = jnp.where(odd == 1, i, slab - 1 - i)
            for ref, out_ref in zip(refs[:number], refs[number:]):

                def put(at, value, out_ref=out_ref):
                    out_ref[i, at : at + ROWS, :] = value

                interleave(put, lambda spot, ref=ref: ref[plane, spot, :], width)

        march(slab, body)

    outs = [f32(slab, width, length)] * number
    return kernel_call(kernel, [], list(arrays), outs, [], 8)


def pack(field, adjoint_field):
    odd = lax.axis_index("depth") % 2
    far = field.shape[0] - HALO
    found = []
    for start in ((1 - odd) * far, odd * far):
        planes = [lax.dynamic_slice_in_dim(v, start, HALO, 0) for v in (field, adjoint_field)]
        found.append(jnp.concatenate(planes, axis=0))
    return found


def refresh(courant, inner_parts, outer_parts, curv, table, plan):
    slab, width, length = courant.shape
    half = inner_parts[0].shape[0]
    number = len(inner_parts)
    cells = slab * width * length * lax.axis_size("depth")

    def kernel(table_ref, plan_ref, c_ref, curv_ref, *rest):
        inner_refs = rest[:number]
        outer_refs = rest[number : 2 * number]
        out_ref = rest[2 * number]
        tail = slice(HALO * width, HALO * width + 8)
        tile = outer_refs[0][tail, :]
        for ref in outer_refs[1:]:
            tile = tile + ref[tail, :]
        level = jnp.sum(tile) / cells + 1e-06
        extra = table_ref[plan_ref[0]] * level
        core = lax.axis_index("shot") % 2
        odd = lax.axis_index("depth") % 2
        size = half + HALO

        def store(q, value):
            plane = jnp.where(odd == 1, q, size - 1 - q)
            for g in range(width // ROWS):
                spot = pl.ds(g, ROWS, stride=width // ROWS)
                out_ref[plane, spot, :] = value[g * ROWS : (g + 1) * ROWS]

        def body(i, _):
            grad = inner_refs[0][i]
            for ref in inner_refs[1:]:
                grad = grad + ref[i]
            model = c_ref[HALO + core * half + i]
            store((1 - core) * HALO + i, model - grad / (curv_ref[i] + extra))

        march(half, body)
        for i in range(HALO):
            rows = slice(i * width, (i + 1) * width)
            grad = outer_refs[0][rows, :]
            for ref in outer_refs[1:]:
                grad = grad + ref[rows, :]
            model = c_ref[core * (slab - HALO) + i]
            store(core * half + i, model - grad / (curv_ref[half + i] + extra))

    arrays = [courant, curv, *inner_parts, *outer_parts]
    outs = [f32(half + HALO, width, length)]
    return kernel_call(kernel, [table, plan], arrays, outs, [], half)[0]


def assemble(own, other):
    half, width, length = own.shape

    def kernel(own_ref, other_ref, out_ref, sems):
        core = lax.axis_index("shot") % 2
        upper = (lax.axis_index("depth") + core + 1) % 2
        copies = []
        for n, (ref, place) in enumerate([(own_ref, upper), (other_ref, 1 - upper)]):
            spot = out_ref.at[pl.ds(place * half, half)]
            copies.append(pltpu.make_async_copy(ref, spot, sems.at[n]))
        for copy in copies:
            copy.start()
        for copy in copies:
            copy.wait()

    return pl.pallas_call(
        kernel,
        out_shape=f32(2 * half, width, length),
        in_specs=[VMEM] * 2,
        out_specs=HBM,
        scratch_shapes=[pltpu.SemaphoreType.DMA((2,))],
        compiler_params=params(),
        cost_estimate=cost(8),
    )(own, other)


def exchange(values, side):
    links = []
    for i in range(side, lax.axis_size("depth") - 1, 2):
        links += [(i, i + 1), (i + 1, i)]
    return lax.ppermute(values, "depth", links)


def swap(values, axis, bit):
    count = lax.axis_size(axis)
    return lax.ppermute(values, axis, [(i, i ^ bit) for i in range(count)])


def sum_of(values, pieces, after):
    size = pieces[0].shape[0]

    def kernel(values_ref, *refs):
        for i in range(values.shape[0]):
            refs[-1][i] = values_ref[i] + refs[i // size][i % size]

    arrays = [values, *pieces, *after]
    return kernel_call(kernel, [], arrays, [f32(*values.shape)], [], 8)[0]


def total_parts(keep, send, after=()):
    if isinstance(send, (list, tuple)):
        parts = [keep, [swap(piece, "shot", 1) for piece in send]]
    else:
        parts = [keep, swap(send, "shot", 1)]
    bit = 2
    while bit < lax.axis_size("shot"):
        if isinstance(parts[1], list):
            here = sum_of(*parts, after)
        else:
            here = parts[0] + parts[1]
        parts = [here, swap(here, "shot", bit)]
        bit *= 2
    return parts


def write_piece(refs, i, value):
    size = refs[0].shape[0]
    refs[i // size][i % size] = value


def on_device(
    field_prev,
    field_now,
    adjoint_next,
    adjoint_after,
    courant,
    wavelet,
    source_cell,
    receiver_cell,
    observed,
    damping_table,
    plan_step,
):
    slab, width, length = courant.shape
    halos = [exchange(v, side) for side, v in enumerate(pack(field_now[0], adjoint_next[0]))]
    places = ranges(slab)
    starts = [first for first, _ in places]
    spot, number, waves, sums = points(
        wavelet, source_cell, receiver_cell[0], observed[0], slab, width, length
    )
    start, before, courant = interleaved(field_now[0], field_prev[0], courant)
    first, second = interleaved(adjoint_next[0], adjoint_after[0])
    old, cur = [(before, 0)], [(start, 0)]
    coming = [(halos[0], 0, True), (halos[1], 0, True)]

    def ahead(step, side, halo, cur, old, after):
        return forward(
            places[side], halo, cur, old, courant, spot, waves[step], after
        )

    def back(step, side, halo, cur, old, field, after):
        return adjoint(
            places[side], halo, cur, old, courant, [field], number, sums[step], after
        )

    laps, fields = [], []
    near = ahead(0, 1, None, cur, old, ())
    far = ahead(0, 2, None, cur, old, ())
    for step in range(STEPS):
        last = step == STEPS - 1
        after = [near[0], far[0]]
        if last:
            rest, more = [(second, 0)], [(first, 0)]
            near_adj = back(step, 1, None, more, rest, (near[0], starts[1]), ())
            far_adj = back(step, 2, None, more, rest, (far[0], starts[2]), ())
            after += [near_adj, far_adj]
        one = ahead(step, 0, coming[0], cur, old, after)
        if last:
            edge = (halos[0], HALO, True)
            one_adj = back(step, 0, edge, more, rest, (one[0], starts[0]), after)
            newer = [(one_adj, starts[0]), (near_adj, starts[1]), (far_adj, starts[2])]
            near_next = back(step - 1, 1, None, newer, more, (fields[-1][1], starts[1]), ())
            two = ahead(step, 3, coming[1], cur, old, [near_next])
            edge = (halos[1], HALO, True)
            two_adj = back(step, 3, edge, more, rest, (two[0], starts[3]), [near_next])
            newer.append((two_adj, starts[3]))
        else:
            message = exchange(one[0], 0)
            newer = [(one[0], starts[0]), (near[0], starts[1]), (far[0], starts[2])]
            near_next = ahead(step + 1, 1, None, newer, cur, ())
            two = ahead(step, 3, coming[1], cur, old, [near_next[0]])
            newer.append((two[0], starts[3]))
        laps.append((one[1], near[1], far[1], two[1]))
        fields.append((one[0], near[0], far[0], two[0]))
        if not last:
            coming = [(message, 0, False), (exchange(two[0], 1), 0, False)]
            far = ahead(step + 1, 2, None, newer, cur, ())
            near, old, cur = near_next, cur, newer
    keep, *send, tile, message = curvature(laps, one_adj, two_adj)
    message = exchange(message, 0)
    coming = [(message, 0, False), (exchange(two_adj, 1), 0, False)]
    tiles = message[HALO * width :, :]
    bit = 2
    old, cur, near = more, newer, near_next
    adjoints = [arrays_of(cur)]
    for step in range(STEPS - 2, 0, -1):
        far = back(step, 2, None, cur, old, (fields[step][2], starts[2]), ())
        after = [near, far]
        one = back(step, 0, coming[0], cur, old, (fields[step][0], starts[0]), after)
        message = exchange(one, 0)
        if bit < lax.axis_size("depth"):
            tile = tile + tiles
            tiles = swap(tile, "depth", bit)
            bit *= 2
        newer = [(one, starts[0]), (near, starts[1]), (far, starts[2])]
        if step > 1:
            near_next = back(step - 1, 1, None, newer, cur, (fields[step - 1][1], starts[1]), ())
            after = [near_next, tiles]
        else:
            after = [one, tiles]
        two = back(step, 3, coming[1], cur, old, (fields[step][3], starts[3]), after)
        newer.append((two, starts[3]))
        coming = [(message, 0, False), (exchange(two, 1), 0, False)]
        near, old, cur = near_next, cur, newer
        adjoints.insert(0, arrays_of(cur))
        if step == STEPS - 2:
            curv = sum(total_parts(keep, send, [two]))
    while bit < lax.axis_size("depth"):
        tile = tile + tiles
        tiles = swap(tile, "depth", bit)
        bit *= 2
    pieces = [(values, at) for values, at in zip(fields[0], starts)]
    inner = (starts[1], 2 * places[1][1])

    def finish(place, halo, sides, both, other, after):
        return adjoint_last(
            place, halo, cur, old, courant, [pieces[n] for n in sides], number, sums[0],
            [[lap[n] for n in sides] for lap in laps],
            [[a[n] for n in sides] for a in adjoints], both, other, after,
        )

    inside = finish(inner, None, (1, 2), [], [], [])
    one = finish(places[0], coming[0], (0,), [], [], inside[:1])
    outside = finish(places[3], coming[1], (3,), [tile, tiles], one, [curv])
    inner_parts = total_parts(inside[0], inside[1:])
    outer_parts = total_parts(*outside)
    own = refresh(courant, inner_parts, outer_parts, curv, damping_table, plan_step)
    return assemble(own, swap(own, "shot", 1))


def solution(mesh):
    in_specs = (
        P("shot", "depth", None, None),
        P("shot", "depth", None, None),
        P("shot", "depth", None, None),
        P("shot", "depth", None, None),
        P("depth", None, None),
        P("shot", None),
        P("shot"),
        P("shot", None),
        P("shot", None, None),
        P(),
        P(),
    )
    out_specs = P("depth", None, None)
    return jax.shard_map(
        on_device, mesh=mesh, in_specs=in_specs, out_specs=out_specs, check_vma=False
    )
```

```python
import jax
import jax.numpy as jnp
from jax import lax
from jax.experimental import pallas as pl
from jax.experimental.pallas import tpu as pltpu
from jax.sharding import PartitionSpec as P

STEPS = 4
HALO = 4
ROWS = 8
PAD = HALO * ROWS

coeffs = (-205.0 / 72.0, 8.0 / 5.0, -1.0 / 5.0, 8.0 / 315.0, -1.0 / 560.0)

VMEM = pl.BlockSpec(memory_space=pltpu.VMEM)
SMEM = pl.BlockSpec(memory_space=pltpu.SMEM)
HBM = pl.BlockSpec(memory_space=pltpu.HBM)


def f32(*shape):
    return jax.ShapeDtypeStruct(shape, jnp.float32)


def params():
    return pltpu.CompilerParams(vmem_limit_bytes=6 * 2**20)


def cost(planes):
    return pl.CostEstimate(
        flops=planes * 10**4, bytes_accessed=planes * 2**10, transcendentals=0
    )


def split(value, size):
    if size & (size - 1) == 0:
        return value >> (size.bit_length() - 1), value & (size - 1)
    return value // size, value % size


def spread(x, width):
    s, g = split(x, width // ROWS)
    return g * ROWS + s


def interleave(put, get, width):
    for g in range(width // ROWS):
        put(g * ROWS, get(pl.ds(g, ROWS, stride=width // ROWS)))


def margins(pad, first, count, width):
    length = pad.shape[2]
    place = lax.broadcasted_iota(jnp.int32, (ROWS, length), 0)

    def body(i, _):
        p = first + i
        for j in range(HALO):
            at = j * ROWS
            low = pltpu.roll(pad[p, width + at : width + at + ROWS, :], 1, 0)
            pad[p, at : at + ROWS, :] = jnp.where(place == 0, 0.0, low)
            top = pltpu.roll(pad[p, PAD + at : PAD + at + ROWS, :], ROWS - 1, 0)
            beyond = PAD + width + at
            pad[p, beyond : beyond + ROWS, :] = jnp.where(place == ROWS - 1, 0.0, top)

    march(count, body)


def fill(pad, base, pieces, width):
    top = base + pad.shape[0]
    for ref, origin in pieces:
        begin = max(base, origin)
        end = min(top, origin + ref.shape[0])
        if end > begin:
            pad[begin - base : end - base, PAD : PAD + width, :] = ref[begin - origin : end - origin]


def fill_halo(pad, at, ref, ref_at, natural, width):
    odd = lax.axis_index("depth") % 2
    for i in range(HALO):
        if natural:

            def put(row, value, i=i):
                pad[at + i, PAD + row : PAD + row + ROWS, :] = value

            source = ref_at + jnp.where(odd == 1, i, HALO - 1 - i)
            interleave(put, lambda spot, source=source: ref[source, spot, :], width)
        elif len(ref.shape) == 2:
            rows = slice((HALO - 1 - i) * width, (HALO - i) * width)
            pad[at + i, PAD : PAD + width, :] = ref[rows, :]
        else:
            pad[at + i, PAD : PAD + width, :] = ref[HALO - 1 - i]


def find(pieces, plane):
    for ref, origin in pieces:
        if origin <= plane < origin + ref.shape[0]:
            return ref, plane - origin


def columns(pad, along_ref, width):
    planes, _, length = along_ref.shape
    apart = lax.broadcasted_iota(jnp.int32, (length, length), 0)
    apart = jnp.abs(apart - lax.broadcasted_iota(jnp.int32, (length, length), 1))
    band = jnp.where(apart == 0, 3.0 * coeffs[0], 0.0)
    for k in range(1, 5):
        band = jnp.where(apart == k, coeffs[k], band)
    size = HALO if planes % (2 * HALO) else 2 * HALO
    for begin in range(0, planes, size):
        block = pad[HALO + begin : HALO + begin + size, PAD : PAD + width, :]
        product = jnp.dot(
            block.reshape(size * width, length),
            band,
            precision=lax.Precision.HIGHEST,
            preferred_element_type=jnp.float32,
        )
        along_ref[begin : begin + size] = product.reshape(size, width, length)


def stencil(pad, p, width, result):
    rows = slice(PAD, PAD + width)
    plane = pad[p]
    for k in range(1, 5):
        along = pad[p + k, rows, :] + pad[p - k, rows, :]
        along = along + plane[PAD + k * ROWS : PAD + k * ROWS + width]
        along = along + plane[PAD - k * ROWS : PAD - k * ROWS + width]
        result = result + coeffs[k] * along
    return plane[rows], result


def fold(values):
    width, length = values.shape
    return jnp.sum(values.reshape(width // 8, 8, length), axis=0)


def march(count, body, carry=None):
    return lax.fori_loop(0, count, body, carry, unroll=4 if count % 4 == 0 else 2)


def kernel_call(kernel, small, arrays, outs, scratch, planes):
    return pl.pallas_call(
        kernel,
        out_shape=tuple(outs),
        in_specs=[SMEM] * len(small) + [VMEM] * len(arrays),
        out_specs=tuple([VMEM] * len(outs)),
        scratch_shapes=scratch,
        compiler_params=params(),
        cost_estimate=cost(planes),
    )(*small, *arrays)


def grouped(refs, sizes):
    found = []
    for size in sizes:
        found.append(refs[:size])
        refs = refs[size:]
    return found, list(refs)


def ranges(slab):
    half = slab // 2 - HALO
    return [(0, HALO), (HALO, half), (HALO + half, half), (slab - HALO, HALO)]


def scratch_of(count, width, length):
    return [
        pltpu.VMEM((count, width, length), jnp.float32),
        pltpu.VMEM((count + 2 * HALO, width + 2 * PAD, length), jnp.float32),
    ]


def origins(field):
    return [at for _, at in field]


def arrays_of(field):
    return [values for values, _ in field]


def prepare(first, pad, along_ref, halo, cur, slab, width):
    count = along_ref.shape[0]
    fill(pad, first - HALO, cur, width)
    if halo is not None:
        fill_halo(pad, 0 if first == 0 else HALO + count, *halo, width)
    margins(pad, HALO, count, width)
    columns(pad, along_ref, width)


def forward(place, halo, cur, old, courant, source, wave, after):
    slab, width, length = courant.shape
    first, count = place
    groups = [[halo[0]] if halo else [], arrays_of(cur), arrays_of(old)]
    groups += [[courant, source, wave], list(after)]
    sizes = [len(g) for g in groups]

    def kernel(*refs):
        (halo_ref, cur_refs, old_refs, (c_ref, source_ref, wave_ref), _), refs = grouped(refs, sizes)
        next_ref, lap_ref, along_ref, pad = refs
        coming = (halo_ref[0], *halo[1:]) if halo else None
        prepare(first, pad, along_ref, coming, list(zip(cur_refs, origins(cur))), slab, width)
        old_ref, old_at = find(list(zip(old_refs, origins(old))), first)
        amplitude = wave_ref[0:1, :]

        def body(i, _):
            center, lap = stencil(pad, HALO + i, width, along_ref[i])
            lap_ref[i] = lap
            value = 2.0 * center - old_ref[old_at + i] + c_ref[first + i] * lap
            next_ref[i] = value + source_ref[first + i] * amplitude

        march(count, body)

    outs = [f32(count, width, length)] * 2
    return kernel_call(kernel, [], sum(groups, []), outs, scratch_of(count, width, length), count)


def adjoint(place, halo, cur, old, courant, field, number, observed, after):
    slab, width, length = courant.shape
    first, count = place
    groups = [[halo[0]] if halo else [], arrays_of(cur), arrays_of(old), arrays_of(field)]
    groups += [[courant, number, observed], list(after)]
    sizes = [len(g) for g in groups]

    def kernel(*refs):
        found, refs = grouped(refs, sizes)
        next_ref, along_ref, pad = refs
        adjoint_step(place, halo, cur, old, field, found, next_ref, along_ref, pad)

    outs = [f32(count, width, length)]
    scratch = scratch_of(count, width, length)
    return kernel_call(kernel, [], sum(groups, []), outs, scratch, count)[0]


def adjoint_step(place, halo, cur, old, field, found, next_ref, along_ref, pad):
    halo_ref, cur_refs, old_refs, field_refs, (c_ref, number_ref, observed_ref) = found[:5]
    slab, width, length = c_ref.shape
    first, count = place
    coming = (halo_ref[0], *halo[1:]) if halo else None
    prepare(first, pad, along_ref, coming, list(zip(cur_refs, origins(cur))), slab, width)
    for field_ref, field_at in zip(field_refs, origins(field)):
        begin, end = max(first, field_at), min(first + count, field_at + field_ref.shape[0])
        if end <= begin:
            continue
        old_ref, old_at = find(list(zip(old_refs, origins(old))), begin)

        def body(i, _, field_ref=field_ref, field_at=field_at, begin=begin, old_ref=old_ref, old_at=old_at):
            q = begin + i
            center, lap = stencil(pad, begin - first + HALO + i, width, along_ref[begin - first + i])
            value = 2.0 * center - old_ref[old_at + i] + c_ref[q] * lap
            miss = number_ref[q] * field_ref[begin - field_at + i] - observed_ref[q]
            next_ref[begin - first + i] = value + miss

        march(end - begin, body)


def adjoint_last(
    place, halo, cur, old, courant, field, number, observed, laps, adjoints, tile, other, after
):
    slab, width, length = courant.shape
    first, count = place
    inner = count > HALO
    groups = [[halo[0]] if halo else [], arrays_of(cur), arrays_of(old), arrays_of(field)]
    groups += [[courant, number, observed], sum(laps, []), sum(adjoints, [])]
    groups += [list(tile) + list(other), list(after)]
    sizes = [len(g) for g in groups]
    steps, parts = len(laps), len(laps[0])

    def kernel(*refs):
        found, refs = grouped(refs, sizes)
        next_ref, along_ref, pad = refs[-3:]
        adjoint_step(place, halo, cur, old, field, found, next_ref, along_ref, pad)
        lap_refs, adj_refs, more = found[5:8]
        core = lax.axis_index("shot") % 2

        def product(part, i):
            value = next_ref[part * (count // parts) + i] * lap_refs[part][i]
            for n in range(1, steps):
                value = value + adj_refs[(n - 1) * parts + part][i] * lap_refs[n * parts + part][i]
            return value

        def either(write):
            @pl.when(core == 0)
            def _():
                write(refs[0], refs[1])

            @pl.when(core == 1)
            def _():
                write(refs[1], refs[0])

        if inner:
            for part in (0, 1):

                @pl.when(core == part)
                def _(part=part):
                    for i in range(count // 2):
                        refs[0][i] = product(part, i)
                        write_piece(refs[1:-3], i, product(1 - part, i))

        elif not other:
            for i in range(HALO):
                refs[0][i] = product(0, i)
        else:
            tile_ref, tiles_ref, other_ref = more

            def write(first_ref, second_ref):
                for i in range(HALO):
                    rows = slice(i * width, (i + 1) * width)
                    first_ref[rows, :] = other_ref[i]
                    second_ref[rows, :] = product(0, i)

            either(write)
            for ref in refs[:2]:
                ref[HALO * width : HALO * width + 8, :] = tile_ref[...] + tiles_ref[...]

    if inner:
        outs = [f32(count // 2, width, length)]
        outs += [f32(count // 2 // 1, width, length)] * 1
    elif not other:
        outs = [f32(count, width, length)]
    else:
        outs = [f32(HALO * width + 8, length)] * 2
    scratch = [pltpu.VMEM((count, width, length), jnp.float32)] + scratch_of(count, width, length)
    return kernel_call(kernel, [], sum(groups, []), outs, scratch, count)


def curvature(laps, message, after):
    number = len(laps)
    half, width, length = laps[0][1].shape
    size = half + HALO

    def kernel(*refs):
        ranged = [refs[n * number : (n + 1) * number] for n in range(4)]
        planes_ref = refs[4 * number]
        keep_ref, *send_refs, tile_ref, message_ref = refs[4 * number + 2 :]
        for i in range(HALO):
            message_ref[i * width : (i + 1) * width, :] = planes_ref[i]
        core = lax.axis_index("shot") % 2

        def squares(lap_refs, at):
            value = lap_refs[0][at] * lap_refs[0][at]
            for ref in lap_refs[1:]:
                value = value + ref[at] * ref[at]
            return value

        for part in (0, 1):

            @pl.when(core == part)
            def _(part=part):
                total = jnp.zeros((8, length), jnp.float32)
                own, far = (0, 1) if part == 0 else (3, 2)
                other = (3, 2) if part == 0 else (0, 1)
                for i in range(size):
                    outer = i >= half
                    value = squares(ranged[own if outer else far], i % half)
                    keep_ref[i] = value
                    total = total + fold(value)
                    value = squares(ranged[other[0] if outer else other[1]], i % half)
                    write_piece(send_refs, i, value)
                    total = total + fold(value)
                tile_ref[...] = total
                message_ref[HALO * width : HALO * width + 8, :] = total

    outs = [f32(size, width, length)]
    outs += [f32(size // 1, width, length)] * 1 + [f32(8, length), f32(HALO * width + 8, length)]
    arrays = [lap[n] for n in range(4) for lap in laps] + [message, after]
    return kernel_call(kernel, [], arrays, outs, [], 8)


def points(wavelet, source, cells, observed, slab, width, length):
    receivers = cells.shape[0]
    steps = observed.shape[0]
    area = width * length

    def kernel(wave_ref, source_ref, cell_ref, obs_ref, spot_ref, number_ref, *refs):
        row_refs, sum_refs = refs[:steps], refs[steps:]
        blank = jnp.zeros((width, length), jnp.float32)

        def clear(i, _):
            for ref in (spot_ref, number_ref) + sum_refs:
                ref[i] = blank

        march(slab, clear)
        depth = lax.axis_index("depth")
        offset = depth * (slab * area)
        odd = depth % 2
        column = lax.broadcasted_iota(jnp.int32, (1, length), 1)

        def add(local, terms):
            @pl.when((local >= 0) & (local < slab * area))
            def _():
                row, y = split(local, length)
                plane, x = split(row, width)
                q = jnp.where(odd == 1, plane, slab - 1 - plane)
                at = pl.ds(spread(x, width), 1)
                for ref, term in terms():
                    ref[q, at, :] = ref[q, at, :] + jnp.where(column == y, term, 0.0)

        add(source_ref[0] - offset, lambda: [(spot_ref, 1.0)])
        for n in range(steps):
            row_refs[n][...] = jnp.full((8, length), wave_ref[0, n], jnp.float32)

        def body(r, _):
            def terms():
                found = [(number_ref, 1.0)]
                for n in range(steps):
                    found.append((sum_refs[n], obs_ref[n, r]))
                return found

            add(cell_ref[r] - offset, terms)

        lax.fori_loop(0, receivers, body, None)

    volume = f32(slab, width, length)
    outs = [volume, volume] + [f32(8, length)] * steps + [volume] * steps
    small = [wavelet, source, cells, observed]
    found = kernel_call(kernel, small, [], outs, [], 8)
    return found[0], found[1], found[2 : 2 + steps], found[2 + steps :]


def interleaved(*arrays):
    number = len(arrays)
    slab, width, length = arrays[0].shape

    def kernel(*refs):
        odd = lax.axis_index("depth") % 2

        def body(i, _):
            plane = jnp.where(odd == 1, i, slab - 1 - i)
            for ref, out_ref in zip(refs[:number], refs[number:]):

                def put(at, value, out_ref=out_ref):
                    out_ref[i, at : at + ROWS, :] = value

                interleave(put, lambda spot, ref=ref: ref[plane, spot, :], width)

        march(slab, body)

    outs = [f32(slab, width, length)] * number
    return kernel_call(kernel, [], list(arrays), outs, [], 8)


def pack(field, adjoint_field):
    odd = lax.axis_index("depth") % 2
    far = field.shape[0] - HALO
    found = []
    for start in ((1 - odd) * far, odd * far):
        planes = [lax.dynamic_slice_in_dim(v, start, HALO, 0) for v in (field, adjoint_field)]
        found.append(jnp.concatenate(planes, axis=0))
    return found


def refresh(courant, inner_parts, outer_parts, curv, table, plan):
    slab, width, length = courant.shape
    half = inner_parts[0].shape[0]
    number = len(inner_parts)
    cells = slab * width * length * lax.axis_size("depth")

    def kernel(table_ref, plan_ref, c_ref, curv_ref, *rest):
        inner_refs = rest[:number]
        outer_refs = rest[number : 2 * number]
        out_ref = rest[2 * number]
        tail = slice(HALO * width, HALO * width + 8)
        tile = outer_refs[0][tail, :]
        for ref in outer_refs[1:]:
            tile = tile + ref[tail, :]
        level = jnp.sum(tile) / cells + 1e-06
        extra = table_ref[plan_ref[0]] * level
        core = lax.axis_index("shot") % 2
        odd = lax.axis_index("depth") % 2
        size = half + HALO

        def store(q, value):
            plane = jnp.where(odd == 1, q, size - 1 - q)
            for g in range(width // ROWS):
                spot = pl.ds(g, ROWS, stride=width // ROWS)
                out_ref[plane, spot, :] = value[g * ROWS : (g + 1) * ROWS]

        def body(i, _):
            grad = inner_refs[0][i]
            for ref in inner_refs[1:]:
                grad = grad + ref[i]
            model = c_ref[HALO + core * half + i]
            store((1 - core) * HALO + i, model - grad / (curv_ref[i] + extra))

        march(half, body)
        for i in range(HALO):
            rows = slice(i * width, (i + 1) * width)
            grad = outer_refs[0][rows, :]
            for ref in outer_refs[1:]:
                grad = grad + ref[rows, :]
            model = c_ref[core * (slab - HALO) + i]
            store(core * half + i, model - grad / (curv_ref[half + i] + extra))

    arrays = [courant, curv, *inner_parts, *outer_parts]
    outs = [f32(half + HALO, width, length)]
    return kernel_call(kernel, [table, plan], arrays, outs, [], half)[0]


def place_half(values, own, result=None):
    half, width, length = values.shape

    def kernel(values_ref, *refs):
        out_ref, sem = refs[-2:]
        core = lax.axis_index("shot") % 2
        upper = (lax.axis_index("depth") + core + 1) % 2
        place = upper if own else 1 - upper
        copy = pltpu.make_async_copy(values_ref, out_ref.at[pl.ds(place * half, half)], sem)
        copy.start()
        copy.wait()

    return pl.pallas_call(
        kernel,
        out_shape=f32(2 * half, width, length),
        in_specs=[VMEM] if own else [VMEM, HBM],
        out_specs=HBM,
        input_output_aliases={} if own else {1: 0},
        scratch_shapes=[pltpu.SemaphoreType.DMA],
        compiler_params=params(),
        cost_estimate=cost(8),
    )(*([values] if own else [values, result]))


def exchange(values, side):
    links = []
    for i in range(side, lax.axis_size("depth") - 1, 2):
        links += [(i, i + 1), (i + 1, i)]
    return lax.ppermute(values, "depth", links)


def swap(values, axis, bit):
    count = lax.axis_size(axis)
    return lax.ppermute(values, axis, [(i, i ^ bit) for i in range(count)])


def sum_of(values, pieces, after):
    size = pieces[0].shape[0]

    def kernel(values_ref, *refs):
        for i in range(values.shape[0]):
            refs[-1][i] = values_ref[i] + refs[i // size][i % size]

    arrays = [values, *pieces, *after]
    return kernel_call(kernel, [], arrays, [f32(*values.shape)], [], 8)[0]


def total_parts(keep, send, after=()):
    if isinstance(send, (list, tuple)):
        parts = [keep, [swap(piece, "shot", 1) for piece in send]]
    else:
        parts = [keep, swap(send, "shot", 1)]
    bit = 2
    while bit < lax.axis_size("shot"):
        if isinstance(parts[1], list):
            here = sum_of(*parts, after)
        else:
            here = parts[0] + parts[1]
        parts = [here, swap(here, "shot", bit)]
        bit *= 2
    return parts


def write_piece(refs, i, value):
    size = refs[0].shape[0]
    refs[i // size][i % size] = value


def on_device(
    field_prev,
    field_now,
    adjoint_next,
    adjoint_after,
    courant,
    wavelet,
    source_cell,
    receiver_cell,
    observed,
    damping_table,
    plan_step,
):
    slab, width, length = courant.shape
    halos = [exchange(v, side) for side, v in enumerate(pack(field_now[0], adjoint_next[0]))]
    places = ranges(slab)
    starts = [first for first, _ in places]
    spot, number, waves, sums = points(
        wavelet, source_cell, receiver_cell[0], observed[0], slab, width, length
    )
    start, before, courant = interleaved(field_now[0], field_prev[0], courant)
    first, second = interleaved(adjoint_next[0], adjoint_after[0])
    old, cur = [(before, 0)], [(start, 0)]
    coming = [(halos[0], 0, True), (halos[1], 0, True)]

    def ahead(step, side, halo, cur, old, after):
        return forward(
            places[side], halo, cur, old, courant, spot, waves[step], after
        )

    def back(step, side, halo, cur, old, field, after):
        return adjoint(
            places[side], halo, cur, old, courant, [field], number, sums[step], after
        )

    laps, fields = [], []
    near = ahead(0, 1, None, cur, old, ())
    far = ahead(0, 2, None, cur, old, ())
    for step in range(STEPS):
        last = step == STEPS - 1
        after = [near[0], far[0]]
        if last:
            rest, more = [(second, 0)], [(first, 0)]
            near_adj = back(step, 1, None, more, rest, (near[0], starts[1]), ())
            far_adj = back(step, 2, None, more, rest, (far[0], starts[2]), ())
            after += [near_adj, far_adj]
        one = ahead(step, 0, coming[0], cur, old, after)
        if last:
            edge = (halos[0], HALO, True)
            one_adj = back(step, 0, edge, more, rest, (one[0], starts[0]), after)
            newer = [(one_adj, starts[0]), (near_adj, starts[1]), (far_adj, starts[2])]
            near_next = back(step - 1, 1, None, newer, more, (fields[-1][1], starts[1]), ())
            two = ahead(step, 3, coming[1], cur, old, [one_adj])
            edge = (halos[1], HALO, True)
            two_adj = back(step, 3, edge, more, rest, (two[0], starts[3]), [one_adj])
            newer.append((two_adj, starts[3]))
        else:
            message = exchange(one[0], 0)
            newer = [(one[0], starts[0]), (near[0], starts[1]), (far[0], starts[2])]
            near_next = ahead(step + 1, 1, None, newer, cur, ())
            two = ahead(step, 3, coming[1], cur, old, [near_next[0]])
            newer.append((two[0], starts[3]))
        laps.append((one[1], near[1], far[1], two[1]))
        fields.append((one[0], near[0], far[0], two[0]))
        if not last:
            coming = [(message, 0, False), (exchange(two[0], 1), 0, False)]
            far = ahead(step + 1, 2, None, newer, cur, ())
            near, old, cur = near_next, cur, newer
    keep, *send, tile, message = curvature(laps, one_adj, two_adj)
    message = exchange(message, 0)
    coming = [(message, 0, False), (exchange(two_adj, 1), 0, False)]
    tiles = message[HALO * width :, :]
    bit = 2
    old, cur, near = more, newer, near_next
    adjoints = [arrays_of(cur)]
    for step in range(STEPS - 2, 0, -1):
        far = back(step, 2, None, cur, old, (fields[step][2], starts[2]), ())
        after = [near, far]
        one = back(step, 0, coming[0], cur, old, (fields[step][0], starts[0]), after)
        message = exchange(one, 0)
        newer = [(one, starts[0]), (near, starts[1]), (far, starts[2])]
        if step > 1:
            near_next = back(step - 1, 1, None, newer, cur, (fields[step - 1][1], starts[1]), ())
            after = [near_next, tiles]
        else:
            after = [one, tiles]
        two = back(step, 3, coming[1], cur, old, (fields[step][3], starts[3]), after)
        newer.append((two, starts[3]))
        coming = [(message, 0, False), (exchange(two, 1), 0, False)]
        near, old, cur = near_next, cur, newer
        adjoints.insert(0, arrays_of(cur))
        if step == STEPS - 2:
            curv = sum(total_parts(keep, send, [two]))
        if bit < lax.axis_size("depth"):
            tile = tile + tiles
            tiles = swap(tile, "depth", bit)
            bit *= 2
    while bit < lax.axis_size("depth"):
        tile = tile + tiles
        tiles = swap(tile, "depth", bit)
        bit *= 2
    pieces = [(values, at) for values, at in zip(fields[0], starts)]
    inner = (starts[1], 2 * places[1][1])

    def finish(place, halo, sides, both, other, after):
        return adjoint_last(
            place, halo, cur, old, courant, [pieces[n] for n in sides], number, sums[0],
            [[lap[n] for n in sides] for lap in laps],
            [[a[n] for n in sides] for a in adjoints], both, other, after,
        )

    inside = finish(inner, None, (1, 2), [], [], [])
    one = finish(places[0], coming[0], (0,), [], [], inside[:1])
    outside = finish(places[3], coming[1], (3,), [tile, tiles], one, [curv])
    inner_parts = total_parts(inside[0], inside[1:])
    outer_parts = total_parts(*outside)
    own = refresh(courant, inner_parts, outer_parts, curv, damping_table, plan_step)
    other = swap(own, "shot", 1)
    return place_half(other, False, place_half(own, True))


def solution(mesh):
    in_specs = (
        P("shot", "depth", None, None),
        P("shot", "depth", None, None),
        P("shot", "depth", None, None),
        P("shot", "depth", None, None),
        P("depth", None, None),
        P("shot", None),
        P("shot"),
        P("shot", None),
        P("shot", None, None),
        P(),
        P(),
    )
    out_specs = P("depth", None, None)
    return jax.shard_map(
        on_device, mesh=mesh, in_specs=in_specs, out_specs=out_specs, check_vma=False
    )
```

```python
import jax
import jax.numpy as jnp
from jax import lax
from jax.experimental import pallas as pl
from jax.experimental.pallas import tpu as pltpu
from jax.sharding import PartitionSpec as P

STEPS = 4
HALO = 4
ROWS = 8
PAD = HALO * ROWS

coeffs = (-205.0 / 72.0, 8.0 / 5.0, -1.0 / 5.0, 8.0 / 315.0, -1.0 / 560.0)

VMEM = pl.BlockSpec(memory_space=pltpu.VMEM)
SMEM = pl.BlockSpec(memory_space=pltpu.SMEM)
HBM = pl.BlockSpec(memory_space=pltpu.HBM)


def f32(*shape):
    return jax.ShapeDtypeStruct(shape, jnp.float32)


def params():
    return pltpu.CompilerParams(vmem_limit_bytes=6 * 2**20)


def cost(planes):
    return pl.CostEstimate(
        flops=planes * 10**4, bytes_accessed=planes * 2**10, transcendentals=0
    )


def split(value, size):
    if size & (size - 1) == 0:
        return value >> (size.bit_length() - 1), value & (size - 1)
    return value // size, value % size


def spread(x, width):
    s, g = split(x, width // ROWS)
    return g * ROWS + s


def interleave(put, get, width):
    for g in range(width // ROWS):
        put(g * ROWS, get(pl.ds(g, ROWS, stride=width // ROWS)))


def margins(pad, first, count, width):
    length = pad.shape[2]
    place = lax.broadcasted_iota(jnp.int32, (ROWS, length), 0)

    def body(i, _):
        p = first + i
        for j in range(HALO):
            at = j * ROWS
            low = pltpu.roll(pad[p, width + at : width + at + ROWS, :], 1, 0)
            pad[p, at : at + ROWS, :] = jnp.where(place == 0, 0.0, low)
            top = pltpu.roll(pad[p, PAD + at : PAD + at + ROWS, :], ROWS - 1, 0)
            beyond = PAD + width + at
            pad[p, beyond : beyond + ROWS, :] = jnp.where(place == ROWS - 1, 0.0, top)

    march(count, body)


def fill(pad, base, pieces, width):
    top = base + pad.shape[0]
    for ref, origin in pieces:
        begin = max(base, origin)
        end = min(top, origin + ref.shape[0])
        if end > begin:
            pad[begin - base : end - base, PAD : PAD + width, :] = ref[begin - origin : end - origin]


def fill_halo(pad, at, ref, ref_at, natural, width):
    odd = lax.axis_index("depth") % 2
    for i in range(HALO):
        if natural:

            def put(row, value, i=i):
                pad[at + i, PAD + row : PAD + row + ROWS, :] = value

            source = ref_at + jnp.where(odd == 1, i, HALO - 1 - i)
            interleave(put, lambda spot, source=source: ref[source, spot, :], width)
        elif len(ref.shape) == 2:
            rows = slice((HALO - 1 - i) * width, (HALO - i) * width)
            pad[at + i, PAD : PAD + width, :] = ref[rows, :]
        else:
            pad[at + i, PAD : PAD + width, :] = ref[HALO - 1 - i]


def find(pieces, plane):
    for ref, origin in pieces:
        if origin <= plane < origin + ref.shape[0]:
            return ref, plane - origin


def columns(pad, along_ref, width):
    planes, _, length = along_ref.shape
    apart = lax.broadcasted_iota(jnp.int32, (length, length), 0)
    apart = jnp.abs(apart - lax.broadcasted_iota(jnp.int32, (length, length), 1))
    band = jnp.where(apart == 0, 3.0 * coeffs[0], 0.0)
    for k in range(1, 5):
        band = jnp.where(apart == k, coeffs[k], band)
    size = HALO if planes % (2 * HALO) else 2 * HALO
    for begin in range(0, planes, size):
        block = pad[HALO + begin : HALO + begin + size, PAD : PAD + width, :]
        product = jnp.dot(
            block.reshape(size * width, length),
            band,
            precision=lax.Precision.HIGHEST,
            preferred_element_type=jnp.float32,
        )
        along_ref[begin : begin + size] = product.reshape(size, width, length)


def stencil(pad, p, width, result):
    rows = slice(PAD, PAD + width)
    plane = pad[p]
    for k in range(1, 5):
        along = pad[p + k, rows, :] + pad[p - k, rows, :]
        along = along + plane[PAD + k * ROWS : PAD + k * ROWS + width]
        along = along + plane[PAD - k * ROWS : PAD - k * ROWS + width]
        result = result + coeffs[k] * along
    return plane[rows], result


def fold(values):
    width, length = values.shape
    return jnp.sum(values.reshape(width // 8, 8, length), axis=0)


def march(count, body, carry=None):
    return lax.fori_loop(0, count, body, carry, unroll=4 if count % 4 == 0 else 2)


def kernel_call(kernel, small, arrays, outs, scratch, planes):
    return pl.pallas_call(
        kernel,
        out_shape=tuple(outs),
        in_specs=[SMEM] * len(small) + [VMEM] * len(arrays),
        out_specs=tuple([VMEM] * len(outs)),
        scratch_shapes=scratch,
        compiler_params=params(),
        cost_estimate=cost(planes),
    )(*small, *arrays)


def grouped(refs, sizes):
    found = []
    for size in sizes:
        found.append(refs[:size])
        refs = refs[size:]
    return found, list(refs)


def ranges(slab):
    half = slab // 2 - HALO
    return [(0, HALO), (HALO, half), (HALO + half, half), (slab - HALO, HALO)]


def scratch_of(count, width, length):
    return [
        pltpu.VMEM((count, width, length), jnp.float32),
        pltpu.VMEM((count + 2 * HALO, width + 2 * PAD, length), jnp.float32),
    ]


def origins(field):
    return [at for _, at in field]


def arrays_of(field):
    return [values for values, _ in field]


def prepare(first, pad, along_ref, halo, cur, slab, width):
    count = along_ref.shape[0]
    fill(pad, first - HALO, cur, width)
    if halo is not None:
        fill_halo(pad, 0 if first == 0 else HALO + count, *halo, width)
    margins(pad, HALO, count, width)
    columns(pad, along_ref, width)


def forward(place, halo, cur, old, courant, source, wave, after):
    slab, width, length = courant.shape
    first, count = place
    groups = [[halo[0]] if halo else [], arrays_of(cur), arrays_of(old)]
    groups += [[courant, source, wave], list(after)]
    sizes = [len(g) for g in groups]

    def kernel(*refs):
        (halo_ref, cur_refs, old_refs, (c_ref, source_ref, wave_ref), _), refs = grouped(refs, sizes)
        next_ref, lap_ref, along_ref, pad = refs
        coming = (halo_ref[0], *halo[1:]) if halo else None
        prepare(first, pad, along_ref, coming, list(zip(cur_refs, origins(cur))), slab, width)
        old_ref, old_at = find(list(zip(old_refs, origins(old))), first)
        amplitude = wave_ref[0:1, :]

        def body(i, _):
            center, lap = stencil(pad, HALO + i, width, along_ref[i])
            lap_ref[i] = lap
            value = 2.0 * center - old_ref[old_at + i] + c_ref[first + i] * lap
            next_ref[i] = value + source_ref[first + i] * amplitude

        march(count, body)

    outs = [f32(count, width, length)] * 2
    return kernel_call(kernel, [], sum(groups, []), outs, scratch_of(count, width, length), count)


def adjoint(place, halo, cur, old, courant, field, number, observed, after):
    slab, width, length = courant.shape
    first, count = place
    groups = [[halo[0]] if halo else [], arrays_of(cur), arrays_of(old), arrays_of(field)]
    groups += [[courant, number, observed], list(after)]
    sizes = [len(g) for g in groups]

    def kernel(*refs):
        found, refs = grouped(refs, sizes)
        next_ref, along_ref, pad = refs
        adjoint_step(place, halo, cur, old, field, found, next_ref, along_ref, pad)

    outs = [f32(count, width, length)]
    scratch = scratch_of(count, width, length)
    return kernel_call(kernel, [], sum(groups, []), outs, scratch, count)[0]


def adjoint_step(place, halo, cur, old, field, found, next_ref, along_ref, pad):
    halo_ref, cur_refs, old_refs, field_refs, (c_ref, number_ref, observed_ref) = found[:5]
    slab, width, length = c_ref.shape
    first, count = place
    coming = (halo_ref[0], *halo[1:]) if halo else None
    prepare(first, pad, along_ref, coming, list(zip(cur_refs, origins(cur))), slab, width)
    for field_ref, field_at in zip(field_refs, origins(field)):
        begin, end = max(first, field_at), min(first + count, field_at + field_ref.shape[0])
        if end <= begin:
            continue
        old_ref, old_at = find(list(zip(old_refs, origins(old))), begin)

        def body(i, _, field_ref=field_ref, field_at=field_at, begin=begin, old_ref=old_ref, old_at=old_at):
            q = begin + i
            center, lap = stencil(pad, begin - first + HALO + i, width, along_ref[begin - first + i])
            value = 2.0 * center - old_ref[old_at + i] + c_ref[q] * lap
            miss = number_ref[q] * field_ref[begin - field_at + i] - observed_ref[q]
            next_ref[begin - first + i] = value + miss

        march(end - begin, body)


def adjoint_last(
    place, halo, cur, old, courant, field, number, observed, laps, adjoints, tile, other, after
):
    slab, width, length = courant.shape
    first, count = place
    inner = count > HALO
    groups = [[halo[0]] if halo else [], arrays_of(cur), arrays_of(old), arrays_of(field)]
    groups += [[courant, number, observed], sum(laps, []), sum(adjoints, [])]
    groups += [list(tile) + list(other), list(after)]
    sizes = [len(g) for g in groups]
    steps, parts = len(laps), len(laps[0])

    def kernel(*refs):
        found, refs = grouped(refs, sizes)
        next_ref, along_ref, pad = refs[-3:]
        adjoint_step(place, halo, cur, old, field, found, next_ref, along_ref, pad)
        lap_refs, adj_refs, more = found[5:8]
        core = lax.axis_index("shot") % 2

        def product(part, i):
            value = next_ref[part * (count // parts) + i] * lap_refs[part][i]
            for n in range(1, steps):
                value = value + adj_refs[(n - 1) * parts + part][i] * lap_refs[n * parts + part][i]
            return value

        def either(write):
            @pl.when(core == 0)
            def _():
                write(refs[0], refs[1])

            @pl.when(core == 1)
            def _():
                write(refs[1], refs[0])

        if inner:
            for part in (0, 1):

                @pl.when(core == part)
                def _(part=part):
                    for i in range(count // 2):
                        refs[0][i] = product(part, i)
                        write_piece(refs[1:-3], i, product(1 - part, i))

        elif not other:
            for i in range(HALO):
                refs[0][i] = product(0, i)
        else:
            tile_ref, tiles_ref, other_ref = more

            def write(first_ref, second_ref):
                for i in range(HALO):
                    rows = slice(i * width, (i + 1) * width)
                    first_ref[rows, :] = other_ref[i]
                    second_ref[rows, :] = product(0, i)

            either(write)
            for ref in refs[:2]:
                ref[HALO * width : HALO * width + 8, :] = tile_ref[...] + tiles_ref[...]

    if inner:
        outs = [f32(count // 2, width, length)]
        outs += [f32(count // 2 // 1, width, length)] * 1
    elif not other:
        outs = [f32(count, width, length)]
    else:
        outs = [f32(HALO * width + 8, length)] * 2
    scratch = [pltpu.VMEM((count, width, length), jnp.float32)] + scratch_of(count, width, length)
    return kernel_call(kernel, [], sum(groups, []), outs, scratch, count)


def curvature(laps, message, after):
    number = len(laps)
    half, width, length = laps[0][1].shape
    size = half + HALO

    def kernel(*refs):
        ranged = [refs[n * number : (n + 1) * number] for n in range(4)]
        planes_ref = refs[4 * number]
        keep_ref, *send_refs, tile_ref, message_ref = refs[4 * number + 2 :]
        for i in range(HALO):
            message_ref[i * width : (i + 1) * width, :] = planes_ref[i]
        core = lax.axis_index("shot") % 2

        def squares(lap_refs, at):
            value = lap_refs[0][at] * lap_refs[0][at]
            for ref in lap_refs[1:]:
                value = value + ref[at] * ref[at]
            return value

        for part in (0, 1):

            @pl.when(core == part)
            def _(part=part):
                total = jnp.zeros((8, length), jnp.float32)
                own, far = (0, 1) if part == 0 else (3, 2)
                other = (3, 2) if part == 0 else (0, 1)
                for i in range(size):
                    outer = i >= half
                    value = squares(ranged[own if outer else far], i % half)
                    keep_ref[i] = value
                    total = total + fold(value)
                    value = squares(ranged[other[0] if outer else other[1]], i % half)
                    write_piece(send_refs, i, value)
                    total = total + fold(value)
                tile_ref[...] = total
                message_ref[HALO * width : HALO * width + 8, :] = total

    outs = [f32(size, width, length)]
    outs += [f32(size // 1, width, length)] * 1 + [f32(8, length), f32(HALO * width + 8, length)]
    arrays = [lap[n] for n in range(4) for lap in laps] + [message, after]
    return kernel_call(kernel, [], arrays, outs, [], 8)


def points(wavelet, source, cells, observed, slab, width, length):
    receivers = cells.shape[0]
    steps = observed.shape[0]
    area = width * length

    def kernel(wave_ref, source_ref, cell_ref, obs_ref, spot_ref, number_ref, *refs):
        row_refs, sum_refs = refs[:steps], refs[steps:]
        blank = jnp.zeros((width, length), jnp.float32)

        def clear(i, _):
            for ref in (spot_ref, number_ref) + sum_refs:
                ref[i] = blank

        march(slab, clear)
        depth = lax.axis_index("depth")
        offset = depth * (slab * area)
        odd = depth % 2
        column = lax.broadcasted_iota(jnp.int32, (1, length), 1)

        def add(local, terms):
            @pl.when((local >= 0) & (local < slab * area))
            def _():
                row, y = split(local, length)
                plane, x = split(row, width)
                q = jnp.where(odd == 1, plane, slab - 1 - plane)
                at = pl.ds(spread(x, width), 1)
                for ref, term in terms():
                    ref[q, at, :] = ref[q, at, :] + jnp.where(column == y, term, 0.0)

        add(source_ref[0] - offset, lambda: [(spot_ref, 1.0)])
        for n in range(steps):
            row_refs[n][...] = jnp.full((8, length), wave_ref[0, n], jnp.float32)

        def body(r, _):
            def terms():
                found = [(number_ref, 1.0)]
                for n in range(steps):
                    found.append((sum_refs[n], obs_ref[n, r]))
                return found

            add(cell_ref[r] - offset, terms)

        lax.fori_loop(0, receivers, body, None)

    volume = f32(slab, width, length)
    outs = [volume, volume] + [f32(8, length)] * steps + [volume] * steps
    small = [wavelet, source, cells, observed]
    found = kernel_call(kernel, small, [], outs, [], 8)
    return found[0], found[1], found[2 : 2 + steps], found[2 + steps :]


def interleaved(*arrays):
    number = len(arrays)
    slab, width, length = arrays[0].shape

    def kernel(*refs):
        odd = lax.axis_index("depth") % 2

        def body(i, _):
            plane = jnp.where(odd == 1, i, slab - 1 - i)
            for ref, out_ref in zip(refs[:number], refs[number:]):

                def put(at, value, out_ref=out_ref):
                    out_ref[i, at : at + ROWS, :] = value

                interleave(put, lambda spot, ref=ref: ref[plane, spot, :], width)

        march(slab, body)

    outs = [f32(slab, width, length)] * number
    return kernel_call(kernel, [], list(arrays), outs, [], 8)


def pack(field, adjoint_field):
    odd = lax.axis_index("depth") % 2
    far = field.shape[0] - HALO
    found = []
    for start in ((1 - odd) * far, odd * far):
        planes = [lax.dynamic_slice_in_dim(v, start, HALO, 0) for v in (field, adjoint_field)]
        found.append(jnp.concatenate(planes, axis=0))
    return found


def refresh(courant, inner_parts, outer_parts, curv, table, plan):
    slab, width, length = courant.shape
    half = inner_parts[0].shape[0]
    number = len(inner_parts)
    cells = slab * width * length * lax.axis_size("depth")

    def kernel(table_ref, plan_ref, c_ref, curv_ref, *rest):
        inner_refs = rest[:number]
        outer_refs = rest[number : 2 * number]
        out_ref = rest[2 * number]
        tail = slice(HALO * width, HALO * width + 8)
        tile = outer_refs[0][tail, :]
        for ref in outer_refs[1:]:
            tile = tile + ref[tail, :]
        level = jnp.sum(tile) / cells + 1e-06
        extra = table_ref[plan_ref[0]] * level
        core = lax.axis_index("shot") % 2
        odd = lax.axis_index("depth") % 2
        size = half + HALO

        def store(q, value):
            plane = jnp.where(odd == 1, q, size - 1 - q)
            for g in range(width // ROWS):
                spot = pl.ds(g, ROWS, stride=width // ROWS)
                out_ref[plane, spot, :] = value[g * ROWS : (g + 1) * ROWS]

        def body(i, _):
            grad = inner_refs[0][i]
            for ref in inner_refs[1:]:
                grad = grad + ref[i]
            model = c_ref[HALO + core * half + i]
            store((1 - core) * HALO + i, model - grad / (curv_ref[i] + extra))

        march(half, body)
        for i in range(HALO):
            rows = slice(i * width, (i + 1) * width)
            grad = outer_refs[0][rows, :]
            for ref in outer_refs[1:]:
                grad = grad + ref[rows, :]
            model = c_ref[core * (slab - HALO) + i]
            store(core * half + i, model - grad / (curv_ref[half + i] + extra))

    arrays = [courant, curv, *inner_parts, *outer_parts]
    outs = [f32(half + HALO, width, length)]
    return kernel_call(kernel, [table, plan], arrays, outs, [], half)[0]


def place_half(values, own, result=None):
    half, width, length = values.shape

    def kernel(values_ref, *refs):
        out_ref, sem = refs[-2:]
        core = lax.axis_index("shot") % 2
        upper = (lax.axis_index("depth") + core + 1) % 2
        place = upper if own else 1 - upper
        copy = pltpu.make_async_copy(values_ref, out_ref.at[pl.ds(place * half, half)], sem)
        copy.start()
        copy.wait()

    return pl.pallas_call(
        kernel,
        out_shape=f32(2 * half, width, length),
        in_specs=[VMEM] if own else [VMEM, HBM],
        out_specs=HBM,
        input_output_aliases={} if own else {1: 0},
        scratch_shapes=[pltpu.SemaphoreType.DMA],
        compiler_params=params(),
        cost_estimate=cost(8),
    )(*([values] if own else [values, result]))


def exchange(values, side):
    links = []
    for i in range(side, lax.axis_size("depth") - 1, 2):
        links += [(i, i + 1), (i + 1, i)]
    return lax.ppermute(values, "depth", links)


def swap(values, axis, bit):
    count = lax.axis_size(axis)
    return lax.ppermute(values, axis, [(i, i ^ bit) for i in range(count)])


def sum_of(values, pieces, after):
    size = pieces[0].shape[0]

    def kernel(values_ref, *refs):
        for i in range(values.shape[0]):
            refs[-1][i] = values_ref[i] + refs[i // size][i % size]

    arrays = [values, *pieces, *after]
    return kernel_call(kernel, [], arrays, [f32(*values.shape)], [], 8)[0]


def total_parts(keep, send, after=()):
    if isinstance(send, (list, tuple)):
        parts = [keep, [swap(piece, "shot", 1) for piece in send]]
    else:
        parts = [keep, swap(send, "shot", 1)]
    bit = 2
    while bit < lax.axis_size("shot"):
        if isinstance(parts[1], list):
            here = sum_of(*parts, after)
        else:
            here = parts[0] + parts[1]
        parts = [here, swap(here, "shot", bit)]
        bit *= 2
    return parts


def write_piece(refs, i, value):
    size = refs[0].shape[0]
    refs[i // size][i % size] = value


def on_device(
    field_prev,
    field_now,
    adjoint_next,
    adjoint_after,
    courant,
    wavelet,
    source_cell,
    receiver_cell,
    observed,
    damping_table,
    plan_step,
):
    slab, width, length = courant.shape
    halos = [exchange(v, side) for side, v in enumerate(pack(field_now[0], adjoint_next[0]))]
    places = ranges(slab)
    starts = [first for first, _ in places]
    spot, number, waves, sums = points(
        wavelet, source_cell, receiver_cell[0], observed[0], slab, width, length
    )
    start, before, courant = interleaved(field_now[0], field_prev[0], courant)
    first, second = interleaved(adjoint_next[0], adjoint_after[0])
    old, cur = [(before, 0)], [(start, 0)]
    coming = [(halos[0], 0, True), (halos[1], 0, True)]

    def ahead(step, side, halo, cur, old, after):
        return forward(
            places[side], halo, cur, old, courant, spot, waves[step], after
        )

    def back(step, side, halo, cur, old, field, after):
        return adjoint(
            places[side], halo, cur, old, courant, [field], number, sums[step], after
        )

    laps, fields = [], []
    near = ahead(0, 1, None, cur, old, ())
    far = ahead(0, 2, None, cur, old, ())
    for step in range(STEPS):
        last = step == STEPS - 1
        after = [near[0], far[0]]
        if last:
            rest, more = [(second, 0)], [(first, 0)]
            near_adj = back(step, 1, None, more, rest, (near[0], starts[1]), ())
            far_adj = back(step, 2, None, more, rest, (far[0], starts[2]), ())
            after += [near_adj, far_adj]
        one = ahead(step, 0, coming[0], cur, old, after)
        if last:
            edge = (halos[0], HALO, True)
            one_adj = back(step, 0, edge, more, rest, (one[0], starts[0]), after)
            newer = [(one_adj, starts[0]), (near_adj, starts[1]), (far_adj, starts[2])]
            near_next = back(step - 1, 1, None, newer, more, (fields[-1][1], starts[1]), ())
            two = ahead(step, 3, coming[1], cur, old, [near_next])
            edge = (halos[1], HALO, True)
            two_adj = back(step, 3, edge, more, rest, (two[0], starts[3]), [near_next])
            newer.append((two_adj, starts[3]))
        else:
            message = exchange(one[0], 0)
            newer = [(one[0], starts[0]), (near[0], starts[1]), (far[0], starts[2])]
            near_next = ahead(step + 1, 1, None, newer, cur, ())
            two = ahead(step, 3, coming[1], cur, old, [near_next[0]])
            newer.append((two[0], starts[3]))
        laps.append((one[1], near[1], far[1], two[1]))
        fields.append((one[0], near[0], far[0], two[0]))
        if not last:
            coming = [(message, 0, False), (exchange(two[0], 1), 0, False)]
            far = ahead(step + 1, 2, None, newer, cur, ())
            near, old, cur = near_next, cur, newer
    keep, *send, tile, message = curvature(laps, one_adj, two_adj)
    message = exchange(message, 0)
    coming = [(message, 0, False), (exchange(two_adj, 1), 0, False)]
    tiles = message[HALO * width :, :]
    bit = 2
    old, cur, near = more, newer, near_next
    adjoints = [arrays_of(cur)]
    for step in range(STEPS - 2, 0, -1):
        behind = [tiles] if step == STEPS - 2 else ()
        far = back(step, 2, None, cur, old, (fields[step][2], starts[2]), behind)
        if step == STEPS - 2:
            curv = sum(total_parts(keep, send, [far]))
        after = [near, far]
        one = back(step, 0, coming[0], cur, old, (fields[step][0], starts[0]), after)
        message = exchange(one, 0)
        newer = [(one, starts[0]), (near, starts[1]), (far, starts[2])]
        if step > 1:
            near_next = back(step - 1, 1, None, newer, cur, (fields[step - 1][1], starts[1]), ())
            after = [near_next, tiles]
        else:
            after = [one, tiles]
        two = back(step, 3, coming[1], cur, old, (fields[step][3], starts[3]), after)
        newer.append((two, starts[3]))
        coming = [(message, 0, False), (exchange(two, 1), 0, False)]
        near, old, cur = near_next, cur, newer
        adjoints.insert(0, arrays_of(cur))
        if bit < lax.axis_size("depth"):
            tile = tile + tiles
            tiles = swap(tile, "depth", bit)
            bit *= 2
    while bit < lax.axis_size("depth"):
        tile = tile + tiles
        tiles = swap(tile, "depth", bit)
        bit *= 2
    pieces = [(values, at) for values, at in zip(fields[0], starts)]
    inner = (starts[1], 2 * places[1][1])

    def finish(place, halo, sides, both, other, after):
        return adjoint_last(
            place, halo, cur, old, courant, [pieces[n] for n in sides], number, sums[0],
            [[lap[n] for n in sides] for lap in laps],
            [[a[n] for n in sides] for a in adjoints], both, other, after,
        )

    inside = finish(inner, None, (1, 2), [], [], [])
    one = finish(places[0], coming[0], (0,), [], [], inside[:1])
    outside = finish(places[3], coming[1], (3,), [tile, tiles], one, [curv])
    inner_parts = total_parts(inside[0], inside[1:])
    outer_parts = total_parts(*outside)
    own = refresh(courant, inner_parts, outer_parts, curv, damping_table, plan_step)
    other = swap(own, "shot", 1)
    return place_half(other, False, place_half(own, True))


def solution(mesh):
    in_specs = (
        P("shot", "depth", None, None),
        P("shot", "depth", None, None),
        P("shot", "depth", None, None),
        P("shot", "depth", None, None),
        P("depth", None, None),
        P("shot", None),
        P("shot"),
        P("shot", None),
        P("shot", None, None),
        P(),
        P(),
    )
    out_specs = P("depth", None, None)
    return jax.shard_map(
        on_device, mesh=mesh, in_specs=in_specs, out_specs=out_specs, check_vma=False
    )
```

```python
import jax
import jax.numpy as jnp
from jax import lax
from jax.experimental import pallas as pl
from jax.experimental.pallas import tpu as pltpu
from jax.sharding import PartitionSpec as P

STEPS = 4
HALO = 4
ROWS = 8
PAD = HALO * ROWS

coeffs = (-205.0 / 72.0, 8.0 / 5.0, -1.0 / 5.0, 8.0 / 315.0, -1.0 / 560.0)

VMEM = pl.BlockSpec(memory_space=pltpu.VMEM)
SMEM = pl.BlockSpec(memory_space=pltpu.SMEM)
HBM = pl.BlockSpec(memory_space=pltpu.HBM)


def f32(*shape):
    return jax.ShapeDtypeStruct(shape, jnp.float32)


def params():
    return pltpu.CompilerParams(vmem_limit_bytes=6 * 2**20)


def cost(planes):
    return pl.CostEstimate(
        flops=planes * 10**4, bytes_accessed=planes * 2**10, transcendentals=0
    )


def split(value, size):
    if size & (size - 1) == 0:
        return value >> (size.bit_length() - 1), value & (size - 1)
    return value // size, value % size


def spread(x, width):
    s, g = split(x, width // ROWS)
    return g * ROWS + s


def interleave(put, get, width):
    for g in range(width // ROWS):
        put(g * ROWS, get(pl.ds(g, ROWS, stride=width // ROWS)))


def margins(pad, first, count, width):
    length = pad.shape[2]
    place = lax.broadcasted_iota(jnp.int32, (ROWS, length), 0)

    def body(i, _):
        p = first + i
        for j in range(HALO):
            at = j * ROWS
            low = pltpu.roll(pad[p, width + at : width + at + ROWS, :], 1, 0)
            pad[p, at : at + ROWS, :] = jnp.where(place == 0, 0.0, low)
            top = pltpu.roll(pad[p, PAD + at : PAD + at + ROWS, :], ROWS - 1, 0)
            beyond = PAD + width + at
            pad[p, beyond : beyond + ROWS, :] = jnp.where(place == ROWS - 1, 0.0, top)

    march(count, body)


def fill(pad, base, pieces, width):
    top = base + pad.shape[0]
    for ref, origin in pieces:
        begin = max(base, origin)
        end = min(top, origin + ref.shape[0])
        if end > begin:
            pad[begin - base : end - base, PAD : PAD + width, :] = ref[begin - origin : end - origin]


def fill_halo(pad, at, ref, ref_at, natural, width):
    odd = lax.axis_index("depth") % 2
    for i in range(HALO):
        if natural:

            def put(row, value, i=i):
                pad[at + i, PAD + row : PAD + row + ROWS, :] = value

            source = ref_at + jnp.where(odd == 1, i, HALO - 1 - i)
            interleave(put, lambda spot, source=source: ref[source, spot, :], width)
        else:
            pad[at + i, PAD : PAD + width, :] = ref[HALO - 1 - i]


def find(pieces, plane):
    for ref, origin in pieces:
        if origin <= plane < origin + ref.shape[0]:
            return ref, plane - origin


def columns(pad, along_ref, width):
    planes, _, length = along_ref.shape
    apart = lax.broadcasted_iota(jnp.int32, (length, length), 0)
    apart = jnp.abs(apart - lax.broadcasted_iota(jnp.int32, (length, length), 1))
    band = jnp.where(apart == 0, 3.0 * coeffs[0], 0.0)
    for k in range(1, 5):
        band = jnp.where(apart == k, coeffs[k], band)
    size = HALO if planes % (2 * HALO) else 2 * HALO
    for begin in range(0, planes, size):
        block = pad[HALO + begin : HALO + begin + size, PAD : PAD + width, :]
        product = jnp.dot(
            block.reshape(size * width, length),
            band,
            precision=lax.Precision.HIGHEST,
            preferred_element_type=jnp.float32,
        )
        along_ref[begin : begin + size] = product.reshape(size, width, length)


def stencil(pad, p, width, result):
    rows = slice(PAD, PAD + width)
    plane = pad[p]
    for k in range(1, 5):
        along = pad[p + k, rows, :] + pad[p - k, rows, :]
        along = along + plane[PAD + k * ROWS : PAD + k * ROWS + width]
        along = along + plane[PAD - k * ROWS : PAD - k * ROWS + width]
        result = result + coeffs[k] * along
    return plane[rows], result


def fold(values):
    width, length = values.shape
    return jnp.sum(values.reshape(width // 8, 8, length), axis=0)


def march(count, body, carry=None):
    return lax.fori_loop(0, count, body, carry, unroll=4 if count % 4 == 0 else 2)


def kernel_call(kernel, small, arrays, outs, scratch, planes):
    return pl.pallas_call(
        kernel,
        out_shape=tuple(outs),
        in_specs=[SMEM] * len(small) + [VMEM] * len(arrays),
        out_specs=tuple([VMEM] * len(outs)),
        scratch_shapes=scratch,
        compiler_params=params(),
        cost_estimate=cost(planes),
    )(*small, *arrays)


def grouped(refs, sizes):
    found = []
    for size in sizes:
        found.append(refs[:size])
        refs = refs[size:]
    return found, list(refs)


def ranges(slab):
    half = slab // 2 - HALO
    return [(0, HALO), (HALO, half), (HALO + half, half), (slab - HALO, HALO)]


def scratch_of(count, width, length):
    return [
        pltpu.VMEM((count, width, length), jnp.float32),
        pltpu.VMEM((count + 2 * HALO, width + 2 * PAD, length), jnp.float32),
    ]


def origins(field):
    return [at for _, at in field]


def arrays_of(field):
    return [values for values, _ in field]


def prepare(first, pad, along_ref, halo, cur, slab, width):
    count = along_ref.shape[0]
    fill(pad, first - HALO, cur, width)
    if halo is not None:
        fill_halo(pad, 0 if first == 0 else HALO + count, *halo, width)
    margins(pad, HALO, count, width)
    columns(pad, along_ref, width)


def forward(place, halo, cur, old, courant, source, wave, after):
    slab, width, length = courant.shape
    first, count = place
    groups = [[halo[0]] if halo else [], arrays_of(cur), arrays_of(old)]
    groups += [[courant, source, wave], list(after)]
    sizes = [len(g) for g in groups]

    def kernel(*refs):
        (halo_ref, cur_refs, old_refs, (c_ref, source_ref, wave_ref), _), refs = grouped(refs, sizes)
        next_ref, lap_ref, along_ref, pad = refs
        coming = (halo_ref[0], *halo[1:]) if halo else None
        prepare(first, pad, along_ref, coming, list(zip(cur_refs, origins(cur))), slab, width)
        old_ref, old_at = find(list(zip(old_refs, origins(old))), first)
        amplitude = wave_ref[0:1, :]

        def body(i, _):
            center, lap = stencil(pad, HALO + i, width, along_ref[i])
            lap_ref[i] = lap
            value = 2.0 * center - old_ref[old_at + i] + c_ref[first + i] * lap
            next_ref[i] = value + source_ref[first + i] * amplitude

        march(count, body)

    outs = [f32(count, width, length)] * 2
    return kernel_call(kernel, [], sum(groups, []), outs, scratch_of(count, width, length), count)


def adjoint(place, halo, cur, old, courant, field, number, observed, after):
    slab, width, length = courant.shape
    first, count = place
    groups = [[halo[0]] if halo else [], arrays_of(cur), arrays_of(old), arrays_of(field)]
    groups += [[courant, number, observed], list(after)]
    sizes = [len(g) for g in groups]

    def kernel(*refs):
        found, refs = grouped(refs, sizes)
        next_ref, along_ref, pad = refs
        adjoint_step(place, halo, cur, old, field, found, next_ref, along_ref, pad)

    outs = [f32(count, width, length)]
    scratch = scratch_of(count, width, length)
    return kernel_call(kernel, [], sum(groups, []), outs, scratch, count)[0]


def adjoint_base(place, cur, old, courant):
    slab, width, length = courant.shape
    first, count = place
    groups = [arrays_of(cur), arrays_of(old), [courant]]
    sizes = [len(g) for g in groups]

    def kernel(*refs):
        (cur_refs, old_refs, (c_ref,)), refs = grouped(refs, sizes)
        next_ref, along_ref, pad = refs
        prepare(first, pad, along_ref, None, list(zip(cur_refs, origins(cur))), slab, width)
        old_ref, old_at = find(list(zip(old_refs, origins(old))), first)

        def body(i, _):
            center, lap = stencil(pad, HALO + i, width, along_ref[i])
            next_ref[i] = 2.0 * center - old_ref[old_at + i] + c_ref[first + i] * lap

        march(count, body)

    outs = [f32(count, width, length)]
    scratch = scratch_of(count, width, length)
    return kernel_call(kernel, [], sum(groups, []), outs, scratch, count)[0]


def with_points(bases, firsts, fields, number, observed):
    many = len(bases)

    def kernel(*refs):
        base_refs, field_refs = refs[:many], refs[many : 2 * many]
        number_ref, observed_ref = refs[2 * many : 2 * many + 2]
        for n in range(many):

            def body(i, _, n=n):
                q = firsts[n] + i
                miss = number_ref[q] * field_refs[n][i] - observed_ref[q]
                refs[2 * many + 2 + n][i] = base_refs[n][i] + miss

            march(bases[n].shape[0], body)

    outs = [f32(*base.shape) for base in bases]
    return kernel_call(kernel, [], [*bases, *fields, number, observed], outs, [], 8)


def adjoint_step(place, halo, cur, old, field, found, next_ref, along_ref, pad):
    halo_ref, cur_refs, old_refs, field_refs, (c_ref, number_ref, observed_ref) = found[:5]
    slab, width, length = c_ref.shape
    first, count = place
    coming = (halo_ref[0], *halo[1:]) if halo else None
    prepare(first, pad, along_ref, coming, list(zip(cur_refs, origins(cur))), slab, width)
    for field_ref, field_at in zip(field_refs, origins(field)):
        begin, end = max(first, field_at), min(first + count, field_at + field_ref.shape[0])
        if end <= begin:
            continue
        old_ref, old_at = find(list(zip(old_refs, origins(old))), begin)

        def body(i, _, field_ref=field_ref, field_at=field_at, begin=begin, old_ref=old_ref, old_at=old_at):
            q = begin + i
            center, lap = stencil(pad, begin - first + HALO + i, width, along_ref[begin - first + i])
            value = 2.0 * center - old_ref[old_at + i] + c_ref[q] * lap
            miss = number_ref[q] * field_ref[begin - field_at + i] - observed_ref[q]
            next_ref[begin - first + i] = value + miss

        march(end - begin, body)


def adjoint_last(
    place, halo, cur, old, courant, field, number, observed, laps, adjoints, tile, other, after
):
    slab, width, length = courant.shape
    first, count = place
    inner = count > HALO
    groups = [[halo[0]] if halo else [], arrays_of(cur), arrays_of(old), arrays_of(field)]
    groups += [[courant, number, observed], sum(laps, []), sum(adjoints, [])]
    groups += [list(tile) + list(other), list(after)]
    sizes = [len(g) for g in groups]
    steps, parts = len(laps), len(laps[0])

    def kernel(*refs):
        found, refs = grouped(refs, sizes)
        next_ref, along_ref, pad = refs[-3:]
        adjoint_step(place, halo, cur, old, field, found, next_ref, along_ref, pad)
        lap_refs, adj_refs, more = found[5:8]
        core = lax.axis_index("shot") % 2

        def product(part, i):
            value = next_ref[part * (count // parts) + i] * lap_refs[part][i]
            for n in range(1, steps):
                value = value + adj_refs[(n - 1) * parts + part][i] * lap_refs[n * parts + part][i]
            return value

        def either(write):
            @pl.when(core == 0)
            def _():
                write(refs[0], refs[1])

            @pl.when(core == 1)
            def _():
                write(refs[1], refs[0])

        if inner:
            for part in (0, 1):

                @pl.when(core == part)
                def _(part=part):
                    for i in range(count // 2):
                        refs[0][i] = product(part, i)
                        write_piece(refs[1:-3], i, product(1 - part, i))

        elif not other:
            for i in range(HALO):
                refs[0][i] = product(0, i)
        else:
            tile_ref, tiles_ref, other_ref = more

            def write(first_ref, second_ref):
                for i in range(HALO):
                    rows = slice(i * width, (i + 1) * width)
                    first_ref[rows, :] = other_ref[i]
                    second_ref[rows, :] = product(0, i)

            either(write)
            for ref in refs[:2]:
                ref[HALO * width : HALO * width + 8, :] = tile_ref[...] + tiles_ref[...]

    if inner:
        outs = [f32(count // 2, width, length)]
        outs += [f32(count // 2 // 1, width, length)] * 1
    elif not other:
        outs = [f32(count, width, length)]
    else:
        outs = [f32(HALO * width + 8, length)] * 2
    scratch = [pltpu.VMEM((count, width, length), jnp.float32)] + scratch_of(count, width, length)
    return kernel_call(kernel, [], sum(groups, []), outs, scratch, count)


def curvature(laps, after):
    number = len(laps)
    half, width, length = laps[0][1].shape
    size = half + HALO

    def kernel(*refs):
        ranged = [refs[n * number : (n + 1) * number] for n in range(4)]
        keep_ref, *send_refs, tile_ref = refs[4 * number + 1 :]
        core = lax.axis_index("shot") % 2

        def squares(lap_refs, at):
            value = lap_refs[0][at] * lap_refs[0][at]
            for ref in lap_refs[1:]:
                value = value + ref[at] * ref[at]
            return value

        for part in (0, 1):

            @pl.when(core == part)
            def _(part=part):
                total = jnp.zeros((8, length), jnp.float32)
                own, far = (0, 1) if part == 0 else (3, 2)
                other = (3, 2) if part == 0 else (0, 1)
                for i in range(size):
                    outer = i >= half
                    value = squares(ranged[own if outer else far], i % half)
                    keep_ref[i] = value
                    total = total + fold(value)
                    value = squares(ranged[other[0] if outer else other[1]], i % half)
                    write_piece(send_refs, i, value)
                    total = total + fold(value)
                tile_ref[...] = total

    outs = [f32(size, width, length)]
    outs += [f32(size // 1, width, length)] * 1 + [f32(8, length)]
    arrays = [lap[n] for n in range(4) for lap in laps] + [after]
    return kernel_call(kernel, [], arrays, outs, [], 8)


def points(wavelet, source, cells, observed, slab, width, length):
    receivers = cells.shape[0]
    steps = observed.shape[0]
    area = width * length

    def kernel(wave_ref, source_ref, cell_ref, obs_ref, spot_ref, number_ref, *refs):
        row_refs, sum_refs = refs[:steps], refs[steps:]
        blank = jnp.zeros((width, length), jnp.float32)

        def clear(i, _):
            for ref in (spot_ref, number_ref) + sum_refs:
                ref[i] = blank

        march(slab, clear)
        depth = lax.axis_index("depth")
        offset = depth * (slab * area)
        odd = depth % 2
        column = lax.broadcasted_iota(jnp.int32, (1, length), 1)

        def add(local, terms):
            @pl.when((local >= 0) & (local < slab * area))
            def _():
                row, y = split(local, length)
                plane, x = split(row, width)
                q = jnp.where(odd == 1, plane, slab - 1 - plane)
                at = pl.ds(spread(x, width), 1)
                for ref, term in terms():
                    ref[q, at, :] = ref[q, at, :] + jnp.where(column == y, term, 0.0)

        add(source_ref[0] - offset, lambda: [(spot_ref, 1.0)])
        for n in range(steps):
            row_refs[n][...] = jnp.full((8, length), wave_ref[0, n], jnp.float32)

        def body(r, _):
            def terms():
                found = [(number_ref, 1.0)]
                for n in range(steps):
                    found.append((sum_refs[n], obs_ref[n, r]))
                return found

            add(cell_ref[r] - offset, terms)

        lax.fori_loop(0, receivers, body, None)

    volume = f32(slab, width, length)
    outs = [volume, volume] + [f32(8, length)] * steps + [volume] * steps
    small = [wavelet, source, cells, observed]
    found = kernel_call(kernel, small, [], outs, [], 8)
    return found[0], found[1], found[2 : 2 + steps], found[2 + steps :]


def interleaved(*arrays):
    number = len(arrays)
    slab, width, length = arrays[0].shape

    def kernel(*refs):
        odd = lax.axis_index("depth") % 2

        def body(i, _):
            plane = jnp.where(odd == 1, i, slab - 1 - i)
            for ref, out_ref in zip(refs[:number], refs[number:]):

                def put(at, value, out_ref=out_ref):
                    out_ref[i, at : at + ROWS, :] = value

                interleave(put, lambda spot, ref=ref: ref[plane, spot, :], width)

        march(slab, body)

    outs = [f32(slab, width, length)] * number
    return kernel_call(kernel, [], list(arrays), outs, [], 8)


def pack(field, adjoint_field):
    odd = lax.axis_index("depth") % 2
    far = field.shape[0] - HALO
    found = []
    for start in ((1 - odd) * far, odd * far):
        planes = [lax.dynamic_slice_in_dim(v, start, HALO, 0) for v in (field, adjoint_field)]
        found.append(jnp.concatenate(planes, axis=0))
    return found


def refresh(courant, inner_parts, outer_parts, curv, table, plan):
    slab, width, length = courant.shape
    half = inner_parts[0].shape[0]
    number = len(inner_parts)
    cells = slab * width * length * lax.axis_size("depth")

    def kernel(table_ref, plan_ref, c_ref, curv_ref, *rest):
        inner_refs = rest[:number]
        outer_refs = rest[number : 2 * number]
        out_ref = rest[2 * number]
        tail = slice(HALO * width, HALO * width + 8)
        tile = outer_refs[0][tail, :]
        for ref in outer_refs[1:]:
            tile = tile + ref[tail, :]
        level = jnp.sum(tile) / cells + 1e-06
        extra = table_ref[plan_ref[0]] * level
        core = lax.axis_index("shot") % 2
        odd = lax.axis_index("depth") % 2
        size = half + HALO

        def store(q, value):
            plane = jnp.where(odd == 1, q, size - 1 - q)
            for g in range(width // ROWS):
                spot = pl.ds(g, ROWS, stride=width // ROWS)
                out_ref[plane, spot, :] = value[g * ROWS : (g + 1) * ROWS]

        def body(i, _):
            grad = inner_refs[0][i]
            for ref in inner_refs[1:]:
                grad = grad + ref[i]
            model = c_ref[HALO + core * half + i]
            store((1 - core) * HALO + i, model - grad / (curv_ref[i] + extra))

        march(half, body)
        for i in range(HALO):
            rows = slice(i * width, (i + 1) * width)
            grad = outer_refs[0][rows, :]
            for ref in outer_refs[1:]:
                grad = grad + ref[rows, :]
            model = c_ref[core * (slab - HALO) + i]
            store(core * half + i, model - grad / (curv_ref[half + i] + extra))

    arrays = [courant, curv, *inner_parts, *outer_parts]
    outs = [f32(half + HALO, width, length)]
    return kernel_call(kernel, [table, plan], arrays, outs, [], half)[0]


def assemble(own, other):
    half, width, length = own.shape

    def kernel(own_ref, other_ref, out_ref, sems):
        core = lax.axis_index("shot") % 2
        upper = (lax.axis_index("depth") + core + 1) % 2
        copies = []
        for n, (ref, place) in enumerate([(own_ref, upper), (other_ref, 1 - upper)]):
            spot = out_ref.at[pl.ds(place * half, half)]
            copies.append(pltpu.make_async_copy(ref, spot, sems.at[n]))
        for copy in copies:
            copy.start()
        for copy in copies:
            copy.wait()

    return pl.pallas_call(
        kernel,
        out_shape=f32(2 * half, width, length),
        in_specs=[VMEM] * 2,
        out_specs=HBM,
        scratch_shapes=[pltpu.SemaphoreType.DMA((2,))],
        compiler_params=params(),
        cost_estimate=cost(8),
    )(own, other)


def exchange(values, side):
    links = []
    for i in range(side, lax.axis_size("depth") - 1, 2):
        links += [(i, i + 1), (i + 1, i)]
    return lax.ppermute(values, "depth", links)


def swap(values, axis, bit):
    count = lax.axis_size(axis)
    return lax.ppermute(values, axis, [(i, i ^ bit) for i in range(count)])


def sum_of(values, pieces, after):
    size = pieces[0].shape[0]

    def kernel(values_ref, *refs):
        for i in range(values.shape[0]):
            refs[-1][i] = values_ref[i] + refs[i // size][i % size]

    arrays = [values, *pieces, *after]
    return kernel_call(kernel, [], arrays, [f32(*values.shape)], [], 8)[0]


def total_parts(keep, send, after=()):
    if isinstance(send, (list, tuple)):
        parts = [keep, [swap(piece, "shot", 1) for piece in send]]
    else:
        parts = [keep, swap(send, "shot", 1)]
    bit = 2
    while bit < lax.axis_size("shot"):
        if isinstance(parts[1], list):
            here = sum_of(*parts, after)
        else:
            here = parts[0] + parts[1]
        parts = [here, swap(here, "shot", bit)]
        bit *= 2
    return parts


def write_piece(refs, i, value):
    size = refs[0].shape[0]
    refs[i // size][i % size] = value


def on_device(
    field_prev,
    field_now,
    adjoint_next,
    adjoint_after,
    courant,
    wavelet,
    source_cell,
    receiver_cell,
    observed,
    damping_table,
    plan_step,
):
    slab, width, length = courant.shape
    halos = [exchange(v, side) for side, v in enumerate(pack(field_now[0], adjoint_next[0]))]
    places = ranges(slab)
    starts = [first for first, _ in places]
    spot, number, waves, sums = points(
        wavelet, source_cell, receiver_cell[0], observed[0], slab, width, length
    )
    start, before, courant = interleaved(field_now[0], field_prev[0], courant)
    first, second = interleaved(adjoint_next[0], adjoint_after[0])
    old, cur = [(before, 0)], [(start, 0)]
    coming = [(halos[0], 0, True), (halos[1], 0, True)]

    def ahead(step, side, halo, cur, old, after):
        return forward(
            places[side], halo, cur, old, courant, spot, waves[step], after
        )

    def back(step, side, halo, cur, old, field, after):
        return adjoint(
            places[side], halo, cur, old, courant, [field], number, sums[step], after
        )

    laps, fields, bases = [], [], []
    near = ahead(0, 1, None, cur, old, ())
    far = ahead(0, 2, None, cur, old, ())
    for step in range(STEPS):
        last = step == STEPS - 1
        after = [near[0], far[0]]
        if last:
            rest, more = [(second, 0)], [(first, 0)]
            near_adj, far_adj = with_points(
                bases, starts[1:3], [near[0], far[0]], number, sums[step]
            )
            after += [near_adj, far_adj]
        one = ahead(step, 0, coming[0], cur, old, after)
        if last:
            edge = (halos[0], HALO, True)
            one_adj = back(step, 0, edge, more, rest, (one[0], starts[0]), after)
            message = exchange(one_adj, 0)
            newer = [(one_adj, starts[0]), (near_adj, starts[1]), (far_adj, starts[2])]
            near_next = back(step - 1, 1, None, newer, more, (fields[-1][1], starts[1]), ())
            two = ahead(step, 3, coming[1], cur, old, [near_next])
            edge = (halos[1], HALO, True)
            two_adj = back(step, 3, edge, more, rest, (two[0], starts[3]), [near_next])
            newer.append((two_adj, starts[3]))
        else:
            message = exchange(one[0], 0)
            newer = [(one[0], starts[0]), (near[0], starts[1]), (far[0], starts[2])]
            near_next = ahead(step + 1, 1, None, newer, cur, ())
            behind = [near_next[0]]
            if 0 < step < STEPS - 1:
                bases.append(adjoint_base(places[step], [(first, 0)], [(second, 0)], courant))
                behind.append(bases[-1])
            two = ahead(step, 3, coming[1], cur, old, behind)
            newer.append((two[0], starts[3]))
        laps.append((one[1], near[1], far[1], two[1]))
        fields.append((one[0], near[0], far[0], two[0]))
        if not last:
            coming = [(message, 0, False), (exchange(two[0], 1), 0, False)]
            far = ahead(step + 1, 2, None, newer, cur, ())
            near, old, cur = near_next, cur, newer
    coming = [(message, 0, False), (exchange(two_adj, 1), 0, False)]
    keep, *send, tile = curvature(laps, two_adj)
    tiles = swap(tile, "depth", 1)
    bit = 2
    old, cur, near = more, newer, near_next
    adjoints = [arrays_of(cur)]
    for step in range(STEPS - 2, 0, -1):
        far = back(step, 2, None, cur, old, (fields[step][2], starts[2]), ())
        after = [near, far]
        one = back(step, 0, coming[0], cur, old, (fields[step][0], starts[0]), after)
        message = exchange(one, 0)
        newer = [(one, starts[0]), (near, starts[1]), (far, starts[2])]
        if step > 1:
            near_next = back(step - 1, 1, None, newer, cur, (fields[step - 1][1], starts[1]), ())
            after = [near_next, tiles]
        else:
            after = [one, tiles]
        two = back(step, 3, coming[1], cur, old, (fields[step][3], starts[3]), after)
        newer.append((two, starts[3]))
        coming = [(message, 0, False), (exchange(two, 1), 0, False)]
        near, old, cur = near_next, cur, newer
        adjoints.insert(0, arrays_of(cur))
        if step == STEPS - 2:
            curv = sum(total_parts(keep, send, [two]))
        tile = tile + tiles
        if bit < lax.axis_size("depth"):
            tiles = swap(tile, "depth", bit)
            bit *= 2
    while bit < lax.axis_size("depth"):
        tile = tile + tiles
        tiles = swap(tile, "depth", bit)
        bit *= 2
    pieces = [(values, at) for values, at in zip(fields[0], starts)]
    inner = (starts[1], 2 * places[1][1])

    def finish(place, halo, sides, both, other, after):
        return adjoint_last(
            place, halo, cur, old, courant, [pieces[n] for n in sides], number, sums[0],
            [[lap[n] for n in sides] for lap in laps],
            [[a[n] for n in sides] for a in adjoints], both, other, after,
        )

    inside = finish(inner, None, (1, 2), [], [], [])
    one = finish(places[0], coming[0], (0,), [], [], inside[:1])
    outside = finish(places[3], coming[1], (3,), [tile, tiles], one, [curv])
    inner_parts = total_parts(inside[0], inside[1:])
    outer_parts = total_parts(*outside)
    own = refresh(courant, inner_parts, outer_parts, curv, damping_table, plan_step)
    return assemble(own, swap(own, "shot", 1))


def solution(mesh):
    in_specs = (
        P("shot", "depth", None, None),
        P("shot", "depth", None, None),
        P("shot", "depth", None, None),
        P("shot", "depth", None, None),
        P("depth", None, None),
        P("shot", None),
        P("shot"),
        P("shot", None),
        P("shot", None, None),
        P(),
        P(),
    )
    out_specs = P("depth", None, None)
    return jax.shard_map(
        on_device, mesh=mesh, in_specs=in_specs, out_specs=out_specs, check_vma=False
    )
```

```python
import jax
import jax.numpy as jnp
from jax import lax
from jax.experimental import pallas as pl
from jax.experimental.pallas import tpu as pltpu
from jax.sharding import PartitionSpec as P

STEPS = 4
HALO = 4
ROWS = 8
PAD = HALO * ROWS

coeffs = (-205.0 / 72.0, 8.0 / 5.0, -1.0 / 5.0, 8.0 / 315.0, -1.0 / 560.0)

VMEM = pl.BlockSpec(memory_space=pltpu.VMEM)
SMEM = pl.BlockSpec(memory_space=pltpu.SMEM)
HBM = pl.BlockSpec(memory_space=pltpu.HBM)


def f32(*shape):
    return jax.ShapeDtypeStruct(shape, jnp.float32)


def params():
    return pltpu.CompilerParams(vmem_limit_bytes=6 * 2**20)


def cost(planes):
    return pl.CostEstimate(
        flops=planes * 10**4, bytes_accessed=planes * 2**10, transcendentals=0
    )


def split(value, size):
    if size & (size - 1) == 0:
        return value >> (size.bit_length() - 1), value & (size - 1)
    return value // size, value % size


def spread(x, width):
    s, g = split(x, width // ROWS)
    return g * ROWS + s


def interleave(put, get, width):
    for g in range(width // ROWS):
        put(g * ROWS, get(pl.ds(g, ROWS, stride=width // ROWS)))


def margins(pad, first, count, width):
    length = pad.shape[2]
    place = lax.broadcasted_iota(jnp.int32, (ROWS, length), 0)

    def body(i, _):
        p = first + i
        for j in range(HALO):
            at = j * ROWS
            low = pltpu.roll(pad[p, width + at : width + at + ROWS, :], 1, 0)
            pad[p, at : at + ROWS, :] = jnp.where(place == 0, 0.0, low)
            top = pltpu.roll(pad[p, PAD + at : PAD + at + ROWS, :], ROWS - 1, 0)
            beyond = PAD + width + at
            pad[p, beyond : beyond + ROWS, :] = jnp.where(place == ROWS - 1, 0.0, top)

    march(count, body)


def fill(pad, base, pieces, width):
    top = base + pad.shape[0]
    for ref, origin in pieces:
        begin = max(base, origin)
        end = min(top, origin + ref.shape[0])
        if end > begin:
            pad[begin - base : end - base, PAD : PAD + width, :] = ref[begin - origin : end - origin]


def fill_halo(pad, at, ref, ref_at, natural, width):
    odd = lax.axis_index("depth") % 2
    for i in range(HALO):
        if natural:

            def put(row, value, i=i):
                pad[at + i, PAD + row : PAD + row + ROWS, :] = value

            source = ref_at + jnp.where(odd == 1, i, HALO - 1 - i)
            interleave(put, lambda spot, source=source: ref[source, spot, :], width)
        elif len(ref.shape) == 2:
            rows = slice((HALO - 1 - i) * width, (HALO - i) * width)
            pad[at + i, PAD : PAD + width, :] = ref[rows, :]
        else:
            pad[at + i, PAD : PAD + width, :] = ref[HALO - 1 - i]


def find(pieces, plane):
    for ref, origin in pieces:
        if origin <= plane < origin + ref.shape[0]:
            return ref, plane - origin


def columns(pad, along_ref, width):
    planes, _, length = along_ref.shape
    apart = lax.broadcasted_iota(jnp.int32, (length, length), 0)
    apart = jnp.abs(apart - lax.broadcasted_iota(jnp.int32, (length, length), 1))
    band = jnp.where(apart == 0, 3.0 * coeffs[0], 0.0)
    for k in range(1, 5):
        band = jnp.where(apart == k, coeffs[k], band)
    size = HALO if planes % (2 * HALO) else 2 * HALO
    for begin in range(0, planes, size):
        block = pad[HALO + begin : HALO + begin + size, PAD : PAD + width, :]
        product = jnp.dot(
            block.reshape(size * width, length),
            band,
            precision=lax.Precision.HIGHEST,
            preferred_element_type=jnp.float32,
        )
        along_ref[begin : begin + size] = product.reshape(size, width, length)


def stencil(pad, p, width, result):
    rows = slice(PAD, PAD + width)
    plane = pad[p]
    for k in range(1, 5):
        along = pad[p + k, rows, :] + pad[p - k, rows, :]
        along = along + plane[PAD + k * ROWS : PAD + k * ROWS + width]
        along = along + plane[PAD - k * ROWS : PAD - k * ROWS + width]
        result = result + coeffs[k] * along
    return plane[rows], result


def fold(values):
    width, length = values.shape
    return jnp.sum(values.reshape(width // 8, 8, length), axis=0)


def march(count, body, carry=None):
    return lax.fori_loop(0, count, body, carry, unroll=4 if count % 4 == 0 else 2)


def kernel_call(kernel, small, arrays, outs, scratch, planes):
    return pl.pallas_call(
        kernel,
        out_shape=tuple(outs),
        in_specs=[SMEM] * len(small) + [VMEM] * len(arrays),
        out_specs=tuple([VMEM] * len(outs)),
        scratch_shapes=scratch,
        compiler_params=params(),
        cost_estimate=cost(planes),
    )(*small, *arrays)


def grouped(refs, sizes):
    found = []
    for size in sizes:
        found.append(refs[:size])
        refs = refs[size:]
    return found, list(refs)


def ranges(slab):
    half = slab // 2 - HALO
    return [(0, HALO), (HALO, half), (HALO + half, half), (slab - HALO, HALO)]


def scratch_of(count, width, length):
    return [
        pltpu.VMEM((count, width, length), jnp.float32),
        pltpu.VMEM((count + 2 * HALO, width + 2 * PAD, length), jnp.float32),
    ]


def origins(field):
    return [at for _, at in field]


def arrays_of(field):
    return [values for values, _ in field]


def prepare(first, pad, along_ref, halo, cur, slab, width):
    count = along_ref.shape[0]
    fill(pad, first - HALO, cur, width)
    if halo is not None:
        fill_halo(pad, 0 if first == 0 else HALO + count, *halo, width)
    margins(pad, HALO, count, width)
    columns(pad, along_ref, width)


def forward(place, halo, cur, old, courant, source, wave, after):
    slab, width, length = courant.shape
    first, count = place
    groups = [[halo[0]] if halo else [], arrays_of(cur), arrays_of(old)]
    groups += [[courant, source, wave], list(after)]
    sizes = [len(g) for g in groups]

    def kernel(*refs):
        (halo_ref, cur_refs, old_refs, (c_ref, source_ref, wave_ref), _), refs = grouped(refs, sizes)
        next_ref, lap_ref, along_ref, pad = refs
        coming = (halo_ref[0], *halo[1:]) if halo else None
        prepare(first, pad, along_ref, coming, list(zip(cur_refs, origins(cur))), slab, width)
        old_ref, old_at = find(list(zip(old_refs, origins(old))), first)
        amplitude = wave_ref[0:1, :]

        def body(i, _):
            center, lap = stencil(pad, HALO + i, width, along_ref[i])
            lap_ref[i] = lap
            value = 2.0 * center - old_ref[old_at + i] + c_ref[first + i] * lap
            next_ref[i] = value + source_ref[first + i] * amplitude

        march(count, body)

    outs = [f32(count, width, length)] * 2
    return kernel_call(kernel, [], sum(groups, []), outs, scratch_of(count, width, length), count)


def adjoint(place, halo, cur, old, courant, field, number, observed, after):
    slab, width, length = courant.shape
    first, count = place
    groups = [[halo[0]] if halo else [], arrays_of(cur), arrays_of(old), arrays_of(field)]
    groups += [[courant, number, observed], list(after)]
    sizes = [len(g) for g in groups]

    def kernel(*refs):
        found, refs = grouped(refs, sizes)
        next_ref, along_ref, pad = refs
        adjoint_step(place, halo, cur, old, field, found, next_ref, along_ref, pad)

    outs = [f32(count, width, length)]
    scratch = scratch_of(count, width, length)
    return kernel_call(kernel, [], sum(groups, []), outs, scratch, count)[0]


def adjoint_base(place, cur, old, courant):
    slab, width, length = courant.shape
    first, count = place
    groups = [arrays_of(cur), arrays_of(old), [courant]]
    sizes = [len(g) for g in groups]

    def kernel(*refs):
        (cur_refs, old_refs, (c_ref,)), refs = grouped(refs, sizes)
        next_ref, along_ref, pad = refs
        prepare(first, pad, along_ref, None, list(zip(cur_refs, origins(cur))), slab, width)
        old_ref, old_at = find(list(zip(old_refs, origins(old))), first)

        def body(i, _):
            center, lap = stencil(pad, HALO + i, width, along_ref[i])
            next_ref[i] = 2.0 * center - old_ref[old_at + i] + c_ref[first + i] * lap

        march(count, body)

    outs = [f32(count, width, length)]
    scratch = scratch_of(count, width, length)
    return kernel_call(kernel, [], sum(groups, []), outs, scratch, count)[0]


def with_points(bases, firsts, fields, number, observed):
    many = len(bases)

    def kernel(*refs):
        base_refs, field_refs = refs[:many], refs[many : 2 * many]
        number_ref, observed_ref = refs[2 * many : 2 * many + 2]
        for n in range(many):

            def body(i, _, n=n):
                q = firsts[n] + i
                miss = number_ref[q] * field_refs[n][i] - observed_ref[q]
                refs[2 * many + 2 + n][i] = base_refs[n][i] + miss

            march(bases[n].shape[0], body)

    outs = [f32(*base.shape) for base in bases]
    return kernel_call(kernel, [], [*bases, *fields, number, observed], outs, [], 8)


def adjoint_step(place, halo, cur, old, field, found, next_ref, along_ref, pad):
    halo_ref, cur_refs, old_refs, field_refs, (c_ref, number_ref, observed_ref) = found[:5]
    slab, width, length = c_ref.shape
    first, count = place
    coming = (halo_ref[0], *halo[1:]) if halo else None
    prepare(first, pad, along_ref, coming, list(zip(cur_refs, origins(cur))), slab, width)
    for field_ref, field_at in zip(field_refs, origins(field)):
        begin, end = max(first, field_at), min(first + count, field_at + field_ref.shape[0])
        if end <= begin:
            continue
        old_ref, old_at = find(list(zip(old_refs, origins(old))), begin)

        def body(i, _, field_ref=field_ref, field_at=field_at, begin=begin, old_ref=old_ref, old_at=old_at):
            q = begin + i
            center, lap = stencil(pad, begin - first + HALO + i, width, along_ref[begin - first + i])
            value = 2.0 * center - old_ref[old_at + i] + c_ref[q] * lap
            miss = number_ref[q] * field_ref[begin - field_at + i] - observed_ref[q]
            next_ref[begin - first + i] = value + miss

        march(end - begin, body)


def adjoint_last(
    place, halo, cur, old, courant, field, number, observed, laps, adjoints, tile, other, after
):
    slab, width, length = courant.shape
    first, count = place
    inner = count > HALO
    groups = [[halo[0]] if halo else [], arrays_of(cur), arrays_of(old), arrays_of(field)]
    groups += [[courant, number, observed], sum(laps, []), sum(adjoints, [])]
    groups += [list(tile) + list(other), list(after)]
    sizes = [len(g) for g in groups]
    steps, parts = len(laps), len(laps[0])

    def kernel(*refs):
        found, refs = grouped(refs, sizes)
        next_ref, along_ref, pad = refs[-3:]
        adjoint_step(place, halo, cur, old, field, found, next_ref, along_ref, pad)
        lap_refs, adj_refs, more = found[5:8]
        core = lax.axis_index("shot") % 2

        def product(part, i):
            value = next_ref[part * (count // parts) + i] * lap_refs[part][i]
            for n in range(1, steps):
                value = value + adj_refs[(n - 1) * parts + part][i] * lap_refs[n * parts + part][i]
            return value

        def either(write):
            @pl.when(core == 0)
            def _():
                write(refs[0], refs[1])

            @pl.when(core == 1)
            def _():
                write(refs[1], refs[0])

        if inner:
            for part in (0, 1):

                @pl.when(core == part)
                def _(part=part):
                    for i in range(count // 2):
                        refs[0][i] = product(part, i)
                        write_piece(refs[1:-3], i, product(1 - part, i))

        elif not other:
            for i in range(HALO):
                refs[0][i] = product(0, i)
        else:
            tile_ref, tiles_ref, other_ref = more

            def write(first_ref, second_ref):
                for i in range(HALO):
                    rows = slice(i * width, (i + 1) * width)
                    first_ref[rows, :] = other_ref[i]
                    second_ref[rows, :] = product(0, i)

            either(write)
            for ref in refs[:2]:
                ref[HALO * width : HALO * width + 8, :] = tile_ref[...] + tiles_ref[...]

    if inner:
        outs = [f32(count // 2, width, length)]
        outs += [f32(count // 2 // 1, width, length)] * 1
    elif not other:
        outs = [f32(count, width, length)]
    else:
        outs = [f32(HALO * width + 8, length)] * 2
    scratch = [pltpu.VMEM((count, width, length), jnp.float32)] + scratch_of(count, width, length)
    return kernel_call(kernel, [], sum(groups, []), outs, scratch, count)


def curvature(laps, message, after):
    number = len(laps)
    half, width, length = laps[0][1].shape
    size = half + HALO

    def kernel(*refs):
        ranged = [refs[n * number : (n + 1) * number] for n in range(4)]
        planes_ref = refs[4 * number]
        keep_ref, *send_refs, tile_ref, message_ref = refs[4 * number + 2 :]
        for i in range(HALO):
            message_ref[i * width : (i + 1) * width, :] = planes_ref[i]
        core = lax.axis_index("shot") % 2

        def squares(lap_refs, at):
            value = lap_refs[0][at] * lap_refs[0][at]
            for ref in lap_refs[1:]:
                value = value + ref[at] * ref[at]
            return value

        for part in (0, 1):

            @pl.when(core == part)
            def _(part=part):
                total = jnp.zeros((8, length), jnp.float32)
                own, far = (0, 1) if part == 0 else (3, 2)
                other = (3, 2) if part == 0 else (0, 1)
                for i in range(size):
                    outer = i >= half
                    value = squares(ranged[own if outer else far], i % half)
                    keep_ref[i] = value
                    total = total + fold(value)
                    value = squares(ranged[other[0] if outer else other[1]], i % half)
                    write_piece(send_refs, i, value)
                    total = total + fold(value)
                tile_ref[...] = total
                message_ref[HALO * width : HALO * width + 8, :] = total

    outs = [f32(size, width, length)]
    outs += [f32(size // 1, width, length)] * 1 + [f32(8, length), f32(HALO * width + 8, length)]
    arrays = [lap[n] for n in range(4) for lap in laps] + [message, after]
    return kernel_call(kernel, [], arrays, outs, [], 8)


def points(wavelet, source, cells, observed, slab, width, length):
    receivers = cells.shape[0]
    steps = observed.shape[0]
    area = width * length

    def kernel(wave_ref, source_ref, cell_ref, obs_ref, spot_ref, number_ref, *refs):
        row_refs, sum_refs = refs[:steps], refs[steps:]
        blank = jnp.zeros((width, length), jnp.float32)

        def clear(i, _):
            for ref in (spot_ref, number_ref) + sum_refs:
                ref[i] = blank

        march(slab, clear)
        depth = lax.axis_index("depth")
        offset = depth * (slab * area)
        odd = depth % 2
        column = lax.broadcasted_iota(jnp.int32, (1, length), 1)

        def add(local, terms):
            @pl.when((local >= 0) & (local < slab * area))
            def _():
                row, y = split(local, length)
                plane, x = split(row, width)
                q = jnp.where(odd == 1, plane, slab - 1 - plane)
                at = pl.ds(spread(x, width), 1)
                for ref, term in terms():
                    ref[q, at, :] = ref[q, at, :] + jnp.where(column == y, term, 0.0)

        add(source_ref[0] - offset, lambda: [(spot_ref, 1.0)])
        for n in range(steps):
            row_refs[n][...] = jnp.full((8, length), wave_ref[0, n], jnp.float32)

        def body(r, _):
            def terms():
                found = [(number_ref, 1.0)]
                for n in range(steps):
                    found.append((sum_refs[n], obs_ref[n, r]))
                return found

            add(cell_ref[r] - offset, terms)

        lax.fori_loop(0, receivers, body, None)

    volume = f32(slab, width, length)
    outs = [volume, volume] + [f32(8, length)] * steps + [volume] * steps
    small = [wavelet, source, cells, observed]
    found = kernel_call(kernel, small, [], outs, [], 8)
    return found[0], found[1], found[2 : 2 + steps], found[2 + steps :]


def interleaved(*arrays):
    number = len(arrays)
    slab, width, length = arrays[0].shape

    def kernel(*refs):
        odd = lax.axis_index("depth") % 2

        def body(i, _):
            plane = jnp.where(odd == 1, i, slab - 1 - i)
            for ref, out_ref in zip(refs[:number], refs[number:]):

                def put(at, value, out_ref=out_ref):
                    out_ref[i, at : at + ROWS, :] = value

                interleave(put, lambda spot, ref=ref: ref[plane, spot, :], width)

        march(slab, body)

    outs = [f32(slab, width, length)] * number
    return kernel_call(kernel, [], list(arrays), outs, [], 8)


def pack(field, adjoint_field):
    odd = lax.axis_index("depth") % 2
    far = field.shape[0] - HALO
    found = []
    for start in ((1 - odd) * far, odd * far):
        planes = [lax.dynamic_slice_in_dim(v, start, HALO, 0) for v in (field, adjoint_field)]
        found.append(jnp.concatenate(planes, axis=0))
    return found


def refresh(courant, inner_parts, outer_parts, curv, table, plan):
    slab, width, length = courant.shape
    half = inner_parts[0].shape[0]
    number = len(inner_parts)
    cells = slab * width * length * lax.axis_size("depth")

    def kernel(table_ref, plan_ref, c_ref, curv_ref, *rest):
        inner_refs = rest[:number]
        outer_refs = rest[number : 2 * number]
        out_ref = rest[2 * number]
        tail = slice(HALO * width, HALO * width + 8)
        tile = outer_refs[0][tail, :]
        for ref in outer_refs[1:]:
            tile = tile + ref[tail, :]
        level = jnp.sum(tile) / cells + 1e-06
        extra = table_ref[plan_ref[0]] * level
        core = lax.axis_index("shot") % 2
        odd = lax.axis_index("depth") % 2
        size = half + HALO

        def store(q, value):
            plane = jnp.where(odd == 1, q, size - 1 - q)
            for g in range(width // ROWS):
                spot = pl.ds(g, ROWS, stride=width // ROWS)
                out_ref[plane, spot, :] = value[g * ROWS : (g + 1) * ROWS]

        def body(i, _):
            grad = inner_refs[0][i]
            for ref in inner_refs[1:]:
                grad = grad + ref[i]
            model = c_ref[HALO + core * half + i]
            store((1 - core) * HALO + i, model - grad / (curv_ref[i] + extra))

        march(half, body)
        for i in range(HALO):
            rows = slice(i * width, (i + 1) * width)
            grad = outer_refs[0][rows, :]
            for ref in outer_refs[1:]:
                grad = grad + ref[rows, :]
            model = c_ref[core * (slab - HALO) + i]
            store(core * half + i, model - grad / (curv_ref[half + i] + extra))

    arrays = [courant, curv, *inner_parts, *outer_parts]
    outs = [f32(half + HALO, width, length)]
    return kernel_call(kernel, [table, plan], arrays, outs, [], half)[0]


def place_half(values, own, result=None):
    half, width, length = values.shape

    def kernel(values_ref, *refs):
        out_ref, sem = refs[-2:]
        core = lax.axis_index("shot") % 2
        upper = (lax.axis_index("depth") + core + 1) % 2
        place = upper if own else 1 - upper
        copy = pltpu.make_async_copy(values_ref, out_ref.at[pl.ds(place * half, half)], sem)
        copy.start()
        copy.wait()

    return pl.pallas_call(
        kernel,
        out_shape=f32(2 * half, width, length),
        in_specs=[VMEM] if own else [VMEM, HBM],
        out_specs=HBM,
        input_output_aliases={} if own else {1: 0},
        scratch_shapes=[pltpu.SemaphoreType.DMA],
        compiler_params=params(),
        cost_estimate=cost(8),
    )(*([values] if own else [values, result]))


def exchange(values, side):
    links = []
    for i in range(side, lax.axis_size("depth") - 1, 2):
        links += [(i, i + 1), (i + 1, i)]
    return lax.ppermute(values, "depth", links)


def swap(values, axis, bit):
    count = lax.axis_size(axis)
    return lax.ppermute(values, axis, [(i, i ^ bit) for i in range(count)])


def sum_of(values, pieces, after):
    size = pieces[0].shape[0]

    def kernel(values_ref, *refs):
        for i in range(values.shape[0]):
            refs[-1][i] = values_ref[i] + refs[i // size][i % size]

    arrays = [values, *pieces, *after]
    return kernel_call(kernel, [], arrays, [f32(*values.shape)], [], 8)[0]


def total_parts(keep, send, after=()):
    if isinstance(send, (list, tuple)):
        parts = [keep, [swap(piece, "shot", 1) for piece in send]]
    else:
        parts = [keep, swap(send, "shot", 1)]
    bit = 2
    while bit < lax.axis_size("shot"):
        if isinstance(parts[1], list):
            here = sum_of(*parts, after)
        else:
            here = parts[0] + parts[1]
        parts = [here, swap(here, "shot", bit)]
        bit *= 2
    return parts


def write_piece(refs, i, value):
    size = refs[0].shape[0]
    refs[i // size][i % size] = value


def on_device(
    field_prev,
    field_now,
    adjoint_next,
    adjoint_after,
    courant,
    wavelet,
    source_cell,
    receiver_cell,
    observed,
    damping_table,
    plan_step,
):
    slab, width, length = courant.shape
    halos = [exchange(v, side) for side, v in enumerate(pack(field_now[0], adjoint_next[0]))]
    places = ranges(slab)
    starts = [first for first, _ in places]
    spot, number, waves, sums = points(
        wavelet, source_cell, receiver_cell[0], observed[0], slab, width, length
    )
    start, before, courant = interleaved(field_now[0], field_prev[0], courant)
    first, second = interleaved(adjoint_next[0], adjoint_after[0])
    old, cur = [(before, 0)], [(start, 0)]
    coming = [(halos[0], 0, True), (halos[1], 0, True)]

    def ahead(step, side, halo, cur, old, after):
        return forward(
            places[side], halo, cur, old, courant, spot, waves[step], after
        )

    def back(step, side, halo, cur, old, field, after):
        return adjoint(
            places[side], halo, cur, old, courant, [field], number, sums[step], after
        )

    laps, fields, bases = [], [], []
    near = ahead(0, 1, None, cur, old, ())
    far = ahead(0, 2, None, cur, old, ())
    for step in range(STEPS):
        last = step == STEPS - 1
        after = [near[0], far[0]]
        if last:
            rest, more = [(second, 0)], [(first, 0)]
            near_adj, far_adj = with_points(
                bases, starts[1:3], [near[0], far[0]], number, sums[step]
            )
            after += [near_adj, far_adj]
        one = ahead(step, 0, coming[0], cur, old, after)
        if last:
            edge = (halos[0], HALO, True)
            one_adj = back(step, 0, edge, more, rest, (one[0], starts[0]), after)
            newer = [(one_adj, starts[0]), (near_adj, starts[1]), (far_adj, starts[2])]
            near_next = back(step - 1, 1, None, newer, more, (fields[-1][1], starts[1]), ())
            two = ahead(step, 3, coming[1], cur, old, [near_next])
            edge = (halos[1], HALO, True)
            two_adj = back(step, 3, edge, more, rest, (two[0], starts[3]), [near_next])
            newer.append((two_adj, starts[3]))
        else:
            message = exchange(one[0], 0)
            newer = [(one[0], starts[0]), (near[0], starts[1]), (far[0], starts[2])]
            near_next = ahead(step + 1, 1, None, newer, cur, ())
            behind = [near_next[0]]
            if 0 < step < STEPS - 1:
                bases.append(adjoint_base(places[step], [(first, 0)], [(second, 0)], courant))
                behind.append(bases[-1])
            two = ahead(step, 3, coming[1], cur, old, behind)
            newer.append((two[0], starts[3]))
        laps.append((one[1], near[1], far[1], two[1]))
        fields.append((one[0], near[0], far[0], two[0]))
        if not last:
            coming = [(message, 0, False), (exchange(two[0], 1), 0, False)]
            far = ahead(step + 1, 2, None, newer, cur, ())
            near, old, cur = near_next, cur, newer
    keep, *send, tile, message = curvature(laps, one_adj, two_adj)
    message = exchange(message, 0)
    coming = [(message, 0, False), (exchange(two_adj, 1), 0, False)]
    tiles = message[HALO * width :, :]
    bit = 2
    old, cur, near = more, newer, near_next
    adjoints = [arrays_of(cur)]
    for step in range(STEPS - 2, 0, -1):
        far = back(step, 2, None, cur, old, (fields[step][2], starts[2]), ())
        after = [near, far]
        one = back(step, 0, coming[0], cur, old, (fields[step][0], starts[0]), after)
        message = exchange(one, 0)
        newer = [(one, starts[0]), (near, starts[1]), (far, starts[2])]
        if step > 1:
            near_next = back(step - 1, 1, None, newer, cur, (fields[step - 1][1], starts[1]), ())
            after = [near_next, tiles]
        else:
            after = [one, tiles]
        two = back(step, 3, coming[1], cur, old, (fields[step][3], starts[3]), after)
        newer.append((two, starts[3]))
        coming = [(message, 0, False), (exchange(two, 1), 0, False)]
        near, old, cur = near_next, cur, newer
        adjoints.insert(0, arrays_of(cur))
        if step == STEPS - 2:
            curv = sum(total_parts(keep, send, [two]))
        if bit < lax.axis_size("depth"):
            tile = tile + tiles
            tiles = swap(tile, "depth", bit)
            bit *= 2
    while bit < lax.axis_size("depth"):
        tile = tile + tiles
        tiles = swap(tile, "depth", bit)
        bit *= 2
    pieces = [(values, at) for values, at in zip(fields[0], starts)]
    inner = (starts[1], 2 * places[1][1])

    def finish(place, halo, sides, both, other, after):
        return adjoint_last(
            place, halo, cur, old, courant, [pieces[n] for n in sides], number, sums[0],
            [[lap[n] for n in sides] for lap in laps],
            [[a[n] for n in sides] for a in adjoints], both, other, after,
        )

    inside = finish(inner, None, (1, 2), [], [], [])
    one = finish(places[0], coming[0], (0,), [], [], inside[:1])
    outside = finish(places[3], coming[1], (3,), [tile, tiles], one, [curv])
    inner_parts = total_parts(inside[0], inside[1:])
    outer_parts = total_parts(*outside)
    own = refresh(courant, inner_parts, outer_parts, curv, damping_table, plan_step)
    other = swap(own, "shot", 1)
    return place_half(other, False, place_half(own, True))


def solution(mesh):
    in_specs = (
        P("shot", "depth", None, None),
        P("shot", "depth", None, None),
        P("shot", "depth", None, None),
        P("shot", "depth", None, None),
        P("depth", None, None),
        P("shot", None),
        P("shot"),
        P("shot", None),
        P("shot", None, None),
        P(),
        P(),
    )
    out_specs = P("depth", None, None)
    return jax.shard_map(
        on_device, mesh=mesh, in_specs=in_specs, out_specs=out_specs, check_vma=False
    )
```

```python
import jax
import jax.numpy as jnp
from jax import lax
from jax.experimental import pallas as pl
from jax.experimental.pallas import tpu as pltpu
from jax.sharding import PartitionSpec as P

STEPS = 4
HALO = 4
ROWS = 8
PAD = HALO * ROWS

coeffs = (-205.0 / 72.0, 8.0 / 5.0, -1.0 / 5.0, 8.0 / 315.0, -1.0 / 560.0)

VMEM = pl.BlockSpec(memory_space=pltpu.VMEM)
SMEM = pl.BlockSpec(memory_space=pltpu.SMEM)
HBM = pl.BlockSpec(memory_space=pltpu.HBM)


def f32(*shape):
    return jax.ShapeDtypeStruct(shape, jnp.float32)


def params():
    return pltpu.CompilerParams(vmem_limit_bytes=6 * 2**20)


def cost(planes):
    return pl.CostEstimate(
        flops=planes * 10**4, bytes_accessed=planes * 2**10, transcendentals=0
    )


def split(value, size):
    if size & (size - 1) == 0:
        return value >> (size.bit_length() - 1), value & (size - 1)
    return value // size, value % size


def spread(x, width):
    s, g = split(x, width // ROWS)
    return g * ROWS + s


def interleave(put, get, width):
    for g in range(width // ROWS):
        put(g * ROWS, get(pl.ds(g, ROWS, stride=width // ROWS)))


def margins(pad, first, count, width):
    length = pad.shape[2]
    place = lax.broadcasted_iota(jnp.int32, (ROWS, length), 0)

    def body(i, _):
        p = first + i
        for j in range(HALO):
            at = j * ROWS
            low = pltpu.roll(pad[p, width + at : width + at + ROWS, :], 1, 0)
            pad[p, at : at + ROWS, :] = jnp.where(place == 0, 0.0, low)
            top = pltpu.roll(pad[p, PAD + at : PAD + at + ROWS, :], ROWS - 1, 0)
            beyond = PAD + width + at
            pad[p, beyond : beyond + ROWS, :] = jnp.where(place == ROWS - 1, 0.0, top)

    march(count, body)


def fill(pad, base, pieces, width):
    top = base + pad.shape[0]
    for ref, origin in pieces:
        begin = max(base, origin)
        end = min(top, origin + ref.shape[0])
        if end > begin:
            pad[begin - base : end - base, PAD : PAD + width, :] = ref[begin - origin : end - origin]


def fill_halo(pad, at, ref, ref_at, natural, width):
    odd = lax.axis_index("depth") % 2
    for i in range(HALO):
        if natural:

            def put(row, value, i=i):
                pad[at + i, PAD + row : PAD + row + ROWS, :] = value

            source = ref_at + jnp.where(odd == 1, i, HALO - 1 - i)
            interleave(put, lambda spot, source=source: ref[source, spot, :], width)
        else:
            pad[at + i, PAD : PAD + width, :] = ref[HALO - 1 - i]


def find(pieces, plane):
    for ref, origin in pieces:
        if origin <= plane < origin + ref.shape[0]:
            return ref, plane - origin


def columns(pad, along_ref, width):
    planes, _, length = along_ref.shape
    apart = lax.broadcasted_iota(jnp.int32, (length, length), 0)
    apart = jnp.abs(apart - lax.broadcasted_iota(jnp.int32, (length, length), 1))
    band = jnp.where(apart == 0, 3.0 * coeffs[0], 0.0)
    for k in range(1, 5):
        band = jnp.where(apart == k, coeffs[k], band)
    size = HALO if planes % (2 * HALO) else 2 * HALO
    for begin in range(0, planes, size):
        block = pad[HALO + begin : HALO + begin + size, PAD : PAD + width, :]
        product = jnp.dot(
            block.reshape(size * width, length),
            band,
            precision=lax.Precision.HIGHEST,
            preferred_element_type=jnp.float32,
        )
        along_ref[begin : begin + size] = product.reshape(size, width, length)


def stencil(pad, p, width, result):
    rows = slice(PAD, PAD + width)
    plane = pad[p]
    for k in range(1, 5):
        along = pad[p + k, rows, :] + pad[p - k, rows, :]
        along = along + plane[PAD + k * ROWS : PAD + k * ROWS + width]
        along = along + plane[PAD - k * ROWS : PAD - k * ROWS + width]
        result = result + coeffs[k] * along
    return plane[rows], result


def fold(values):
    width, length = values.shape
    return jnp.sum(values.reshape(width // 8, 8, length), axis=0)


def march(count, body, carry=None):
    return lax.fori_loop(0, count, body, carry, unroll=4 if count % 4 == 0 else 2)


def kernel_call(kernel, small, arrays, outs, scratch, planes):
    return pl.pallas_call(
        kernel,
        out_shape=tuple(outs),
        in_specs=[SMEM] * len(small) + [VMEM] * len(arrays),
        out_specs=tuple([VMEM] * len(outs)),
        scratch_shapes=scratch,
        compiler_params=params(),
        cost_estimate=cost(planes),
    )(*small, *arrays)


def grouped(refs, sizes):
    found = []
    for size in sizes:
        found.append(refs[:size])
        refs = refs[size:]
    return found, list(refs)


def ranges(slab):
    half = slab // 2 - HALO
    return [(0, HALO), (HALO, half), (HALO + half, half), (slab - HALO, HALO)]


def scratch_of(count, width, length):
    return [
        pltpu.VMEM((count, width, length), jnp.float32),
        pltpu.VMEM((count + 2 * HALO, width + 2 * PAD, length), jnp.float32),
    ]


def origins(field):
    return [at for _, at in field]


def arrays_of(field):
    return [values for values, _ in field]


def prepare(first, pad, along_ref, halo, cur, slab, width):
    count = along_ref.shape[0]
    fill(pad, first - HALO, cur, width)
    if halo is not None:
        fill_halo(pad, 0 if first == 0 else HALO + count, *halo, width)
    margins(pad, HALO, count, width)
    columns(pad, along_ref, width)


def forward(place, halo, cur, old, courant, source, wave, after):
    slab, width, length = courant.shape
    first, count = place
    groups = [[halo[0]] if halo else [], arrays_of(cur), arrays_of(old)]
    groups += [[courant, source, wave], list(after)]
    sizes = [len(g) for g in groups]

    def kernel(*refs):
        (halo_ref, cur_refs, old_refs, (c_ref, source_ref, wave_ref), _), refs = grouped(refs, sizes)
        next_ref, lap_ref, along_ref, pad = refs
        coming = (halo_ref[0], *halo[1:]) if halo else None
        prepare(first, pad, along_ref, coming, list(zip(cur_refs, origins(cur))), slab, width)
        old_ref, old_at = find(list(zip(old_refs, origins(old))), first)
        amplitude = wave_ref[0:1, :]

        def body(i, _):
            center, lap = stencil(pad, HALO + i, width, along_ref[i])
            lap_ref[i] = lap
            value = 2.0 * center - old_ref[old_at + i] + c_ref[first + i] * lap
            next_ref[i] = value + source_ref[first + i] * amplitude

        march(count, body)

    outs = [f32(count, width, length)] * 2
    return kernel_call(kernel, [], sum(groups, []), outs, scratch_of(count, width, length), count)


def adjoint(place, halo, cur, old, courant, field, number, observed, after):
    slab, width, length = courant.shape
    first, count = place
    groups = [[halo[0]] if halo else [], arrays_of(cur), arrays_of(old), arrays_of(field)]
    groups += [[courant, number, observed], list(after)]
    sizes = [len(g) for g in groups]

    def kernel(*refs):
        found, refs = grouped(refs, sizes)
        next_ref, along_ref, pad = refs
        adjoint_step(place, halo, cur, old, field, found, next_ref, along_ref, pad)

    outs = [f32(count, width, length)]
    scratch = scratch_of(count, width, length)
    return kernel_call(kernel, [], sum(groups, []), outs, scratch, count)[0]


def adjoint_base(place, cur, old, courant):
    slab, width, length = courant.shape
    first, count = place
    groups = [arrays_of(cur), arrays_of(old), [courant]]
    sizes = [len(g) for g in groups]

    def kernel(*refs):
        (cur_refs, old_refs, (c_ref,)), refs = grouped(refs, sizes)
        next_ref, along_ref, pad = refs
        prepare(first, pad, along_ref, None, list(zip(cur_refs, origins(cur))), slab, width)
        old_ref, old_at = find(list(zip(old_refs, origins(old))), first)

        def body(i, _):
            center, lap = stencil(pad, HALO + i, width, along_ref[i])
            next_ref[i] = 2.0 * center - old_ref[old_at + i] + c_ref[first + i] * lap

        march(count, body)

    outs = [f32(count, width, length)]
    scratch = scratch_of(count, width, length)
    return kernel_call(kernel, [], sum(groups, []), outs, scratch, count)[0]


def with_points(bases, firsts, fields, number, observed):
    many = len(bases)

    def kernel(*refs):
        base_refs, field_refs = refs[:many], refs[many : 2 * many]
        number_ref, observed_ref = refs[2 * many : 2 * many + 2]
        for n in range(many):

            def body(i, _, n=n):
                q = firsts[n] + i
                miss = number_ref[q] * field_refs[n][i] - observed_ref[q]
                refs[2 * many + 2 + n][i] = base_refs[n][i] + miss

            march(bases[n].shape[0], body)

    outs = [f32(*base.shape) for base in bases]
    return kernel_call(kernel, [], [*bases, *fields, number, observed], outs, [], 8)


def adjoint_step(place, halo, cur, old, field, found, next_ref, along_ref, pad):
    halo_ref, cur_refs, old_refs, field_refs, (c_ref, number_ref, observed_ref) = found[:5]
    slab, width, length = c_ref.shape
    first, count = place
    coming = (halo_ref[0], *halo[1:]) if halo else None
    prepare(first, pad, along_ref, coming, list(zip(cur_refs, origins(cur))), slab, width)
    for field_ref, field_at in zip(field_refs, origins(field)):
        begin, end = max(first, field_at), min(first + count, field_at + field_ref.shape[0])
        if end <= begin:
            continue
        old_ref, old_at = find(list(zip(old_refs, origins(old))), begin)

        def body(i, _, field_ref=field_ref, field_at=field_at, begin=begin, old_ref=old_ref, old_at=old_at):
            q = begin + i
            center, lap = stencil(pad, begin - first + HALO + i, width, along_ref[begin - first + i])
            value = 2.0 * center - old_ref[old_at + i] + c_ref[q] * lap
            miss = number_ref[q] * field_ref[begin - field_at + i] - observed_ref[q]
            next_ref[begin - first + i] = value + miss

        march(end - begin, body)


def adjoint_last(
    place, halo, cur, old, courant, field, number, observed, laps, adjoints, tile, other, after
):
    slab, width, length = courant.shape
    first, count = place
    inner = count > HALO
    groups = [[halo[0]] if halo else [], arrays_of(cur), arrays_of(old), arrays_of(field)]
    groups += [[courant, number, observed], sum(laps, []), sum(adjoints, [])]
    groups += [list(tile) + list(other), list(after)]
    sizes = [len(g) for g in groups]
    steps, parts = len(laps), len(laps[0])

    def kernel(*refs):
        found, refs = grouped(refs, sizes)
        next_ref, along_ref, pad = refs[-3:]
        adjoint_step(place, halo, cur, old, field, found, next_ref, along_ref, pad)
        lap_refs, adj_refs, more = found[5:8]
        core = lax.axis_index("shot") % 2

        def product(part, i):
            value = next_ref[part * (count // parts) + i] * lap_refs[part][i]
            for n in range(1, steps):
                value = value + adj_refs[(n - 1) * parts + part][i] * lap_refs[n * parts + part][i]
            return value

        def either(write):
            @pl.when(core == 0)
            def _():
                write(refs[0], refs[1])

            @pl.when(core == 1)
            def _():
                write(refs[1], refs[0])

        if inner:
            for part in (0, 1):

                @pl.when(core == part)
                def _(part=part):
                    for i in range(count // 2):
                        refs[0][i] = product(part, i)
                        write_piece(refs[1:-3], i, product(1 - part, i))

        elif not other:
            for i in range(HALO):
                refs[0][i] = product(0, i)
        else:
            tile_ref, tiles_ref, other_ref = more

            def write(first_ref, second_ref):
                for i in range(HALO):
                    rows = slice(i * width, (i + 1) * width)
                    first_ref[rows, :] = other_ref[i]
                    second_ref[rows, :] = product(0, i)

            either(write)
            for ref in refs[:2]:
                ref[HALO * width : HALO * width + 8, :] = tile_ref[...] + tiles_ref[...]

    if inner:
        outs = [f32(count // 2, width, length)]
        outs += [f32(count // 2 // 1, width, length)] * 1
    elif not other:
        outs = [f32(count, width, length)]
    else:
        outs = [f32(HALO * width + 8, length)] * 2
    scratch = [pltpu.VMEM((count, width, length), jnp.float32)] + scratch_of(count, width, length)
    return kernel_call(kernel, [], sum(groups, []), outs, scratch, count)


def curvature(laps, after):
    number = len(laps)
    half, width, length = laps[0][1].shape
    size = half + HALO

    def kernel(*refs):
        ranged = [refs[n * number : (n + 1) * number] for n in range(4)]
        keep_ref, *send_refs, tile_ref = refs[4 * number + 1 :]
        core = lax.axis_index("shot") % 2

        def squares(lap_refs, at):
            value = lap_refs[0][at] * lap_refs[0][at]
            for ref in lap_refs[1:]:
                value = value + ref[at] * ref[at]
            return value

        for part in (0, 1):

            @pl.when(core == part)
            def _(part=part):
                total = jnp.zeros((8, length), jnp.float32)
                own, far = (0, 1) if part == 0 else (3, 2)
                other = (3, 2) if part == 0 else (0, 1)
                for i in range(size):
                    outer = i >= half
                    value = squares(ranged[own if outer else far], i % half)
                    keep_ref[i] = value
                    total = total + fold(value)
                    value = squares(ranged[other[0] if outer else other[1]], i % half)
                    write_piece(send_refs, i, value)
                    total = total + fold(value)
                tile_ref[...] = total

    outs = [f32(size, width, length)]
    outs += [f32(size // 1, width, length)] * 1 + [f32(8, length)]
    arrays = [lap[n] for n in range(4) for lap in laps] + [after]
    return kernel_call(kernel, [], arrays, outs, [], 8)


def points(wavelet, source, cells, observed, slab, width, length):
    receivers = cells.shape[0]
    steps = observed.shape[0]
    area = width * length

    def kernel(wave_ref, source_ref, cell_ref, obs_ref, spot_ref, number_ref, *refs):
        row_refs, sum_refs = refs[:steps], refs[steps:]
        blank = jnp.zeros((width, length), jnp.float32)

        def clear(i, _):
            for ref in (spot_ref, number_ref) + sum_refs:
                ref[i] = blank

        march(slab, clear)
        depth = lax.axis_index("depth")
        offset = depth * (slab * area)
        odd = depth % 2
        column = lax.broadcasted_iota(jnp.int32, (1, length), 1)

        def add(local, terms):
            @pl.when((local >= 0) & (local < slab * area))
            def _():
                row, y = split(local, length)
                plane, x = split(row, width)
                q = jnp.where(odd == 1, plane, slab - 1 - plane)
                at = pl.ds(spread(x, width), 1)
                for ref, term in terms():
                    ref[q, at, :] = ref[q, at, :] + jnp.where(column == y, term, 0.0)

        add(source_ref[0] - offset, lambda: [(spot_ref, 1.0)])
        for n in range(steps):
            row_refs[n][...] = jnp.full((8, length), wave_ref[0, n], jnp.float32)

        def body(r, _):
            def terms():
                found = [(number_ref, 1.0)]
                for n in range(steps):
                    found.append((sum_refs[n], obs_ref[n, r]))
                return found

            add(cell_ref[r] - offset, terms)

        lax.fori_loop(0, receivers, body, None)

    volume = f32(slab, width, length)
    outs = [volume, volume] + [f32(8, length)] * steps + [volume] * steps
    small = [wavelet, source, cells, observed]
    found = kernel_call(kernel, small, [], outs, [], 8)
    return found[0], found[1], found[2 : 2 + steps], found[2 + steps :]


def interleaved(*arrays):
    number = len(arrays)
    slab, width, length = arrays[0].shape

    def kernel(*refs):
        odd = lax.axis_index("depth") % 2

        def body(i, _):
            plane = jnp.where(odd == 1, i, slab - 1 - i)
            for ref, out_ref in zip(refs[:number], refs[number:]):

                def put(at, value, out_ref=out_ref):
                    out_ref[i, at : at + ROWS, :] = value

                interleave(put, lambda spot, ref=ref: ref[plane, spot, :], width)

        march(slab, body)

    outs = [f32(slab, width, length)] * number
    return kernel_call(kernel, [], list(arrays), outs, [], 8)


def pack(field, adjoint_field):
    odd = lax.axis_index("depth") % 2
    far = field.shape[0] - HALO
    found = []
    for start in ((1 - odd) * far, odd * far):
        planes = [lax.dynamic_slice_in_dim(v, start, HALO, 0) for v in (field, adjoint_field)]
        found.append(jnp.concatenate(planes, axis=0))
    return found


def refresh(courant, inner_parts, outer_parts, curv, table, plan):
    slab, width, length = courant.shape
    half = inner_parts[0].shape[0]
    number = len(inner_parts)
    cells = slab * width * length * lax.axis_size("depth")

    def kernel(table_ref, plan_ref, c_ref, curv_ref, *rest):
        inner_refs = rest[:number]
        outer_refs = rest[number : 2 * number]
        out_ref = rest[2 * number]
        tail = slice(HALO * width, HALO * width + 8)
        tile = outer_refs[0][tail, :]
        for ref in outer_refs[1:]:
            tile = tile + ref[tail, :]
        level = jnp.sum(tile) / cells + 1e-06
        extra = table_ref[plan_ref[0]] * level
        core = lax.axis_index("shot") % 2
        odd = lax.axis_index("depth") % 2
        size = half + HALO

        def store(q, value):
            plane = jnp.where(odd == 1, q, size - 1 - q)
            for g in range(width // ROWS):
                spot = pl.ds(g, ROWS, stride=width // ROWS)
                out_ref[plane, spot, :] = value[g * ROWS : (g + 1) * ROWS]

        def body(i, _):
            grad = inner_refs[0][i]
            for ref in inner_refs[1:]:
                grad = grad + ref[i]
            model = c_ref[HALO + core * half + i]
            store((1 - core) * HALO + i, model - grad / (curv_ref[i] + extra))

        march(half, body)
        for i in range(HALO):
            rows = slice(i * width, (i + 1) * width)
            grad = outer_refs[0][rows, :]
            for ref in outer_refs[1:]:
                grad = grad + ref[rows, :]
            model = c_ref[core * (slab - HALO) + i]
            store(core * half + i, model - grad / (curv_ref[half + i] + extra))

    arrays = [courant, curv, *inner_parts, *outer_parts]
    outs = [f32(half + HALO, width, length)]
    return kernel_call(kernel, [table, plan], arrays, outs, [], half)[0]


def place_half(values, own, result=None):
    half, width, length = values.shape

    def kernel(values_ref, *refs):
        out_ref, sem = refs[-2:]
        core = lax.axis_index("shot") % 2
        upper = (lax.axis_index("depth") + core + 1) % 2
        place = upper if own else 1 - upper
        copy = pltpu.make_async_copy(values_ref, out_ref.at[pl.ds(place * half, half)], sem)
        copy.start()
        copy.wait()

    return pl.pallas_call(
        kernel,
        out_shape=f32(2 * half, width, length),
        in_specs=[VMEM] if own else [VMEM, HBM],
        out_specs=HBM,
        input_output_aliases={} if own else {1: 0},
        scratch_shapes=[pltpu.SemaphoreType.DMA],
        compiler_params=params(),
        cost_estimate=cost(8),
    )(*([values] if own else [values, result]))


def exchange(values, side):
    links = []
    for i in range(side, lax.axis_size("depth") - 1, 2):
        links += [(i, i + 1), (i + 1, i)]
    return lax.ppermute(values, "depth", links)


def swap(values, axis, bit):
    count = lax.axis_size(axis)
    return lax.ppermute(values, axis, [(i, i ^ bit) for i in range(count)])


def sum_of(values, pieces, after):
    size = pieces[0].shape[0]

    def kernel(values_ref, *refs):
        for i in range(values.shape[0]):
            refs[-1][i] = values_ref[i] + refs[i // size][i % size]

    arrays = [values, *pieces, *after]
    return kernel_call(kernel, [], arrays, [f32(*values.shape)], [], 8)[0]


def total_parts(keep, send, after=()):
    if isinstance(send, (list, tuple)):
        parts = [keep, [swap(piece, "shot", 1) for piece in send]]
    else:
        parts = [keep, swap(send, "shot", 1)]
    bit = 2
    while bit < lax.axis_size("shot"):
        if isinstance(parts[1], list):
            here = sum_of(*parts, after)
        else:
            here = parts[0] + parts[1]
        parts = [here, swap(here, "shot", bit)]
        bit *= 2
    return parts


def write_piece(refs, i, value):
    size = refs[0].shape[0]
    refs[i // size][i % size] = value


def on_device(
    field_prev,
    field_now,
    adjoint_next,
    adjoint_after,
    courant,
    wavelet,
    source_cell,
    receiver_cell,
    observed,
    damping_table,
    plan_step,
):
    slab, width, length = courant.shape
    halos = [exchange(v, side) for side, v in enumerate(pack(field_now[0], adjoint_next[0]))]
    places = ranges(slab)
    starts = [first for first, _ in places]
    spot, number, waves, sums = points(
        wavelet, source_cell, receiver_cell[0], observed[0], slab, width, length
    )
    start, before, courant = interleaved(field_now[0], field_prev[0], courant)
    first, second = interleaved(adjoint_next[0], adjoint_after[0])
    old, cur = [(before, 0)], [(start, 0)]
    coming = [(halos[0], 0, True), (halos[1], 0, True)]

    def ahead(step, side, halo, cur, old, after):
        return forward(
            places[side], halo, cur, old, courant, spot, waves[step], after
        )

    def back(step, side, halo, cur, old, field, after):
        return adjoint(
            places[side], halo, cur, old, courant, [field], number, sums[step], after
        )

    laps, fields, bases = [], [], []
    near = ahead(0, 1, None, cur, old, ())
    far = ahead(0, 2, None, cur, old, ())
    for step in range(STEPS):
        last = step == STEPS - 1
        after = [near[0], far[0]]
        if last:
            rest, more = [(second, 0)], [(first, 0)]
            near_adj, far_adj = with_points(
                bases, starts[1:3], [near[0], far[0]], number, sums[step]
            )
            after += [near_adj, far_adj]
        one = ahead(step, 0, coming[0], cur, old, after)
        if last:
            edge = (halos[0], HALO, True)
            one_adj = back(step, 0, edge, more, rest, (one[0], starts[0]), after)
            message = exchange(one_adj, 0)
            newer = [(one_adj, starts[0]), (near_adj, starts[1]), (far_adj, starts[2])]
            near_next = back(step - 1, 1, None, newer, more, (fields[-1][1], starts[1]), ())
            two = ahead(step, 3, coming[1], cur, old, [near_next])
            edge = (halos[1], HALO, True)
            two_adj = back(step, 3, edge, more, rest, (two[0], starts[3]), [near_next])
            newer.append((two_adj, starts[3]))
        else:
            message = exchange(one[0], 0)
            newer = [(one[0], starts[0]), (near[0], starts[1]), (far[0], starts[2])]
            near_next = ahead(step + 1, 1, None, newer, cur, ())
            behind = [near_next[0]]
            if 0 < step < STEPS - 1:
                bases.append(adjoint_base(places[step], [(first, 0)], [(second, 0)], courant))
                behind.append(bases[-1])
            two = ahead(step, 3, coming[1], cur, old, behind)
            newer.append((two[0], starts[3]))
        laps.append((one[1], near[1], far[1], two[1]))
        fields.append((one[0], near[0], far[0], two[0]))
        if not last:
            coming = [(message, 0, False), (exchange(two[0], 1), 0, False)]
            far = ahead(step + 1, 2, None, newer, cur, ())
            near, old, cur = near_next, cur, newer
    coming = [(message, 0, False), (exchange(two_adj, 1), 0, False)]
    keep, *send, tile = curvature(laps, two_adj)
    tiles = swap(tile, "depth", 1)
    bit = 2
    old, cur, near = more, newer, near_next
    adjoints = [arrays_of(cur)]
    for step in range(STEPS - 2, 0, -1):
        far = back(step, 2, None, cur, old, (fields[step][2], starts[2]), ())
        after = [near, far]
        one = back(step, 0, coming[0], cur, old, (fields[step][0], starts[0]), after)
        message = exchange(one, 0)
        newer = [(one, starts[0]), (near, starts[1]), (far, starts[2])]
        if step > 1:
            near_next = back(step - 1, 1, None, newer, cur, (fields[step - 1][1], starts[1]), ())
            after = [near_next, tiles]
        else:
            after = [one, tiles]
        two = back(step, 3, coming[1], cur, old, (fields[step][3], starts[3]), after)
        newer.append((two, starts[3]))
        coming = [(message, 0, False), (exchange(two, 1), 0, False)]
        near, old, cur = near_next, cur, newer
        adjoints.insert(0, arrays_of(cur))
        if step == STEPS - 2:
            curv = sum(total_parts(keep, send, [two]))
        tile = tile + tiles
        if bit < lax.axis_size("depth"):
            tiles = swap(tile, "depth", bit)
            bit *= 2
    while bit < lax.axis_size("depth"):
        tile = tile + tiles
        tiles = swap(tile, "depth", bit)
        bit *= 2
    pieces = [(values, at) for values, at in zip(fields[0], starts)]
    inner = (starts[1], 2 * places[1][1])

    def finish(place, halo, sides, both, other, after):
        return adjoint_last(
            place, halo, cur, old, courant, [pieces[n] for n in sides], number, sums[0],
            [[lap[n] for n in sides] for lap in laps],
            [[a[n] for n in sides] for a in adjoints], both, other, after,
        )

    inside = finish(inner, None, (1, 2), [], [], [])
    one = finish(places[0], coming[0], (0,), [], [], inside[:1])
    outside = finish(places[3], coming[1], (3,), [tile, tiles], one, [curv])
    inner_parts = total_parts(inside[0], inside[1:])
    outer_parts = total_parts(*outside)
    own = refresh(courant, inner_parts, outer_parts, curv, damping_table, plan_step)
    other = swap(own, "shot", 1)
    return place_half(other, False, place_half(own, True))


def solution(mesh):
    in_specs = (
        P("shot", "depth", None, None),
        P("shot", "depth", None, None),
        P("shot", "depth", None, None),
        P("shot", "depth", None, None),
        P("depth", None, None),
        P("shot", None),
        P("shot"),
        P("shot", None),
        P("shot", None, None),
        P(),
        P(),
    )
    out_specs = P("depth", None, None)
    return jax.shard_map(
        on_device, mesh=mesh, in_specs=in_specs, out_specs=out_specs, check_vma=False
    )
```
